256 devices in a mesh: seq: 32 (over z_hi, y, core), tensor: 4 (over x), dp: 2 (over z_lo).
Axes of the slice: x: 4, y: 4, z: 8 (z_hi: 4, z_lo: 2; z = z_hi * 2 + z_lo), core: 2. Of those that a mesh axis runs over, the one named last changes fastest.
Arguments:
- hidden_in: bfloat16 [2, 32, 256, 1152], P('dp', 'seq'), may hold values from -6 to 6
- norm1_gain: float32 [1152], replicated, may hold values from 0.1 to 1.9
- qkv_weight: bfloat16 [1152, 3, 1152], P(None, None, 'tensor'), may hold values from -0.25043365 to 0.25043365
- out_weight: bfloat16 [1152, 1152], P('tensor'), may hold values from -0.1875 to 0.1875
- norm2_gain: float32 [1152], replicated, may hold values from 0.1 to 1.9
- fc1_weight: bfloat16 [1152, 4608], P(None, 'tensor'), may hold values from -0.1875 to 0.1875
- fc2_weight: bfloat16 [1152, 4608], P(None, 'tensor'), may hold values from -0.09375 to 0.09375
- out_grad: bfloat16 [2, 32, 256, 1152], P('dp', 'seq'), may hold values from -8 to 8
Outputs:
- block_out: bfloat16 [2, 32, 256, 1152], P('dp', 'seq')
- grad_mid: bfloat16 [2, 32, 256, 1152], P('dp', 'seq')
- grad_fc1: float32 [1152, 4608], P(('seq', 'dp'), 'tensor')
- grad_fc2: float32 [1152, 4608], P(('seq', 'dp'), 'tensor')
The draws below stay inside these ranges and needn't reach their ends.
All inputs are finite; a program needn't handle non-finite values.
Results may differ from the reference program's by a relative error of at most 0.0077.
Values may be sent and summed in bfloat16 or wider, within the bound.
A program may use at most 128 MiB of HBM per device.

```python
import jax
import jax.numpy as jnp
from jax import lax

D = 1152
HEADS = 16
HDIM = 72
FF = 4608
PATCHES = 256
FRAMES = 32
BATCH = 2


def draw_qkv_weight(key, part):
    key = jax.random.fold_in(key, 11)
    key_base = jax.random.fold_in(key, 0)
    scale = D ** (-0.5)
    base = jnp.clip(jax.random.normal(key_base, (D, 3, HEADS * HDIM), jnp.float32), -6.0, 6.0) * scale
    return base.astype(jnp.bfloat16)


def with_spikes(values, key, source, target, parts, factor):
    def block_of(dim):
        return (jnp.arange(values.shape[dim]) // (values.shape[dim] // parts)).reshape((-1,) + (1,) * (values.ndim - 1 - dim))

    near = jax.random.permutation(key, parts)[block_of(target)]
    far = (block_of(target) + parts // 2) % parts
    return jnp.where((block_of(source) == near) | (block_of(source) == far), factor * values, values)


def shard_levels(rng, shape, cuts, low, largest):
    def one(axis_at, parts):
        heights = jax.random.uniform(jax.random.fold_in(jax.random.fold_in(rng, 6), axis_at), (parts,), jnp.float32, low / len(cuts), largest / len(cuts))
        return jnp.repeat(jnp.exp(heights), shape[axis_at] // parts).reshape((-1,) + (1,) * (len(shape) - axis_at - 1))

    loudness = one(*cuts[0])
    for cut in cuts[1:]:
        loudness = loudness * one(*cut)
    return loudness


def scatter_about(rng, dims, deviation, limit, shards=(), kind=jnp.bfloat16):
    entries = jax.random.normal(rng, dims, jnp.float32) * deviation
    if len(shards) > 0:
        entries = shard_levels(rng, dims, shards, -0.22, 0.18) * entries
    return jnp.clip(entries, min=-limit, max=limit).astype(kind)


def gaussian_with(rng, extent, deviation, reach, pieces, heavy, kind=jnp.bfloat16):
    values = deviation * jax.random.normal(rng, extent, jnp.float32)
    if pieces:
        values = values * shard_levels(rng, extent, pieces, -0.22, 0.18)
    return jnp.clip(with_spikes(values, jax.random.fold_in(rng, 3), *heavy), -reach, reach).astype(kind)


def setup_inputs(seed: int = 0) -> dict:
    key_of = jax.random.split(jax.random.key(seed), 9)
    return {
        "hidden_in": scatter_about(key_of[0], (BATCH, FRAMES, PATCHES, D), 1.0, 6.0, ((0, 2), (1, 32))),
        "norm1_gain": jnp.clip(1.0 + 0.18 * jax.random.normal(key_of[1], (D,), jnp.float32), 0.1, 1.9),
        "qkv_weight": draw_qkv_weight(jax.random.fold_in(key_of[8], 71), 0),
        "out_weight": scatter_about(key_of[3], (HEADS * HDIM, D), (HEADS * HDIM) ** -0.5, 0.1875, ((0, 4),)),
        "norm2_gain": jnp.clip(1.0 + 0.18 * jax.random.normal(key_of[4], (D,), jnp.float32), 0.1, 1.9),
        "fc1_weight": scatter_about(key_of[5], (D, FF), D ** -0.5, 0.1875, ((1, 4),)),
        "fc2_weight": scatter_about(key_of[6], (D, FF), FF ** -0.5, 0.09375, ((1, 4),)),
        "out_grad": gaussian_with(key_of[7], (BATCH, FRAMES, PATCHES, D), 1.0, 8.0, ((0, 2), (1, 32)), (1, 3, 32, 2.75)),
    }


epsilon = 1e-06

def normalize(values):
    values = values.astype(jnp.float32)
    center = values - lax.optimization_barrier(jnp.mean(values, -1, keepdims=True))
    inv_std = lax.rsqrt(lax.optimization_barrier(jnp.mean(center * center, -1, keepdims=True)) + epsilon)
    return (center * inv_std, inv_std)

def gelu_tanh(values):
    return jax.nn.gelu(values, approximate=True)

def norm_back(grad_norm, x_hat, inv_std, gain, upstream):
    scaled = grad_norm * gain
    plain_mean = lax.optimization_barrier(jnp.mean(scaled, -1, keepdims=True))
    cross_mean = lax.optimization_barrier(jnp.mean(scaled * x_hat, -1, keepdims=True))
    total = upstream.astype(jnp.float32) + inv_std * (scaled - plain_mean - x_hat * cross_mean)
    return total.astype(jnp.bfloat16)

def attend(queries, keys_all, values_all):
    scores = jnp.einsum('bfphd,bgphd->bphfg', queries.astype(jnp.float32), keys_all.astype(jnp.float32)) * HDIM ** (-0.5)
    shifted = scores - lax.optimization_barrier(jnp.max(scores, -1, keepdims=True))
    weights = jnp.exp(shifted)
    probs = (weights / lax.optimization_barrier(jnp.sum(weights, -1, keepdims=True))).astype(jnp.bfloat16)
    result = jnp.einsum('bphfg,bgphd->bfphd', probs.astype(jnp.float32), values_all.astype(jnp.float32))
    return result.astype(jnp.bfloat16)

def reference(hidden_in, norm1_gain, qkv_weight, out_weight, norm2_gain, fc1_weight, fc2_weight, out_grad):
    batch, frames, patches, feature = hidden_in.shape
    head_cols = HEADS * HDIM
    tok_rows = batch * frames * patches
    flat_in = hidden_in.reshape(tok_rows, feature)
    x_hat1, _ = normalize(flat_in)
    norm_a = (x_hat1 * norm1_gain).astype(jnp.bfloat16)
    qkv = jnp.dot(norm_a, qkv_weight.reshape(feature, 3 * head_cols), preferred_element_type=jnp.float32).astype(jnp.bfloat16)
    qkv = qkv.reshape(batch, frames, patches, 3, HEADS, HDIM)
    attended = attend(qkv[:, :, :, 0], qkv[:, :, :, 1], qkv[:, :, :, 2]).reshape(tok_rows, head_cols)
    proj = jnp.dot(attended, out_weight, preferred_element_type=jnp.float32)
    mid = (flat_in.astype(jnp.float32) + proj).astype(jnp.bfloat16)
    x_hat2, inv_std2 = normalize(mid)
    norm_b = (x_hat2 * norm2_gain).astype(jnp.bfloat16)
    pre = jnp.dot(norm_b, fc1_weight, preferred_element_type=jnp.float32)
    act_full, gelu_grad = jax.vjp(gelu_tanh, pre)
    act = act_full.astype(jnp.bfloat16)
    down = lax.dot_general(act, fc2_weight, (((1,), (1,)), ((), ())), preferred_element_type=jnp.float32)
    block = (mid.astype(jnp.float32) + down).astype(jnp.bfloat16)
    grad_flat = out_grad.reshape(tok_rows, feature)
    grad_act = jnp.dot(grad_flat, fc2_weight, preferred_element_type=jnp.float32)
    grad_pre = gelu_grad(grad_act)[0].astype(jnp.bfloat16)
    grad_norm = lax.dot_general(grad_pre, fc1_weight, (((1,), (1,)), ((), ())), preferred_element_type=jnp.float32)
    grad_mid = norm_back(grad_norm, x_hat2, inv_std2, norm2_gain, grad_flat)
    grad_fc1 = lax.dot_general(norm_b, grad_pre, (((0,), (0,)), ((), ())), preferred_element_type=jnp.float32)
    grad_fc2 = lax.dot_general(grad_flat, act, (((0,), (0,)), ((), ())), preferred_element_type=jnp.float32)
    shape = hidden_in.shape
    return (block.reshape(shape), grad_mid.reshape(shape), grad_fc1, grad_fc2)
```

```python
import functools

import jax
import jax.numpy as jnp
import numpy as np
from jax import lax
from jax.experimental import pallas as pl
from jax.experimental.pallas import tpu as pltpu
from jax.sharding import PartitionSpec as P

MESH = pl.DeviceIdType.MESH
BF16 = jnp.bfloat16
F32 = jnp.float32

HDIM = 72
D = 1152
FQ = 1152
QC = 288
SLAB = 40
ROWS = 32 * SLAB
CA = 640
CB = 512
EPS = 1e-06
N_SEM = 160


def slab_sources():
    source = np.full((8, 4, SLAB), -1, np.int32)
    for z in range(8):
        for y in range(4):
            for core in range(2):
                first = ((z // 2) * 8 + y * 2 + core) * 36 + (z % 2) * 18
                source[z, y, core * 18 : core * 18 + 18] = np.arange(first, first + 18)
    return np.broadcast_to(source.reshape(1, ROWS), (8, ROWS)).copy()


def nn(a, b):
    return jnp.dot(a, b, preferred_element_type=F32)


def nt(a, b):
    return lax.dot_general(a, b, (((1,), (1,)), ((), ())), preferred_element_type=F32)


def normalize(values):
    center = values - jnp.mean(values, -1, keepdims=True)
    inv_std = lax.rsqrt(jnp.mean(center * center, -1, keepdims=True) + EPS)
    return center * inv_std, inv_std


def kernel(
    hid, gain1, wq_h, wo_h, gain2, w1_h, w2_h, og, idx,
    out_b, out_g, out_1, out_2,
    hs, gs, wq, wo, w1, w2, na, att, gflat, ga, act, gp, nb,
    pf, pb, xr1, xs2, xq, mid, xhat, inv2, bo, go,
    perm, nbp, gpp, lp, rp, lt,
    wa, ya1, yas, yaq, ra, za1, zas, zaq,
    wb, zb1, zbs, zbq, rb, yb1, ybs, ybq, fin,
    ssem, rsem, lsem, asem,
):
    t = lax.axis_index("tensor")
    s = lax.axis_index("seq")
    dp = lax.axis_index("dp")
    zh = s // 8
    y = (s // 2) % 4
    core = s % 2
    zz = zh * 2 + dp

    def wrap(value, size):
        return (value + 2 * size) % size

    def x_dev(step):
        return {"tensor": wrap(t + step, 4)}

    def y_dev(step):
        return {"seq": zh * 8 + wrap(y + step, 4) * 2 + core}

    def z_dev(step):
        other = wrap(zz + step, 8)
        return {"seq": (other // 2) * 8 + y * 2 + core, "dp": other % 2}

    core_dev = {"seq": s + 1 - 2 * core}

    def peer_seq(plane, a, k):
        return a * 8 + wrap(plane - zh - y - a, 4) * 2 + k

    barrier = pltpu.get_barrier_semaphore()
    for dev in (x_dev(1), x_dev(-1), y_dev(1), y_dev(-1), z_dev(1), z_dev(-1), core_dev):
        pl.semaphore_signal(barrier, inc=1, device_id=dev, device_id_type=MESH)
    for a in range(4):
        for k in range(2):
            peer = peer_seq(t, a, k)

            pl.semaphore_signal(barrier, inc=1, device_id={"seq": peer}, device_id_type=MESH)

    loads = [
        pltpu.make_async_copy(src, dst, lsem.at[i])
        for i, (src, dst) in enumerate(((wq_h, wq), (w2_h, w2), (wo_h, wo), (w1_h, w1)))
    ]
    for load in loads:
        load.start()
    pl.semaphore_wait(barrier, 15)

    count = [0]
    started = []

    def fresh(n=1):
        first = count[0]
        count[0] += n
        return first

    def send(src, dst, dev):
        i = fresh()
        copy = pltpu.make_async_remote_copy(
            src_ref=src, dst_ref=dst, send_sem=ssem.at[i], recv_sem=rsem.at[i], device_id=dev, device_id_type=MESH
        )
        copy.start()
        started.append(copy)
        return copy

    def exchange(src_of, dst, base):
        for a in range(4):
            for k in range(2):
                j = a * 2 + k
                peer = peer_seq(t, a, k)
                src = src_of(j, peer)

                @pl.when(peer != s)
                def _():
                    pltpu.make_async_remote_copy(
                        src_ref=src, dst_ref=dst, send_sem=ssem.at[base + j], recv_sem=rsem.at[base + zh * 2 + core],
                        device_id={"seq": peer}, device_id_type=MESH,
                    ).start()

                @pl.when(peer == s)
                def _():
                    pltpu.make_async_copy(src, dst, rsem.at[base + j]).start()

    def exchange_arrived(dst, base, j):
        pltpu.make_async_copy(dst, dst, rsem.at[base + j]).wait()

    def exchange_sent(src_of, base):
        for a in range(4):
            for k in range(2):
                j = a * 2 + k
                peer = peer_seq(t, a, k)
                src = src_of(j, peer)

                @pl.when(peer != s)
                def _():
                    pltpu.make_async_copy(src, src, ssem.at[base + j]).wait()

    base_h, base_g, base_b, base_gm = fresh(8), fresh(8), fresh(8), fresh(8)
    here = hs.at[t, zh * 2 + core]
    exchange(lambda j, peer: hid.at[peer], here, base_h)
    exchange(lambda j, peer: og.at[peer], gs.at[t, zh * 2 + core], base_g)

    def gather_first(view, arrived):
        copies = []
        for a in range(4):
            arrived(a)
            copies.append(
                (send(view(t, a), view(t, a), x_dev(1)), send(view(t, a), view(t, a), x_dev(-1)))
            )
        return copies

    def gather_second(view, copies):
        left, right = wrap(t - 1, 4), wrap(t + 1, 4)
        further = []
        for a in range(2):
            copies[a][0].wait_recv()
            further.append(send(view(left, a), view(left, a), x_dev(1)))
            copies[a + 2][1].wait_recv()
            further.append(send(view(right, a + 2), view(right, a + 2), x_dev(-1)))
        for a in range(2):
            copies[a + 2][0].wait_recv()
            copies[a][1].wait_recv()
        return further

    def gather_third(further):
        for copy in further:
            copy.wait_recv()

    def pair(ref):
        return lambda plane, a: ref.at[plane, pl.ds(a * 2, 2)]

    def slabs_arrived(dst, base):
        def arrived(a):
            for k in range(2):
                exchange_arrived(dst, base, a * 2 + k)

        return arrived

    def make_perm(i, carry):
        first = pl.multiple_of(i * 128, 128)
        row = lax.broadcasted_iota(jnp.int32, (128, ROWS), 0) + first
        perm[pl.ds(first, 128), :] = jnp.where(row == idx[0:1, :], 1.0, 0.0).astype(BF16)
        return carry

    lax.fori_loop(0, 9, make_perm, 0)

    g1 = gain1[0:1, :]

    def norm_share(plane):
        x_hat, _ = normalize(hs[plane].astype(F32).reshape(64, D))
        na[plane] = (x_hat * g1).astype(BF16)

    h_first = gather_first(pair(hs), slabs_arrived(here, base_h))
    norm_share(t)
    h_further = gather_second(pair(hs), h_first)
    norm_share(wrap(t - 1, 4))
    norm_share(wrap(t + 1, 4))
    g_first = gather_first(pair(gs), slabs_arrived(here, base_g))
    gather_third(h_further)
    norm_share(wrap(t + 2, 4))

    loads[0].wait()
    na_all = na[...].reshape(256, D)
    q = nt(na_all, wq[0:QC, :]).astype(BF16)
    k_ = nt(na_all, wq[QC : 2 * QC, :]).astype(BF16)
    v = nt(na_all, wq[2 * QC : 3 * QC, :]).astype(BF16)
    col = lax.broadcasted_iota(jnp.int32, (1, QC), 1)
    same = (lax.broadcasted_iota(jnp.int32, (256, 256), 0) & 7) == (lax.broadcasted_iota(jnp.int32, (256, 256), 1) & 7)
    total = jnp.zeros((256, QC), F32)
    for h in range(QC // HDIM):
        mine = (col >= h * HDIM) & (col < (h + 1) * HDIM)
        qh = jnp.where(mine, q, jnp.zeros_like(q))
        scores = nt(qh, k_) * HDIM ** (-0.5)
        scores = jnp.where(same, scores, -1e30)
        weights = jnp.exp(scores - jnp.max(scores, -1, keepdims=True))
        probs = (weights * (1.0 / jnp.sum(weights, -1, keepdims=True))).astype(BF16)
        total = jnp.where(mine, nn(probs, v), total)
    att[...] = total.astype(BF16)
    loads[2].wait()

    def partial_sums(u, product):
        for n in range(3):
            value = product(n)
            pf[u, :, :, n * 384 : n * 384 + 384] = value.reshape(4, 64, 384)
            pb[u, :, :, n * 384 : n * 384 + 384] = value.astype(BF16).reshape(4, 64, 384)

    def reduce_first(u):
        far, right, left = wrap(t + 2, 4), wrap(t + 1, 4), wrap(t - 1, 4)
        lo, hi = pl.ds(0, 32), pl.ds(32, 32)
        r1 = send(pb.at[u, far, lo], xr1.at[u, 0], x_dev(1))
        l1 = send(pb.at[u, far, hi], xr1.at[u, 1], x_dev(-1))
        r2 = send(pb.at[u, right, hi], xq.at[u, 0, hi], x_dev(1))
        l2 = send(pb.at[u, left, lo], xq.at[u, 1, lo], x_dev(-1))
        return r1, l1, r2, l2

    def reduce_second(u, copies):
        right, left = wrap(t + 1, 4), wrap(t - 1, 4)
        lo, hi = pl.ds(0, 32), pl.ds(32, 32)
        r1, l1, r2, l2 = copies
        r1.wait_recv()
        xs2[u, 0] = (pf[u, right, 0:32, :] + xr1[u, 0].astype(F32)).astype(BF16)
        r3 = send(xs2.at[u, 0], xq.at[u, 0, lo], x_dev(1))
        l1.wait_recv()
        xs2[u, 1] = (pf[u, left, 32:64, :] + xr1[u, 1].astype(F32)).astype(BF16)
        l3 = send(xs2.at[u, 1], xq.at[u, 1, hi], x_dev(-1))
        return r2, l2, r3, l3

    def reduce_third(u, copies):
        for copy in copies:
            copy.wait_recv()
        return pf[u, t] + xq[u, 0].astype(F32) + xq[u, 1].astype(F32)

    partial_sums(0, lambda n: nn(att[...], wo[:, n * 384 : n * 384 + 384]))
    p_first = reduce_first(0)

    g_further = gather_second(pair(gs), g_first)
    p_second = reduce_second(0, p_first)
    gather_third(g_further)
    for plane in range(4):
        gflat[plane] = gs[plane].astype(F32).reshape(64, D).astype(BF16)
    loads[1].wait()
    loads[3].wait()

    proj = reduce_third(0, p_second)
    mid_rows = (hs[t].astype(F32).reshape(64, D) + proj).astype(BF16)
    mid[...] = mid_rows
    x_hat2, inv_std2 = normalize(mid_rows.astype(F32))
    xhat[...] = x_hat2
    inv2[...] = inv_std2
    g2 = gain2[0:1, :]
    nb[t] = (x_hat2 * g2).astype(BF16)

    def quarter(ref):
        return lambda plane, a: ref.at[plane, pl.ds(a * 16, 16)]

    n_first = gather_first(quarter(nb), lambda a: None)

    g_all = gflat[...].reshape(256, D)
    for n in range(3):
        c = slice(n * 384, n * 384 + 384)
        ga[:, c] = nn(g_all, w2[:, c])
    n_further = gather_second(quarter(nb), n_first)
    for n in range(2):
        c = slice(n * 640, n * 640 + 640)
        gpp[:, c] = nn(g_all, perm[:, c]).astype(BF16)
    gather_third(n_further)

    root = (2.0 / np.pi) ** 0.5
    nb_all = nb[...].reshape(256, D)
    for n in range(3):
        c = slice(n * 384, n * 384 + 384)
        pre = nn(nb_all, w1[:, c])
        square = pre * pre
        th = jnp.tanh(root * (pre + 0.044715 * (square * pre)))
        half = 0.5 * (1.0 + th)
        act[:, c] = (pre * half).astype(BF16)
        slope = half + 0.5 * pre * (1.0 - th * th) * (root * (1.0 + 3 * 0.044715 * square))
        gp[:, c] = (ga[:, c] * slope).astype(BF16)
    for n in range(2):
        c = slice(n * 640, n * 640 + 640)
        nbp[:, c] = nn(nb_all, perm[:, c]).astype(BF16)

    sl, sr = fresh(), fresh()

    def swap(src, dst, i):
        return pltpu.make_async_remote_copy(
            src_ref=src, dst_ref=dst, send_sem=ssem.at[i], recv_sem=rsem.at[i], device_id=core_dev, device_id_type=MESH
        )

    @pl.when(core == 0)
    def _():
        swap(gpp, lp, sl).start()
        swap(act, rp.at[1], sr).start()
        rp[0] = gp[...]
        lt[:, 0:256] = nbp[...].T

    @pl.when(core == 1)
    def _():
        swap(nbp, lp, sl).start()
        swap(gp, rp.at[1], sr).start()
        rp[0] = act[...]
        lt[:, 0:256] = gpp[...].T

    swap_l, swap_r = swap(gpp, lp, sl), swap(act, rp.at[1], sr)
    started.extend((swap_l, swap_r))

    partial_sums(1, lambda n: nt(act[...], w2[n * 384 : n * 384 + 384, :]))
    d_first = reduce_first(1)
    partial_sums(2, lambda n: nt(gp[...], w1[n * 384 : n * 384 + 384, :]))
    e_first = reduce_first(2)
    d_second = reduce_second(1, d_first)

    swap_l.wait_recv()
    lt[:, 256:512] = lp[...].T
    swap_r.wait_recv()

    def grad_b(i, carry):
        block = lt[pl.ds(pl.multiple_of(i * 320, 320), 320), :]
        value = nn(block, rp[:, :, CA:].reshape(512, CB))
        for m in range(8):
            wb[i * 2 + m // 4, m % 4] = value[m * SLAB : (m + 1) * SLAB].astype(BF16)
        return carry

    def grad_a(i, carry):
        block = lt[pl.ds(pl.multiple_of(i * 320, 320), 320), :]
        value = nn(block, rp[:, :, :CA].reshape(512, CA))
        for m in range(8):
            wa[m % 4, i * 2 + m // 4] = value[m * SLAB : (m + 1) * SLAB].astype(BF16)
        return carry

    def add(a, b):
        return (a.astype(F32) + b.astype(F32)).astype(BF16)

    def b_first(u):
        far = wrap(zz + 4, 8)
        return [send(wb.at[far, u * 2 + d], zb1.at[u, d], z_dev(1 - 2 * d)) for d in range(2)]

    def b_step(n, u, copies):
        result = []
        for d in range(2):
            sign = 1 - 2 * d
            chunk = wrap(zz + sign * (3 - n), 8)
            copies[d].wait_recv()
            if n == 0:
                zbs[n, u, d, d] = add(wb[chunk, u * 2 + d], zb1[u, d])
                zbs[n, u, d, 1 - d] = wb[chunk, u * 2 + 1 - d]
            else:
                for i in range(2):
                    zbs[n, u, d, i] = add(wb[chunk, u * 2 + i], zbq[n - 1, u, d, i])
            result.append(send(zbs.at[n, u, d], zbq.at[n, u, d], z_dev(sign)))
        return result

    def b_last(u, copies):
        for copy in copies:
            copy.wait_recv()
        for i in range(2):
            rb[u * 2 + i] = (
                wb[zz, u * 2 + i].astype(F32) + zbq[2, u, 0, i].astype(F32) + zbq[2, u, 1, i].astype(F32)
            ).astype(BF16)

    def a_first():
        far, up, down = wrap(y + 2, 4), wrap(y + 1, 4), wrap(y - 1, 4)
        lo, hi = pl.ds(0, 4), pl.ds(4, 4)
        u1 = send(wa.at[far, lo], ya1.at[0], y_dev(1))
        d1 = send(wa.at[far, hi], ya1.at[1], y_dev(-1))
        u2 = send(wa.at[up, hi], yaq.at[0, hi], y_dev(1))
        d2 = send(wa.at[down, lo], yaq.at[1, lo], y_dev(-1))
        return u1, d1, u2, d2

    def a_second(copies):
        up, down = wrap(y + 1, 4), wrap(y - 1, 4)
        u1, d1, u2, d2 = copies
        u1.wait_recv()

        def body_up(i, carry):
            yas[0, i] = add(wa[up, i], ya1[0, i])
            return carry

        lax.fori_loop(0, 4, body_up, 0)
        u3 = send(yas.at[0], yaq.at[0, pl.ds(0, 4)], y_dev(1))
        d1.wait_recv()

        def body_down(i, carry):
            yas[1, i] = add(wa[down, i + 4], ya1[1, i])
            return carry

        lax.fori_loop(0, 4, body_down, 0)
        d3 = send(yas.at[1], yaq.at[1, pl.ds(4, 4)], y_dev(-1))
        return u2, d2, u3, d3

    def a_last(copies):
        for copy in copies:
            copy.wait_recv()

        def body(i, carry):
            ra[i] = (wa[y, i].astype(F32) + yaq[0, i].astype(F32) + yaq[1, i].astype(F32)).astype(BF16)
            return carry

        lax.fori_loop(0, 8, body, 0)

    HALF = 384

    def az_first():
        far = wrap(zz + 4, 8)
        up = send(ra.at[far, :, pl.ds(0, HALF)], za1.at[0, :, pl.ds(0, HALF)], z_dev(1))
        down = send(ra.at[far, :, pl.ds(HALF, CA - HALF)], za1.at[1, :, pl.ds(HALF, CA - HALF)], z_dev(-1))
        return [up, down]

    def az_step(n, copies):
        result = []
        for d in range(2):
            sign = 1 - 2 * d
            chunk = wrap(zz + sign * (3 - n), 8)
            copies[d].wait_recv()
            if n == 0:
                taken = slice(0, HALF) if d == 0 else slice(HALF, CA)
                other = slice(HALF, CA) if d == 0 else slice(0, HALF)
                zas[n, d, :, taken] = add(ra[chunk, :, taken], za1[d, :, taken])
                zas[n, d, :, other] = ra[chunk, :, other]
            else:
                zas[n, d] = add(ra[chunk], zaq[n - 1, d])
            result.append(send(zas.at[n, d], zaq.at[n, d], z_dev(sign)))
        return result

    def az_last(copies):
        for copy in copies:
            copy.wait_recv()
        return ra[zz].astype(F32) + zaq[2, 0].astype(F32) + zaq[2, 1].astype(F32)

    def by_first():
        far, up, down = wrap(y + 2, 4), wrap(y + 1, 4), wrap(y - 1, 4)
        lo, hi = pl.ds(0, 256), pl.ds(256, 256)
        u1 = send(rb.at[far, :, lo], yb1.at[0], y_dev(1))
        d1 = send(rb.at[far, :, hi], yb1.at[1], y_dev(-1))
        u2 = send(rb.at[up, :, hi], ybq.at[0, :, hi], y_dev(1))
        d2 = send(rb.at[down, :, lo], ybq.at[1, :, lo], y_dev(-1))
        return u1, d1, u2, d2

    def by_second(copies):
        up, down = wrap(y + 1, 4), wrap(y - 1, 4)
        u1, d1, u2, d2 = copies
        u1.wait_recv()
        ybs[0] = add(rb[up, :, 0:256], yb1[0])
        u3 = send(ybs.at[0], ybq.at[0, :, pl.ds(0, 256)], y_dev(1))
        d1.wait_recv()
        ybs[1] = add(rb[down, :, 256:512], yb1[1])
        d3 = send(ybs.at[1], ybq.at[1, :, pl.ds(256, 256)], y_dev(-1))
        return u2, d2, u3, d3

    def by_last(copies):
        for copy in copies:
            copy.wait_recv()
        return rb[y].astype(F32) + ybq[0].astype(F32) + ybq[1].astype(F32)

    lax.fori_loop(0, 4, grad_b, 0)
    b1 = [b_first(0), b_first(1)]
    lax.fori_loop(0, 4, grad_a, 0)
    a1 = a_first()
    e_second = reduce_second(2, e_first)
    b2 = [b_step(0, u, b1[u]) for u in range(2)]

    down_rows = reduce_third(1, d_second)
    bo[...] = (mid[...].astype(F32) + down_rows).reshape(8, 8, D).astype(BF16)
    exchange(lambda j, peer: bo.at[j], out_b.at[s], base_b)
    a2 = a_second(a1)
    b3 = [b_step(1, u, b2[u]) for u in range(2)]

    scaled = reduce_third(2, e_second) * g2
    x_hat2 = xhat[...]
    plain = jnp.mean(scaled, -1, keepdims=True)
    cross = jnp.mean(scaled * x_hat2, -1, keepdims=True)
    upstream = gs[t].astype(F32).reshape(64, D)
    go[...] = (upstream + inv2[...] * (scaled - plain - x_hat2 * cross)).reshape(8, 8, D).astype(BF16)
    exchange(lambda j, peer: go.at[j], out_g.at[s], base_gm)

    def out_view(ref):
        return lambda plane, a: ref.at[pl.ds(peer_seq(plane, a, 0), 2)]

    o_first = gather_first(out_view(out_b), slabs_arrived(out_b.at[s], base_b))
    b4 = [b_step(2, u, b3[u]) for u in range(2)]
    m_first = gather_first(out_view(out_g), slabs_arrived(out_g.at[s], base_gm))
    o_further = gather_second(out_view(out_b), o_first)
    a_last(a2)
    az1 = az_first()
    b_last(0, b4[0])
    b_last(1, b4[1])
    by1 = by_first()
    m_further = gather_second(out_view(out_g), m_first)
    az2 = az_step(0, az1)
    by2 = by_second(by1)
    az3 = az_step(1, az2)
    fin_b = by_last(by2)
    az4 = az_step(2, az3)
    fin_a = az_last(az4)
    for c in range(2):
        fin[c, :, 0:CA] = fin_a[c * 18 : c * 18 + 18]
        fin[c, :, CA:] = fin_b[c * 18 : c * 18 + 18]
    sf = fresh()

    @pl.when(core == 0)
    def _():
        swap(fin.at[1], out_1, sf).start()
        own = pltpu.make_async_copy(fin.at[0], out_1, asem)
        own.start()
        own.wait()
        swap(fin.at[1], out_2, sf).wait()

    @pl.when(core == 1)
    def _():
        swap(fin.at[0], out_2, sf).start()
        own = pltpu.make_async_copy(fin.at[1], out_2, asem)
        own.start()
        own.wait()
        swap(fin.at[0], out_1, sf).wait()

    gather_third(o_further)
    gather_third(m_further)

    exchange_sent(lambda j, peer: hid.at[peer], base_h)
    exchange_sent(lambda j, peer: og.at[peer], base_g)
    exchange_sent(lambda j, peer: bo.at[j], base_b)
    exchange_sent(lambda j, peer: go.at[j], base_gm)
    for copy in started:
        copy.wait_send()


def local(hidden_in, norm1_gain, qkv_weight, out_weight, norm2_gain, fc1_weight, fc2_weight, out_grad):
    anywhere = pl.BlockSpec(memory_space=pl.ANY)
    vmem = pl.BlockSpec(memory_space=pltpu.VMEM)
    shapes = [
        ((4, 8, 8, D), BF16), ((4, 8, 8, D), BF16),
        ((3 * QC, D), BF16), ((QC, D), BF16), ((D, FQ), BF16), ((D, FQ), BF16),
        ((4, 64, D), BF16), ((256, QC), BF16), ((4, 64, D), BF16), ((256, FQ), F32),
        ((256, FQ), BF16), ((256, FQ), BF16), ((4, 64, D), BF16),
        ((3, 4, 64, D), F32), ((3, 4, 64, D), BF16),
        ((3, 2, 32, D), BF16), ((3, 2, 32, D), BF16), ((3, 2, 64, D), BF16),
        ((64, D), BF16), ((64, D), F32), ((64, 1), F32), ((8, 8, D), BF16), ((8, 8, D), BF16),
        ((D, ROWS), BF16), ((256, ROWS), BF16), ((256, ROWS), BF16),
        ((256, ROWS), BF16), ((2, 256, FQ), BF16), ((ROWS, 512), BF16),
        ((4, 8, SLAB, CA), BF16), ((2, 4, SLAB, CA), BF16), ((2, 4, SLAB, CA), BF16), ((2, 8, SLAB, CA), BF16),
        ((8, SLAB, CA), BF16), ((2, SLAB, CA), BF16), ((3, 2, SLAB, CA), BF16), ((3, 2, SLAB, CA), BF16),
        ((8, 4, SLAB, CB), BF16), ((2, 2, SLAB, CB), BF16), ((3, 2, 2, 2, SLAB, CB), BF16), ((3, 2, 2, 2, SLAB, CB), BF16),
        ((4, SLAB, CB), BF16), ((2, SLAB, 256), BF16), ((2, SLAB, 256), BF16), ((2, SLAB, CB), BF16),
        ((2, 18, FQ), F32),
    ]
    scratch = [pltpu.VMEM(shape, kind) for shape, kind in shapes]
    scratch += [
        pltpu.SemaphoreType.DMA((N_SEM,)), pltpu.SemaphoreType.DMA((N_SEM,)),
        pltpu.SemaphoreType.DMA((4,)), pltpu.SemaphoreType.DMA,
    ]
    rows = lambda gain: jnp.broadcast_to(gain.reshape(1, D), (8, D))
    block, grad_mid, grad_fc1, grad_fc2 = pl.pallas_call(
        kernel,
        out_shape=[
            jax.ShapeDtypeStruct((32, 8, D), BF16),
            jax.ShapeDtypeStruct((32, 8, D), BF16),
            jax.ShapeDtypeStruct((18, FQ), F32),
            jax.ShapeDtypeStruct((18, FQ), F32),
        ],
        in_specs=[anywhere, vmem, anywhere, anywhere, vmem, anywhere, anywhere, anywhere, vmem],
        out_specs=[anywhere] * 4,
        scratch_shapes=scratch,
        compiler_params=pltpu.CompilerParams(
            collective_id=0, has_side_effects=True, vmem_limit_bytes=60 * 1024 * 1024
        ),
    )(
        hidden_in.reshape(32, 8, D),
        rows(norm1_gain),
        qkv_weight.transpose(1, 2, 0).reshape(3 * QC, D),
        out_weight,
        rows(norm2_gain),
        fc1_weight,
        fc2_weight,
        out_grad.reshape(32, 8, D),
        jnp.asarray(slab_sources()),
    )
    shape = hidden_in.shape
    return block.reshape(shape), grad_mid.reshape(shape), grad_fc1, grad_fc2


def solution(mesh):
    return jax.shard_map(
        local,
        mesh=mesh,
        in_specs=(
            P("dp", "seq", None, None),
            P(),
            P(None, None, "tensor"),
            P("tensor", None),
            P(),
            P(None, "tensor"),
            P(None, "tensor"),
            P("dp", "seq", None, None),
        ),
        out_specs=(
            P("dp", "seq", None, None),
            P("dp", "seq", None, None),
            P(("seq", "dp"), "tensor"),
            P(("seq", "dp"), "tensor"),
        ),
        check_vma=False,
    )
```

```python
import functools

import jax
import jax.numpy as jnp
import numpy as np
from jax import lax
from jax.experimental import pallas as pl
from jax.experimental.pallas import tpu as pltpu
from jax.sharding import PartitionSpec as P

MESH = pl.DeviceIdType.MESH
BF16 = jnp.bfloat16
F32 = jnp.float32

HDIM = 72
D = 1152
FQ = 1152
QC = 288
SLAB = 40
ROWS = 32 * SLAB
CA = 640
CB = 512
EPS = 1e-06
N_SEM = 160


def slab_sources(first, count):
    n = lax.broadcasted_iota(jnp.int32, (count, 1), 0) + first
    slab = (n * 1639) >> 16
    within = n - slab * SLAB
    core = jnp.where(within >= 18, 1, 0)
    z, y = slab >> 2, slab & 3
    source = (((z >> 1) * 4 + y) * 2 + core) * 36 + (z & 1) * 18 + within - core * 18
    return jnp.where(within < 36, source, -1)


def nn(a, b):
    return jnp.dot(a, b, preferred_element_type=F32)


def nt(a, b):
    return lax.dot_general(a, b, (((1,), (1,)), ((), ())), preferred_element_type=F32)


def normalize(values):
    center = values - jnp.mean(values, -1, keepdims=True)
    inv_std = lax.rsqrt(jnp.mean(center * center, -1, keepdims=True) + EPS)
    return center * inv_std, inv_std


def kernel(
    hid, gain1, wq_h, wo_h, gain2, w1_h, w2_h, og,
    out_b, out_g, out_1, out_2,
    hs, gs, wq, wo, w1, w2, na, att, gflat, ga, nb,
    pf, pb, xr1, xs2, xq, ms, mr, xhat, inv2, bo, go,
    perm, lbuf, rbuf,
    wa, ya1, yas, yaq, ra, za1, zas, zaq,
    wb, zb1, zbs, zbq, rb, yb1, ybs, ybq, fin,
    ssem, rsem, lsem, gsem, osem, asem,
):
    t = lax.axis_index("tensor")
    s = lax.axis_index("seq")
    dp = lax.axis_index("dp")
    zh = s // 8
    y = (s // 2) % 4
    core = s % 2
    zz = zh * 2 + dp

    def wrap(value, size):
        return (value + 2 * size) % size

    def x_dev(step):
        return {"tensor": wrap(t + step, 4)}

    def y_dev(step):
        return {"seq": zh * 8 + wrap(y + step, 4) * 2 + core}

    def z_dev(step):
        other = wrap(zz + step, 8)
        return {"seq": (other // 2) * 8 + y * 2 + core, "dp": other % 2}

    core_dev = {"seq": s + 1 - 2 * core}

    def peer_seq(plane, a, k):
        return a * 8 + wrap(plane - zh - y - a, 4) * 2 + k

    barrier = pltpu.get_barrier_semaphore()
    for dev in (x_dev(1), x_dev(-1), y_dev(1), y_dev(-1), z_dev(1), z_dev(-1), core_dev):
        pl.semaphore_signal(barrier, inc=1, device_id=dev, device_id_type=MESH)
    for a in range(4):
        for k in range(2):
            peer = peer_seq(t, a, k)

            pl.semaphore_signal(barrier, inc=1, device_id={"seq": peer}, device_id_type=MESH)

    loads = [
        pltpu.make_async_copy(src, dst, lsem.at[i])
        for i, (src, dst) in enumerate(((wq_h, wq), (w2_h, w2), (wo_h, wo), (w1_h, w1)))
    ]
    for load in loads:
        load.start()
    pl.semaphore_wait(barrier, 15)

    count = [0]
    started = []

    def fresh(n=1):
        first = count[0]
        count[0] += n
        return first

    def send(src, dst, dev):
        i = fresh()
        copy = pltpu.make_async_remote_copy(
            src_ref=src, dst_ref=dst, send_sem=ssem.at[i], recv_sem=rsem.at[i], device_id=dev, device_id_type=MESH
        )
        copy.start()
        started.append(copy)
        return copy

    def exchange(src_of, dst, base):
        for a in range(4):
            for k in range(2):
                j = a * 2 + k
                peer = peer_seq(t, a, k)
                src = src_of(j, peer)

                @pl.when(peer != s)
                def _():
                    pltpu.make_async_remote_copy(
                        src_ref=src, dst_ref=dst, send_sem=ssem.at[base + j], recv_sem=rsem.at[base + zh * 2 + core],
                        device_id={"seq": peer}, device_id_type=MESH,
                    ).start()

                @pl.when(peer == s)
                def _():
                    pltpu.make_async_copy(src, dst, rsem.at[base + j]).start()

    def exchange_arrived(dst, base, j):
        pltpu.make_async_copy(dst, dst, rsem.at[base + j]).wait()

    def exchange_sent(src_of, base):
        for a in range(4):
            for k in range(2):
                j = a * 2 + k
                peer = peer_seq(t, a, k)
                src = src_of(j, peer)

                @pl.when(peer != s)
                def _():
                    pltpu.make_async_copy(src, src, ssem.at[base + j]).wait()

    base_h, base_m = fresh(8), fresh(8)
    here = hs.at[t, zh * 2 + core]
    exchange(lambda j, peer: hid.at[peer], here, base_h)

    turned = [
        pltpu.make_async_copy(
            og.at[pl.ds(peer_seq(plane, a, 0), 2)], gs.at[plane, pl.ds(a * 2, 2)], gsem.at[plane * 4 + a]
        )
        for plane in range(4)
        for a in range(4)
    ]
    for copy in turned:
        copy.start()

    def gather_first(view, arrived, own=None):
        copies = []
        for a in range(4):
            arrived(a)
            src = view(t, a) if own is None else own(a)
            copies.append((send(src, view(t, a), x_dev(1)), send(src, view(t, a), x_dev(-1))))
        return copies

    def gather_second(view, copies):
        left, right = wrap(t - 1, 4), wrap(t + 1, 4)
        further = []
        for a in range(2):
            copies[a][0].wait_recv()
            further.append(send(view(left, a), view(left, a), x_dev(1)))
            copies[a + 2][1].wait_recv()
            further.append(send(view(right, a + 2), view(right, a + 2), x_dev(-1)))
        for a in range(2):
            copies[a + 2][0].wait_recv()
            copies[a][1].wait_recv()
        return further

    def gather_third(further):
        for copy in further:
            copy.wait_recv()

    def pair(ref):
        return lambda plane, a: ref.at[plane, pl.ds(a * 2, 2)]

    def slabs_arrived(dst, base):
        def arrived(a):
            for k in range(2):
                exchange_arrived(dst, base, a * 2 + k)

        return arrived

    def make_perm(i, carry):
        first = pl.multiple_of(i * 128, 128)
        wanted = slab_sources(first, 128)
        perm[pl.ds(first, 128), :] = jnp.where(
            lax.broadcasted_iota(jnp.int32, (128, D), 1) == wanted, 1.0, 0.0
        ).astype(BF16)
        return carry

    lax.fori_loop(0, ROWS // 128, make_perm, 0)

    g1 = gain1[...].reshape(1, D)

    def norm_share(plane):
        x_hat, _ = normalize(hs[plane].astype(F32).reshape(64, D))
        na[plane] = (x_hat * g1).astype(BF16)

    h_first = gather_first(pair(hs), slabs_arrived(here, base_h))
    norm_share(t)
    h_further = gather_second(pair(hs), h_first)
    norm_share(wrap(t - 1, 4))
    norm_share(wrap(t + 1, 4))
    gather_third(h_further)
    norm_share(wrap(t + 2, 4))

    loads[0].wait()
    na_all = na[...].reshape(256, D)
    q = nt(na_all, wq[0:QC, :]).astype(BF16)
    k_ = nt(na_all, wq[QC : 2 * QC, :]).astype(BF16)
    v = nt(na_all, wq[2 * QC : 3 * QC, :]).astype(BF16)
    col = lax.broadcasted_iota(jnp.int32, (1, QC), 1)
    same = (lax.broadcasted_iota(jnp.int32, (256, 256), 0) & 7) == (lax.broadcasted_iota(jnp.int32, (256, 256), 1) & 7)
    total = jnp.zeros((256, QC), F32)
    for h in range(QC // HDIM):
        mine = (col >= h * HDIM) & (col < (h + 1) * HDIM)
        qh = jnp.where(mine, q, jnp.zeros_like(q))
        scores = nt(qh, k_) * HDIM ** (-0.5)
        scores = jnp.where(same, scores, -1e30)
        weights = jnp.exp(scores - jnp.max(scores, -1, keepdims=True))
        probs = (weights * (1.0 / jnp.sum(weights, -1, keepdims=True))).astype(BF16)
        total = jnp.where(mine, nn(probs, v), total)
    att[...] = total.astype(BF16)
    loads[2].wait()

    def partial_sums(u, product):
        for n in range(3):
            value = product(n)
            pf[u, :, :, n * 384 : n * 384 + 384] = value.reshape(4, 64, 384)
            pb[u, :, :, n * 384 : n * 384 + 384] = value.astype(BF16).reshape(4, 64, 384)

    def reduce_first(u):
        far, right, left = wrap(t + 2, 4), wrap(t + 1, 4), wrap(t - 1, 4)
        lo, hi = pl.ds(0, 32), pl.ds(32, 32)
        r1 = send(pb.at[u, far, lo], xr1.at[u, 0], x_dev(1))
        l1 = send(pb.at[u, far, hi], xr1.at[u, 1], x_dev(-1))
        r2 = send(pb.at[u, right, hi], xq.at[u, 0, hi], x_dev(1))
        l2 = send(pb.at[u, left, lo], xq.at[u, 1, lo], x_dev(-1))
        return r1, l1, r2, l2

    def reduce_second(u, copies):
        right, left = wrap(t + 1, 4), wrap(t - 1, 4)
        lo, hi = pl.ds(0, 32), pl.ds(32, 32)
        r1, l1, r2, l2 = copies
        r1.wait_recv()
        xs2[u, 0] = (pf[u, right, 0:32, :] + xr1[u, 0].astype(F32)).astype(BF16)
        r3 = send(xs2.at[u, 0], xq.at[u, 0, lo], x_dev(1))
        l1.wait_recv()
        xs2[u, 1] = (pf[u, left, 32:64, :] + xr1[u, 1].astype(F32)).astype(BF16)
        l3 = send(xs2.at[u, 1], xq.at[u, 1, hi], x_dev(-1))
        return r2, l2, r3, l3

    def reduce_third(u, copies):
        for copy in copies:
            copy.wait_recv()
        return pf[u, t] + xq[u, 0].astype(F32) + xq[u, 1].astype(F32)

    partial_sums(0, lambda n: nn(att[...], wo[:, n * 384 : n * 384 + 384]))
    p_first = reduce_first(0)

    p_second = reduce_second(0, p_first)

    for copy in turned:
        copy.wait()
    for plane in range(4):
        gflat[plane] = gs[plane].astype(F32).reshape(64, D).astype(BF16)
    loads[1].wait()
    loads[3].wait()

    proj = reduce_third(0, p_second)
    ms[...] = (hs[t].astype(F32).reshape(64, D) + proj).reshape(8, 8, D).astype(BF16)
    back = mr.at[zh * 2 + core]
    exchange(lambda j, peer: ms.at[j], back, base_m)
    g_all = gflat[...].reshape(256, D)
    for n in range(3):
        c = slice(n * 384, n * 384 + 384)
        ga[:, c] = nn(g_all, w2[:, c])
    for j in range(8):
        exchange_arrived(back, base_m, j)

    mid_rows = mr[...].astype(F32).reshape(64, D)
    x_hat2, inv_std2 = normalize(mid_rows)
    xhat[...] = x_hat2
    inv2[...] = inv_std2
    g2 = gain2[...].reshape(1, D)
    nb[t] = (x_hat2 * g2).astype(BF16)

    def quarter(ref):
        return lambda plane, a: ref.at[plane, pl.ds(a * 16, 16)]

    n_first = gather_first(quarter(nb), lambda a: None)

    for n in range(2):
        c = slice(n * 640, n * 640 + 640)
        lbuf[0, c, :] = nt(perm[c, :], g_all).astype(BF16)
    n_further = gather_second(quarter(nb), n_first)
    gather_third(n_further)
    nb_all = nb[...].reshape(256, D)
    for n in range(2):
        c = slice(n * 640, n * 640 + 640)
        lbuf[1, c, :] = nt(perm[c, :], nb_all).astype(BF16)

    swapped = [send(lbuf.at[core], lbuf.at[2], core_dev)]
    kept = 1 - core

    root = (2.0 / np.pi) ** 0.5
    for n in range(3):
        c = slice(n * 384, n * 384 + 384)
        pre = nn(nb_all, w1[:, c])
        square = pre * pre
        th = jnp.tanh(root * (pre + 0.044715 * (square * pre)))
        half = 0.5 * (1.0 + th)
        rbuf[0, :, c] = (pre * half).astype(BF16)
        slope = half + 0.5 * pre * (1.0 - th * th) * (root * (1.0 + 3 * 0.044715 * square))
        rbuf[1, :, c] = (ga[:, c] * slope).astype(BF16)
        part = pl.ds(n * 384, 384)
        swapped.append(send(rbuf.at[core, :, part], rbuf.at[2, :, part], core_dev))

    partial_sums(1, lambda n: nt(rbuf[0], w2[n * 384 : n * 384 + 384, :]))
    d_first = reduce_first(1)
    partial_sums(2, lambda n: nt(rbuf[1], w1[n * 384 : n * 384 + 384, :]))
    e_first = reduce_first(2)
    d_second = reduce_second(1, d_first)
    for copy in swapped:
        copy.wait_recv()

    def grad_b(i, carry):
        rows = pl.ds(pl.multiple_of(i * 320, 320), 320)
        value = nn(lbuf[kept, rows, :], rbuf[kept, :, CA:]) + nn(lbuf[2, rows, :], rbuf[2, :, CA:])
        for m in range(8):
            wb[i * 2 + m // 4, m % 4] = value[m * SLAB : (m + 1) * SLAB].astype(BF16)
        return carry

    def grad_a(i, carry):
        rows = pl.ds(pl.multiple_of(i * 320, 320), 320)
        value = nn(lbuf[kept, rows, :], rbuf[kept, :, :CA]) + nn(lbuf[2, rows, :], rbuf[2, :, :CA])
        for m in range(8):
            wa[m % 4, i * 2 + m // 4] = value[m * SLAB : (m + 1) * SLAB].astype(BF16)
        return carry

    def add(a, b):
        return (a.astype(F32) + b.astype(F32)).astype(BF16)

    def b_first(u):
        far = wrap(zz + 4, 8)
        return [send(wb.at[far, u * 2 + d], zb1.at[u, d], z_dev(1 - 2 * d)) for d in range(2)]

    def b_step(n, u, copies):
        result = []
        for d in range(2):
            sign = 1 - 2 * d
            chunk = wrap(zz + sign * (3 - n), 8)
            copies[d].wait_recv()
            if n == 0:
                zbs[n, u, d, d] = add(wb[chunk, u * 2 + d], zb1[u, d])
                zbs[n, u, d, 1 - d] = wb[chunk, u * 2 + 1 - d]
            else:
                for i in range(2):
                    zbs[n, u, d, i] = add(wb[chunk, u * 2 + i], zbq[n - 1, u, d, i])
            result.append(send(zbs.at[n, u, d], zbq.at[n, u, d], z_dev(sign)))
        return result

    def b_last(u, copies):
        for copy in copies:
            copy.wait_recv()
        for i in range(2):
            rb[u * 2 + i] = (
                wb[zz, u * 2 + i].astype(F32) + zbq[2, u, 0, i].astype(F32) + zbq[2, u, 1, i].astype(F32)
            ).astype(BF16)

    def a_first():
        far, up, down = wrap(y + 2, 4), wrap(y + 1, 4), wrap(y - 1, 4)
        lo, hi = pl.ds(0, 4), pl.ds(4, 4)
        u1 = send(wa.at[far, lo], ya1.at[0], y_dev(1))
        d1 = send(wa.at[far, hi], ya1.at[1], y_dev(-1))
        u2 = send(wa.at[up, hi], yaq.at[0, hi], y_dev(1))
        d2 = send(wa.at[down, lo], yaq.at[1, lo], y_dev(-1))
        return u1, d1, u2, d2

    def a_second(copies):
        up, down = wrap(y + 1, 4), wrap(y - 1, 4)
        u1, d1, u2, d2 = copies
        u1.wait_recv()

        def body_up(i, carry):
            yas[0, i] = add(wa[up, i], ya1[0, i])
            return carry

        lax.fori_loop(0, 4, body_up, 0)
        u3 = send(yas.at[0], yaq.at[0, pl.ds(0, 4)], y_dev(1))
        d1.wait_recv()

        def body_down(i, carry):
            yas[1, i] = add(wa[down, i + 4], ya1[1, i])
            return carry

        lax.fori_loop(0, 4, body_down, 0)
        d3 = send(yas.at[1], yaq.at[1, pl.ds(4, 4)], y_dev(-1))
        return u2, d2, u3, d3

    def a_last(copies):
        for copy in copies:
            copy.wait_recv()

        def body(i, carry):
            ra[i] = (wa[y, i].astype(F32) + yaq[0, i].astype(F32) + yaq[1, i].astype(F32)).astype(BF16)
            return carry

        lax.fori_loop(0, 8, body, 0)

    HALF = 384

    def az_first():
        far = wrap(zz + 4, 8)
        up = send(ra.at[far, :, pl.ds(0, HALF)], za1.at[0, :, pl.ds(0, HALF)], z_dev(1))
        down = send(ra.at[far, :, pl.ds(HALF, CA - HALF)], za1.at[1, :, pl.ds(HALF, CA - HALF)], z_dev(-1))
        return [up, down]

    def az_step(n, copies):
        result = []
        for d in range(2):
            sign = 1 - 2 * d
            chunk = wrap(zz + sign * (3 - n), 8)
            copies[d].wait_recv()
            if n == 0:
                taken = slice(0, HALF) if d == 0 else slice(HALF, CA)
                other = slice(HALF, CA) if d == 0 else slice(0, HALF)
                zas[n, d, :, taken] = add(ra[chunk, :, taken], za1[d, :, taken])
                zas[n, d, :, other] = ra[chunk, :, other]
            else:
                zas[n, d] = add(ra[chunk], zaq[n - 1, d])
            result.append(send(zas.at[n, d], zaq.at[n, d], z_dev(sign)))
        return result

    def az_last(copies):
        for copy in copies:
            copy.wait_recv()
        return ra[zz].astype(F32) + zaq[2, 0].astype(F32) + zaq[2, 1].astype(F32)

    def by_first():
        far, up, down = wrap(y + 2, 4), wrap(y + 1, 4), wrap(y - 1, 4)
        lo, hi = pl.ds(0, 256), pl.ds(256, 256)
        u1 = send(rb.at[far, :, lo], yb1.at[0], y_dev(1))
        d1 = send(rb.at[far, :, hi], yb1.at[1], y_dev(-1))
        u2 = send(rb.at[up, :, hi], ybq.at[0, :, hi], y_dev(1))
        d2 = send(rb.at[down, :, lo], ybq.at[1, :, lo], y_dev(-1))
        return u1, d1, u2, d2

    def by_second(copies):
        up, down = wrap(y + 1, 4), wrap(y - 1, 4)
        u1, d1, u2, d2 = copies
        u1.wait_recv()
        ybs[0] = add(rb[up, :, 0:256], yb1[0])
        u3 = send(ybs.at[0], ybq.at[0, :, pl.ds(0, 256)], y_dev(1))
        d1.wait_recv()
        ybs[1] = add(rb[down, :, 256:512], yb1[1])
        d3 = send(ybs.at[1], ybq.at[1, :, pl.ds(256, 256)], y_dev(-1))
        return u2, d2, u3, d3

    def by_last(copies):
        for copy in copies:
            copy.wait_recv()
        return rb[y].astype(F32) + ybq[0].astype(F32) + ybq[1].astype(F32)

    lax.fori_loop(0, 4, grad_b, 0)
    b1 = [b_first(0), b_first(1)]
    lax.fori_loop(0, 4, grad_a, 0)
    a1 = a_first()
    e_second = reduce_second(2, e_first)
    b2 = [b_step(0, u, b1[u]) for u in range(2)]

    def out_view(ref):
        return lambda plane, a: ref.at[pl.ds(peer_seq(plane, a, 0), 2)]

    def give(rows, ref, base):
        for a in range(4):
            copy = pltpu.make_async_copy(rows.at[pl.ds(a * 2, 2)], out_view(ref)(t, a), osem.at[base + a])
            copy.start()
            placed.append(copy)
        return gather_first(out_view(ref), lambda a: None, lambda a: rows.at[pl.ds(a * 2, 2)])

    placed = []
    down_rows = reduce_third(1, d_second)
    bo[...] = (mr[...].astype(F32).reshape(64, D) + down_rows).reshape(8, 8, D).astype(BF16)
    o_first = give(bo, out_b, 0)
    a2 = a_second(a1)
    b3 = [b_step(1, u, b2[u]) for u in range(2)]

    scaled = reduce_third(2, e_second) * g2
    x_hat2 = xhat[...]
    plain = jnp.mean(scaled, -1, keepdims=True)
    cross = jnp.mean(scaled * x_hat2, -1, keepdims=True)
    upstream = gs[t].astype(F32).reshape(64, D)
    go[...] = (upstream + inv2[...] * (scaled - plain - x_hat2 * cross)).reshape(8, 8, D).astype(BF16)
    m_first = give(go, out_g, 4)

    b4 = [b_step(2, u, b3[u]) for u in range(2)]
    a_last(a2)
    az1 = az_first()
    b_last(0, b4[0])
    b_last(1, b4[1])
    by1 = by_first()
    o_further = gather_second(out_view(out_b), o_first)
    az2 = az_step(0, az1)
    by2 = by_second(by1)
    m_further = gather_second(out_view(out_g), m_first)
    az3 = az_step(1, az2)
    fin_b = by_last(by2)
    az4 = az_step(2, az3)
    fin_a = az_last(az4)
    for c in range(2):
        fin[c, :, 0:CA] = fin_a[c * 18 : c * 18 + 18]
        fin[c, :, CA:] = fin_b[c * 18 : c * 18 + 18]
    sf = fresh()

    def hand_over(src, dst):
        return pltpu.make_async_remote_copy(
            src_ref=src, dst_ref=dst, send_sem=ssem.at[sf], recv_sem=rsem.at[sf], device_id=core_dev, device_id_type=MESH
        )

    @pl.when(core == 0)
    def _():
        hand_over(fin.at[1], out_1).start()
        own = pltpu.make_async_copy(fin.at[0], out_1, asem)
        own.start()
        own.wait()
        hand_over(fin.at[1], out_2).wait()

    @pl.when(core == 1)
    def _():
        hand_over(fin.at[0], out_2).start()
        own = pltpu.make_async_copy(fin.at[1], out_2, asem)
        own.start()
        own.wait()
        hand_over(fin.at[0], out_1).wait()

    gather_third(o_further)
    gather_third(m_further)
    for copy in placed:
        copy.wait()

    exchange_sent(lambda j, peer: hid.at[peer], base_h)
    exchange_sent(lambda j, peer: ms.at[j], base_m)
    for copy in started:
        copy.wait_send()


def place(*refs):
    sources, results, sems = refs[:4], refs[4:8], refs[8]
    copies = []
    for src, dst, parts in zip(sources, results, (4, 4, 1, 1)):
        step = src.shape[0] // parts
        for i in range(parts):
            rows = pl.ds(i * step, step)
            copies.append(pltpu.make_async_copy(src.at[rows], dst.at[rows], sems.at[len(copies)]))
    for copy in copies:
        copy.start()
    for copy in copies:
        copy.wait()


def local(hidden_in, norm1_gain, qkv_weight, out_weight, norm2_gain, fc1_weight, fc2_weight, out_grad):
    anywhere = pl.BlockSpec(memory_space=pl.ANY)
    vmem = pl.BlockSpec(memory_space=pltpu.VMEM)
    shapes = [
        ((4, 8, 8, D), BF16), ((4, 8, 8, D), BF16),
        ((3 * QC, D), BF16), ((QC, D), BF16), ((D, FQ), BF16), ((D, FQ), BF16),
        ((4, 64, D), BF16), ((256, QC), BF16), ((4, 64, D), BF16), ((256, FQ), F32), ((4, 64, D), BF16),
        ((3, 4, 64, D), F32), ((3, 4, 64, D), BF16),
        ((3, 2, 32, D), BF16), ((3, 2, 32, D), BF16), ((3, 2, 64, D), BF16),
        ((8, 8, D), BF16), ((8, 8, D), BF16), ((64, D), F32), ((64, 1), F32), ((8, 8, D), BF16), ((8, 8, D), BF16),
        ((ROWS, D), BF16), ((3, ROWS, 256), BF16), ((3, 256, FQ), BF16),
        ((4, 8, SLAB, CA), BF16), ((2, 4, SLAB, CA), BF16), ((2, 4, SLAB, CA), BF16), ((2, 8, SLAB, CA), BF16),
        ((8, SLAB, CA), BF16), ((2, SLAB, CA), BF16), ((3, 2, SLAB, CA), BF16), ((3, 2, SLAB, CA), BF16),
        ((8, 4, SLAB, CB), BF16), ((2, 2, SLAB, CB), BF16), ((3, 2, 2, 2, SLAB, CB), BF16), ((3, 2, 2, 2, SLAB, CB), BF16),
        ((4, SLAB, CB), BF16), ((2, SLAB, 256), BF16), ((2, SLAB, 256), BF16), ((2, SLAB, CB), BF16),
        ((2, 18, FQ), F32),
    ]
    scratch = [pltpu.VMEM(shape, kind) for shape, kind in shapes]
    scratch += [
        pltpu.SemaphoreType.DMA((N_SEM,)), pltpu.SemaphoreType.DMA((N_SEM,)),
        pltpu.SemaphoreType.DMA((4,)), pltpu.SemaphoreType.DMA((16,)), pltpu.SemaphoreType.DMA((8,)),
        pltpu.SemaphoreType.DMA,
    ]
    results = [
        jax.ShapeDtypeStruct((32, 8, D), BF16),
        jax.ShapeDtypeStruct((32, 8, D), BF16),
        jax.ShapeDtypeStruct((18, FQ), F32),
        jax.ShapeDtypeStruct((18, FQ), F32),
    ]
    made = pl.pallas_call(
        kernel,
        out_shape=results,
        in_specs=[anywhere, vmem, anywhere, anywhere, vmem, anywhere, anywhere, anywhere],
        out_specs=[anywhere] * 4,
        scratch_shapes=scratch,
        compiler_params=pltpu.CompilerParams(
            collective_id=0, has_side_effects=True, vmem_limit_bytes=60 * 1024 * 1024
        ),
    )(
        hidden_in.reshape(32, 8, D),
        norm1_gain,
        qkv_weight.transpose(1, 2, 0).reshape(3 * QC, D),
        out_weight,
        norm2_gain,
        fc1_weight,
        fc2_weight,
        out_grad.reshape(32, 8, D),
    )
    block, grad_mid, grad_fc1, grad_fc2 = pl.pallas_call(
        place,
        out_shape=results,
        in_specs=[anywhere] * 4,
        out_specs=[anywhere] * 4,
        scratch_shapes=[pltpu.SemaphoreType.DMA((10,))],
        compiler_params=pltpu.CompilerParams(vmem_limit_bytes=60 * 1024 * 1024),
    )(*made)
    shape = hidden_in.shape
    return block.reshape(shape), grad_mid.reshape(shape), grad_fc1, grad_fc2


def solution(mesh):
    return jax.shard_map(
        local,
        mesh=mesh,
        in_specs=(
            P("dp", "seq", None, None),
            P(),
            P(None, None, "tensor"),
            P("tensor", None),
            P(),
            P(None, "tensor"),
            P(None, "tensor"),
            P("dp", "seq", None, None),
        ),
        out_specs=(
            P("dp", "seq", None, None),
            P("dp", "seq", None, None),
            P(("seq", "dp"), "tensor"),
            P(("seq", "dp"), "tensor"),
        ),
        check_vma=False,
    )
```

```python
import functools

import jax
import jax.numpy as jnp
import numpy as np
from jax import lax
from jax.experimental import pallas as pl
from jax.experimental.pallas import tpu as pltpu
from jax.sharding import PartitionSpec as P

MESH = pl.DeviceIdType.MESH
BF16 = jnp.bfloat16
F32 = jnp.float32

HDIM = 72
D = 1152
FQ = 1152
QC = 288
SLAB = 40
ROWS = 32 * SLAB
CA = 512
CB = 640
EPS = 1e-06
N_SEM = 200


def slab_sources(first, count):
    n = lax.broadcasted_iota(jnp.int32, (count, 1), 0) + first
    slab = (n * 1639) >> 16
    within = n - slab * SLAB
    core = jnp.where(within >= 18, 1, 0)
    z, y = slab >> 2, slab & 3
    source = (((z >> 1) * 4 + y) * 2 + core) * 36 + (z & 1) * 18 + within - core * 18
    return jnp.where(within < 36, source, -1)


def nn(a, b):
    return jnp.dot(a, b, preferred_element_type=F32)


def nt(a, b):
    return lax.dot_general(a, b, (((1,), (1,)), ((), ())), preferred_element_type=F32)


def normalize(values):
    center = values - jnp.mean(values, -1, keepdims=True)
    inv_std = lax.rsqrt(jnp.mean(center * center, -1, keepdims=True) + EPS)
    return center * inv_std, inv_std


def kernel(
    hid, gain1, wq_h, wo_h, gain2, w1_h, w2_h, og,
    out_b, out_g, out_1, out_2,
    hs, gs, hres, wq, wo, w1, w2, na, att, arec, gflat, ga, nb,
    pf, pb, xr1, xs2, xq, mid, xhat, inv2, bo, go,
    perm, lbuf, rbuf,
    wa, ya1, yas, yaq, ra, raq,
    wb, zb1, zbs, zbq, rb, rbq, fin,
    ssem, rsem, lsem, gsem, osem, asem,
):
    t = lax.axis_index("tensor")
    s = lax.axis_index("seq")
    dp = lax.axis_index("dp")
    zh = s // 8
    y = (s // 2) % 4
    core = s % 2
    zz = zh * 2 + dp

    def wrap(value, size):
        return (value + 2 * size) % size

    def x_dev(step):
        return {"tensor": wrap(t + step, 4)}

    def y_dev(step):
        return {"seq": zh * 8 + wrap(y + step, 4) * 2 + core}

    def z_dev(step):
        other = wrap(zz + step, 8)
        return {"seq": (other // 2) * 8 + y * 2 + core, "dp": other % 2}

    core_dev = {"seq": s + 1 - 2 * core}

    def peer_seq(plane, a, k):
        return a * 8 + wrap(plane - zh - y - a, 4) * 2 + k

    barrier = pltpu.get_barrier_semaphore()
    for dev in (x_dev(1), x_dev(-1), core_dev):
        pl.semaphore_signal(barrier, inc=1, device_id=dev, device_id_type=MESH)
    for step in range(1, 4):
        pl.semaphore_signal(barrier, inc=1, device_id=y_dev(step), device_id_type=MESH)
    for step in range(1, 8):
        pl.semaphore_signal(barrier, inc=1, device_id=z_dev(step), device_id_type=MESH)
    for plane in range(4):
        for a in range(4):
            for k in range(2):
                dev = {"seq": peer_seq(t, a, k), "tensor": plane}
                pl.semaphore_signal(barrier, inc=1, device_id=dev, device_id_type=MESH)

    loads = [
        pltpu.make_async_copy(src, dst, lsem.at[i])
        for i, (src, dst) in enumerate(((wo_h, wo.at[t]), (wq_h, wq), (w2_h, w2), (w1_h, w1)))
    ]
    for load in loads:
        load.start()
    pl.semaphore_wait(barrier, 45)

    count = [0]
    started = []

    def fresh(n=1):
        first = count[0]
        count[0] += n
        return first

    def send(src, dst, dev):
        i = fresh()
        copy = pltpu.make_async_remote_copy(
            src_ref=src, dst_ref=dst, send_sem=ssem.at[i], recv_sem=rsem.at[i], device_id=dev, device_id_type=MESH
        )
        copy.start()
        started.append(copy)
        return copy

    def exchange(src_of, dst, base):
        for a in range(4):
            for k in range(2):
                j = a * 2 + k
                peer = peer_seq(t, a, k)
                src = src_of(j, peer)

                @pl.when(peer != s)
                def _():
                    pltpu.make_async_remote_copy(
                        src_ref=src, dst_ref=dst, send_sem=ssem.at[base + j], recv_sem=rsem.at[base + zh * 2 + core],
                        device_id={"seq": peer}, device_id_type=MESH,
                    ).start()

                @pl.when(peer == s)
                def _():
                    pltpu.make_async_copy(src, dst, rsem.at[base + j]).start()

    def exchange_arrived(dst, base, j):
        pltpu.make_async_copy(dst, dst, rsem.at[base + j]).wait()

    def exchange_sent(src_of, base):
        for a in range(4):
            for k in range(2):
                j = a * 2 + k
                peer = peer_seq(t, a, k)
                src = src_of(j, peer)

                @pl.when(peer != s)
                def _():
                    pltpu.make_async_copy(src, src, ssem.at[base + j]).wait()

    base_h, base_m = fresh(8), fresh(32)
    here = hs.at[t, zh * 2 + core]
    exchange(lambda j, peer: hid.at[peer], here, base_h)

    turned = [
        pltpu.make_async_copy(
            og.at[pl.ds(peer_seq(plane, a, 0), 2)], gs.at[plane, pl.ds(a * 2, 2)], gsem.at[plane * 4 + a]
        )
        for plane in range(4)
        for a in range(4)
    ] + [
        pltpu.make_async_copy(hid.at[pl.ds(peer_seq(t, a, 0), 2)], hres.at[pl.ds(a * 2, 2)], gsem.at[16 + a])
        for a in range(4)
    ]
    for copy in turned:
        copy.start()

    def gather_first(view, arrived, own=None):
        copies = []
        for a in range(4):
            arrived(a)
            src = view(t, a) if own is None else own(a)
            copies.append((send(src, view(t, a), x_dev(1)), send(src, view(t, a), x_dev(-1))))
        return copies

    def gather_second(view, copies):
        left, right = wrap(t - 1, 4), wrap(t + 1, 4)
        further = []
        for a in range(2):
            copies[a][0].wait_recv()
            further.append(send(view(left, a), view(left, a), x_dev(1)))
            copies[a + 2][1].wait_recv()
            further.append(send(view(right, a + 2), view(right, a + 2), x_dev(-1)))
        for a in range(2):
            copies[a + 2][0].wait_recv()
            copies[a][1].wait_recv()
        return further

    def gather_third(further):
        for copy in further:
            copy.wait_recv()

    def pair(ref):
        return lambda plane, a: ref.at[plane, pl.ds(a * 2, 2)]

    def slabs_arrived(dst, base):
        def arrived(a):
            for k in range(2):
                exchange_arrived(dst, base, a * 2 + k)

        return arrived

    def wo_part(plane, first, size):
        return wo.at[plane, pl.ds(pl.multiple_of(core * 144 + first, 16), size)]

    def wo_send(first, size):
        src = wo_part(t, first, size)
        return send(src, src, x_dev(1)), send(src, src, x_dev(-1))

    loads[0].wait()
    wo_first = [wo_send(0, 48)]

    def make_perm(i, carry):
        first = pl.multiple_of(i * 128, 128)
        wanted = slab_sources(first, 128)
        perm[pl.ds(first, 128), :] = jnp.where(
            lax.broadcasted_iota(jnp.int32, (128, D), 1) == wanted, 1.0, 0.0
        ).astype(BF16)
        return carry

    lax.fori_loop(0, ROWS // 128, make_perm, 0)

    g1 = gain1[...].reshape(1, D)

    def norm_share(plane):
        x_hat, _ = normalize(hs[plane].astype(F32).reshape(64, D))
        na[plane] = (x_hat * g1).astype(BF16)

    h_first = gather_first(pair(hs), slabs_arrived(here, base_h))
    norm_share(t)
    h_further = gather_second(pair(hs), h_first)
    wo_first.append(wo_send(48, 96))
    norm_share(wrap(t - 1, 4))
    norm_share(wrap(t + 1, 4))
    gather_third(h_further)
    norm_share(wrap(t + 2, 4))

    loads[1].wait()
    na_all = na[...].reshape(256, D)
    q = nt(na_all, wq[0:QC, :]).astype(BF16)
    k_ = nt(na_all, wq[QC : 2 * QC, :]).astype(BF16)
    v = nt(na_all, wq[2 * QC : 3 * QC, :]).astype(BF16)
    for right, left in wo_first:
        right.wait_recv()
        left.wait_recv()
    left, right, far = wrap(t - 1, 4), wrap(t + 1, 4), wrap(t + 2, 4)
    wo_further = [
        send(wo_part(left, 0, 80), wo_part(left, 0, 80), x_dev(1)),
        send(wo_part(right, 80, 64), wo_part(right, 80, 64), x_dev(-1)),
    ]
    wo_swapped = [send(wo_part(plane, 0, 144), wo_part(plane, 0, 144), core_dev) for plane in (left, right)]
    col = lax.broadcasted_iota(jnp.int32, (1, QC), 1)
    same = (lax.broadcasted_iota(jnp.int32, (256, 256), 0) & 7) == (lax.broadcasted_iota(jnp.int32, (256, 256), 1) & 7)
    total = jnp.zeros((256, QC), F32)
    for h in range(QC // HDIM):
        mine = (col >= h * HDIM) & (col < (h + 1) * HDIM)
        qh = jnp.where(mine, q, jnp.zeros_like(q))
        scores = nt(qh, k_) * HDIM ** (-0.5)
        scores = jnp.where(same, scores, -1e30)
        weights = jnp.exp(scores - jnp.max(scores, -1, keepdims=True))
        probs = (weights * (1.0 / jnp.sum(weights, -1, keepdims=True))).astype(BF16)
        total = jnp.where(mine, nn(probs, v), total)
    att[...] = total.reshape(4, 8, 8, QC).astype(BF16)

    def to_frame(step, j, peer):
        plane = wrap(t + step, 4)
        return pltpu.make_async_remote_copy(
            src_ref=att.at[plane, j], dst_ref=arec.at[t, zh * 2 + core],
            send_sem=ssem.at[base_m + step * 8 + j], recv_sem=rsem.at[base_m + t * 8 + zh * 2 + core],
            device_id={"seq": peer, "tensor": plane}, device_id_type=MESH,
        )

    for step in (2, 1, 3, 0):
        for a in range(4):
            for k in range(2):
                j = a * 2 + k
                peer = peer_seq(wrap(t + step, 4), a, k)
                if step:
                    to_frame(step, j, peer).start()
                    continue

                @pl.when(peer != s)
                def _():
                    to_frame(step, j, peer).start()

                @pl.when(peer == s)
                def _():
                    pltpu.make_async_copy(att.at[t, j], arec.at[t, j], rsem.at[base_m + t * 8 + j]).start()

    for copy in wo_further:
        copy.wait_recv()
    wo_swapped.append(send(wo_part(far, 0, 144), wo_part(far, 0, 144), core_dev))

    def partial_sums(u, product):
        for n in range(3):
            value = product(n)
            pf[u, :, :, n * 384 : n * 384 + 384] = value.reshape(4, 64, 384)
            pb[u, :, :, n * 384 : n * 384 + 384] = value.astype(BF16).reshape(4, 64, 384)

    def reduce_first(u):
        far, right, left = wrap(t + 2, 4), wrap(t + 1, 4), wrap(t - 1, 4)
        lo, hi = pl.ds(0, 32), pl.ds(32, 32)
        r1 = send(pb.at[u, far, lo], xr1.at[u, 0], x_dev(1))
        l1 = send(pb.at[u, far, hi], xr1.at[u, 1], x_dev(-1))
        r2 = send(pb.at[u, right, hi], xq.at[u, 0, hi], x_dev(1))
        l2 = send(pb.at[u, left, lo], xq.at[u, 1, lo], x_dev(-1))
        return r1, l1, r2, l2

    def reduce_second(u, copies):
        right, left = wrap(t + 1, 4), wrap(t - 1, 4)
        lo, hi = pl.ds(0, 32), pl.ds(32, 32)
        r1, l1, r2, l2 = copies
        r1.wait_recv()
        xs2[u, 0] = (pf[u, right, 0:32, :] + xr1[u, 0].astype(F32)).astype(BF16)
        r3 = send(xs2.at[u, 0], xq.at[u, 0, lo], x_dev(1))
        l1.wait_recv()
        xs2[u, 1] = (pf[u, left, 32:64, :] + xr1[u, 1].astype(F32)).astype(BF16)
        l3 = send(xs2.at[u, 1], xq.at[u, 1, hi], x_dev(-1))
        return r2, l2, r3, l3

    def reduce_third(u, copies):
        for copy in copies:
            copy.wait_recv()
        return pf[u, t] + xq[u, 0].astype(F32) + xq[u, 1].astype(F32)

    for copy in turned:
        copy.wait()
    for plane in range(4):
        gflat[plane] = gs[plane].astype(F32).reshape(64, D).astype(BF16)
    loads[2].wait()
    loads[3].wait()
    g_all = gflat[...].reshape(256, D)
    for n in range(3):
        c = slice(n * 384, n * 384 + 384)
        ga[:, c] = nn(g_all, w2[:, c])
    for copy in wo_swapped:
        copy.wait_recv()
    for plane in range(4):
        for j in range(8):
            slab = arec.at[plane, j]
            pltpu.make_async_copy(slab, slab, rsem.at[base_m + plane * 8 + j]).wait()

    proj = sum(nn(arec[plane].astype(F32).reshape(64, QC).astype(BF16), wo[plane]) for plane in range(4))
    mid_rows = (hres[...].astype(F32).reshape(64, D) + proj).astype(BF16)
    mid[...] = mid_rows
    x_hat2, inv_std2 = normalize(mid_rows.astype(F32))
    xhat[...] = x_hat2
    inv2[...] = inv_std2
    g2 = gain2[...].reshape(1, D)
    nb[t] = (x_hat2 * g2).astype(BF16)

    def quarter(ref):
        return lambda plane, a: ref.at[plane, pl.ds(a * 16, 16)]

    n_first = gather_first(quarter(nb), lambda a: None)

    for n in range(2):
        c = slice(n * 640, n * 640 + 640)
        lbuf[0, c, :] = nt(perm[c, :], g_all).astype(BF16)
    n_further = gather_second(quarter(nb), n_first)
    gather_third(n_further)
    nb_all = nb[...].reshape(256, D)
    for n in range(2):
        c = slice(n * 640, n * 640 + 640)
        lbuf[1, c, :] = nt(perm[c, :], nb_all).astype(BF16)

    swapped = [send(lbuf.at[core], lbuf.at[2], core_dev)]
    kept = 1 - core

    root = (2.0 / np.pi) ** 0.5
    for n in range(3):
        c = slice(n * 384, n * 384 + 384)
        pre = nn(nb_all, w1[:, c])
        square = pre * pre
        th = jnp.tanh(root * (pre + 0.044715 * (square * pre)))
        half = 0.5 * (1.0 + th)
        rbuf[0, :, c] = (pre * half).astype(BF16)
        slope = half + 0.5 * pre * (1.0 - th * th) * (root * (1.0 + 3 * 0.044715 * square))
        rbuf[1, :, c] = (ga[:, c] * slope).astype(BF16)
        part = pl.ds(n * 384, 384)
        swapped.append(send(rbuf.at[core, :, part], rbuf.at[2, :, part], core_dev))

    partial_sums(0, lambda n: nt(rbuf[0], w2[n * 384 : n * 384 + 384, :]))
    d_first = reduce_first(0)
    for copy in swapped:
        copy.wait_recv()

    def grad_b(i, carry):
        rows = pl.ds(pl.multiple_of(i * 320, 320), 320)
        value = nn(lbuf[kept, rows, :], rbuf[kept, :, CA:]) + nn(lbuf[2, rows, :], rbuf[2, :, CA:])
        for m in range(8):
            wb[i * 2 + m // 4, m % 4] = value[m * SLAB : (m + 1) * SLAB].astype(BF16)
        return carry

    def grad_a(i, carry):
        rows = pl.ds(pl.multiple_of(i * 320, 320), 320)
        value = nn(lbuf[kept, rows, :], rbuf[kept, :, :CA]) + nn(lbuf[2, rows, :], rbuf[2, :, :CA])
        for m in range(8):
            wa[m % 4, i * 2 + m // 4] = value[m * SLAB : (m + 1) * SLAB].astype(BF16)
        return carry

    def add(a, b):
        return (a.astype(F32) + b.astype(F32)).astype(BF16)

    HALF = 384
    halves = (pl.ds(0, HALF), pl.ds(HALF, CB - HALF))

    def b_first(u):
        far = wrap(zz + 4, 8)
        return [
            send(wb.at[far, u, :, halves[d]], zb1.at[u, d, :, halves[d]], z_dev(1 - 2 * d)) for d in range(2)
        ]

    def b_step(n, u, copies):
        result = []
        for d in range(2):
            sign = 1 - 2 * d
            chunk = wrap(zz + sign * (3 - n), 8)
            copies[d].wait_recv()
            if n == 0:
                taken, other = (slice(0, HALF), slice(HALF, CB))[:: 1 - 2 * d]
                zbs[n, u, d, :, taken] = add(wb[chunk, u, :, taken], zb1[u, d, :, taken])
                zbs[n, u, d, :, other] = wb[chunk, u, :, other]
            else:
                zbs[n, u, d] = add(wb[chunk, u], zbq[n - 1, u, d])
            result.append(send(zbs.at[n, u, d], zbq.at[n, u, d], z_dev(sign)))
        return result

    def b_last(u, copies):
        for copy in copies:
            copy.wait_recv()
        rb[u] = (wb[zz, u].astype(F32) + zbq[2, u, 0].astype(F32) + zbq[2, u, 1].astype(F32)).astype(BF16)

    def a_first():
        far, up, down = wrap(y + 2, 4), wrap(y + 1, 4), wrap(y - 1, 4)
        lo, hi = pl.ds(0, 4), pl.ds(4, 4)
        u1 = send(wa.at[far, lo], ya1.at[0], y_dev(1))
        d1 = send(wa.at[far, hi], ya1.at[1], y_dev(-1))
        u2 = send(wa.at[up, hi], yaq.at[0, hi], y_dev(1))
        d2 = send(wa.at[down, lo], yaq.at[1, lo], y_dev(-1))
        return u1, d1, u2, d2

    def a_second(copies):
        up, down = wrap(y + 1, 4), wrap(y - 1, 4)
        u1, d1, u2, d2 = copies
        u1.wait_recv()

        def body_up(i, carry):
            yas[0, i] = add(wa[up, i], ya1[0, i])
            return carry

        lax.fori_loop(0, 4, body_up, 0)
        u3 = send(yas.at[0], yaq.at[0, pl.ds(0, 4)], y_dev(1))
        d1.wait_recv()

        def body_down(i, carry):
            yas[1, i] = add(wa[down, i + 4], ya1[1, i])
            return carry

        lax.fori_loop(0, 4, body_down, 0)
        d3 = send(yas.at[1], yaq.at[1, pl.ds(4, 4)], y_dev(-1))
        return u2, d2, u3, d3

    def a_last(copies):
        for copy in copies:
            copy.wait_recv()

        def body(i, carry):
            ra[i] = (wa[y, i].astype(F32) + yaq[0, i].astype(F32) + yaq[1, i].astype(F32)).astype(BF16)
            return carry

        lax.fori_loop(0, 8, body, 0)

    def straight(rows, place, dev_of, n):
        return [send(rows.at[place(step)], dev_of[1].at[step - 1], dev_of[0](step)) for step in range(1, n)]

    def straight_sum(rows, here, received, copies):
        total = rows[here].astype(F32)
        for i, copy in enumerate(copies):
            copy.wait_recv()
            total = total + received[i].astype(F32)
        return total

    lax.fori_loop(0, 4, grad_b, 0)
    b1 = [b_first(u) for u in range(4)]
    lax.fori_loop(0, 4, grad_a, 0)
    a1 = a_first()
    partial_sums(1, lambda n: nt(rbuf[1], w1[n * 384 : n * 384 + 384, :]))
    e_first = reduce_first(1)
    d_second = reduce_second(0, d_first)
    b2 = [b_step(0, u, b1[u]) for u in range(4)]
    e_second = reduce_second(1, e_first)
    b3 = [b_step(1, u, b2[u]) for u in range(4)]
    a2 = a_second(a1)

    def out_view(ref):
        return lambda plane, a: ref.at[pl.ds(peer_seq(plane, a, 0), 2)]

    def give(rows, ref, base):
        for a in range(4):
            copy = pltpu.make_async_copy(rows.at[pl.ds(a * 2, 2)], out_view(ref)(t, a), osem.at[base + a])
            copy.start()
            placed.append(copy)
        return gather_first(out_view(ref), lambda a: None, lambda a: rows.at[pl.ds(a * 2, 2)])

    placed = []
    down_rows = reduce_third(0, d_second)
    bo[...] = (mid[...].astype(F32) + down_rows).reshape(8, 8, D).astype(BF16)
    o_first = give(bo, out_b, 0)
    b4 = [b_step(2, u, b3[u]) for u in range(4)]

    scaled = reduce_third(1, e_second) * g2
    x_hat2 = xhat[...]
    plain = jnp.mean(scaled, -1, keepdims=True)
    cross = jnp.mean(scaled * x_hat2, -1, keepdims=True)
    upstream = gs[t].astype(F32).reshape(64, D)
    go[...] = (upstream + inv2[...] * (scaled - plain - x_hat2 * cross)).reshape(8, 8, D).astype(BF16)
    m_first = give(go, out_g, 4)

    a_last(a2)
    a3 = straight(ra, lambda step: wrap(zz + step, 8), (z_dev, raq), 8)
    o_further = gather_second(out_view(out_b), o_first)
    for u in range(4):
        b_last(u, b4[u])
    b5 = straight(rb, lambda step: wrap(y + step, 4), (y_dev, rbq), 4)
    m_further = gather_second(out_view(out_g), m_first)
    fin_b = straight_sum(rb, y, rbq, b5)
    fin_a = straight_sum(ra, zz, raq, a3)
    for c in range(2):
        fin[c, :, 0:CA] = fin_a[c * 18 : c * 18 + 18]
        fin[c, :, CA:] = fin_b[c * 18 : c * 18 + 18]
    sf = fresh()

    def hand_over(src, dst):
        return pltpu.make_async_remote_copy(
            src_ref=src, dst_ref=dst, send_sem=ssem.at[sf], recv_sem=rsem.at[sf], device_id=core_dev, device_id_type=MESH
        )

    @pl.when(core == 0)
    def _():
        hand_over(fin.at[1], out_1).start()
        own = pltpu.make_async_copy(fin.at[0], out_1, asem)
        own.start()
        own.wait()
        hand_over(fin.at[1], out_2).wait()

    @pl.when(core == 1)
    def _():
        hand_over(fin.at[0], out_2).start()
        own = pltpu.make_async_copy(fin.at[1], out_2, asem)
        own.start()
        own.wait()
        hand_over(fin.at[0], out_1).wait()

    gather_third(o_further)
    gather_third(m_further)
    for copy in placed:
        copy.wait()

    exchange_sent(lambda j, peer: hid.at[peer], base_h)
    for step in range(4):
        for a in range(4):
            for k in range(2):
                j = a * 2 + k
                gone = pltpu.make_async_copy(att.at[0, j], att.at[0, j], ssem.at[base_m + step * 8 + j])
                if step:
                    gone.wait()
                    continue

                @pl.when(peer_seq(t, a, k) != s)
                def _():
                    gone.wait()

    for copy in started:
        copy.wait_send()


def place(*refs):
    sources, results, (buf_b, buf_g, buf_1, buf_2, sems) = refs[:4], refs[4:8], refs[8:]
    copies = []
    for src, dst, buf, parts in zip(sources, results, (buf_b, buf_g, buf_1, buf_2), (4, 4, 1, 1)):
        step = src.shape[0] // parts
        for i in range(parts):
            rows = pl.ds(i * step, step)
            n = len(copies)
            copies.append(
                (
                    pltpu.make_async_copy(src.at[rows], buf.at[rows], sems.at[0, n]),
                    pltpu.make_async_copy(buf.at[rows], dst.at[rows], sems.at[1, n]),
                )
            )
    for read, _ in copies:
        read.start()
    for read, write in copies:
        read.wait()
        write.start()
    for _, write in copies:
        write.wait()


def local(hidden_in, norm1_gain, qkv_weight, out_weight, norm2_gain, fc1_weight, fc2_weight, out_grad):
    anywhere = pl.BlockSpec(memory_space=pl.ANY)
    vmem = pl.BlockSpec(memory_space=pltpu.VMEM)
    shapes = [
        ((4, 8, 8, D), BF16), ((4, 8, 8, D), BF16), ((8, 8, D), BF16),
        ((3 * QC, D), BF16), ((4, QC, D), BF16), ((D, FQ), BF16), ((D, FQ), BF16),
        ((4, 64, D), BF16), ((4, 8, 8, QC), BF16), ((4, 8, 8, QC), BF16),
        ((4, 64, D), BF16), ((256, FQ), F32), ((4, 64, D), BF16),
        ((2, 4, 64, D), F32), ((2, 4, 64, D), BF16),
        ((2, 2, 32, D), BF16), ((2, 2, 32, D), BF16), ((2, 2, 64, D), BF16),
        ((64, D), BF16), ((64, D), F32), ((64, 1), F32), ((8, 8, D), BF16), ((8, 8, D), BF16),
        ((ROWS, D), BF16), ((3, ROWS, 256), BF16), ((3, 256, FQ), BF16),
        ((4, 8, SLAB, CA), BF16), ((2, 4, SLAB, CA), BF16), ((2, 4, SLAB, CA), BF16), ((2, 8, SLAB, CA), BF16),
        ((8, SLAB, CA), BF16), ((7, SLAB, CA), BF16),
        ((8, 4, SLAB, CB), BF16), ((4, 2, SLAB, CB), BF16), ((3, 4, 2, SLAB, CB), BF16), ((3, 4, 2, SLAB, CB), BF16),
        ((4, SLAB, CB), BF16), ((3, SLAB, CB), BF16),
        ((2, 18, FQ), F32),
    ]
    scratch = [pltpu.VMEM(shape, kind) for shape, kind in shapes]
    scratch += [
        pltpu.SemaphoreType.DMA((N_SEM,)), pltpu.SemaphoreType.DMA((N_SEM,)),
        pltpu.SemaphoreType.DMA((4,)), pltpu.SemaphoreType.DMA((20,)), pltpu.SemaphoreType.DMA((8,)),
        pltpu.SemaphoreType.DMA,
    ]
    results = [
        jax.ShapeDtypeStruct((32, 8, D), BF16),
        jax.ShapeDtypeStruct((32, 8, D), BF16),
        jax.ShapeDtypeStruct((18, FQ), F32),
        jax.ShapeDtypeStruct((18, FQ), F32),
    ]
    made = pl.pallas_call(
        kernel,
        out_shape=results,
        in_specs=[anywhere, vmem, anywhere, anywhere, vmem, anywhere, anywhere, anywhere],
        out_specs=[anywhere] * 4,
        scratch_shapes=scratch,
        compiler_params=pltpu.CompilerParams(
            collective_id=0, has_side_effects=True, vmem_limit_bytes=60 * 1024 * 1024
        ),
    )(
        hidden_in.reshape(32, 8, D),
        norm1_gain,
        qkv_weight.transpose(1, 2, 0).reshape(3 * QC, D),
        out_weight,
        norm2_gain,
        fc1_weight,
        fc2_weight,
        out_grad.reshape(32, 8, D),
    )
    block, grad_mid, grad_fc1, grad_fc2 = pl.pallas_call(
        place,
        out_shape=results,
        in_specs=[anywhere] * 4,
        out_specs=[anywhere] * 4,
        scratch_shapes=[pltpu.VMEM(made_one.shape, made_one.dtype) for made_one in results]
        + [pltpu.SemaphoreType.DMA((2, 10))],
        compiler_params=pltpu.CompilerParams(vmem_limit_bytes=60 * 1024 * 1024),
    )(*made)
    shape = hidden_in.shape
    return block.reshape(shape), grad_mid.reshape(shape), grad_fc1, grad_fc2


def solution(mesh):
    return jax.shard_map(
        local,
        mesh=mesh,
        in_specs=(
            P("dp", "seq", None, None),
            P(),
            P(None, None, "tensor"),
            P("tensor", None),
            P(),
            P(None, "tensor"),
            P(None, "tensor"),
            P("dp", "seq", None, None),
        ),
        out_specs=(
            P("dp", "seq", None, None),
            P("dp", "seq", None, None),
            P(("seq", "dp"), "tensor"),
            P(("seq", "dp"), "tensor"),
        ),
        check_vma=False,
    )
```

```python
import functools

import jax
import jax.numpy as jnp
import numpy as np
from jax import lax
from jax.experimental import pallas as pl
from jax.experimental.pallas import tpu as pltpu
from jax.sharding import PartitionSpec as P

MESH = pl.DeviceIdType.MESH
BF16 = jnp.bfloat16
F32 = jnp.float32

HDIM = 72
D = 1152
FQ = 1152
QC = 288
SLAB = 40
ROWS = 32 * SLAB
CA = 512
CB = 640
EPS = 1e-06
N_SEM = 224


def slab_sources(first, count):
    n = lax.broadcasted_iota(jnp.int32, (count, 1), 0) + first
    slab = (n * 1639) >> 16
    within = n - slab * SLAB
    core = jnp.where(within >= 18, 1, 0)
    z, y = slab >> 2, slab & 3
    source = (((z >> 1) * 4 + y) * 2 + core) * 36 + (z & 1) * 18 + within - core * 18
    return jnp.where(within < 36, source, -1)


def nn(a, b):
    return jnp.dot(a, b, preferred_element_type=F32)


def nt(a, b):
    return lax.dot_general(a, b, (((1,), (1,)), ((), ())), preferred_element_type=F32)


def normalize(values):
    center = values - jnp.mean(values, -1, keepdims=True)
    inv_std = lax.rsqrt(jnp.mean(center * center, -1, keepdims=True) + EPS)
    return center * inv_std, inv_std


def kernel(
    hid, gain1, wq_h, wo_h, gain2, w1_h, w2_h, og,
    out_b, out_g, out_1, out_2,
    hl, gs, hres, wq, wo, w1, w2, na, qkv, qrec, att, arec, gflat, ga, nb,
    pf, pb, xr1, xs2, xq, mid, xhat, inv2, bo, go,
    perm, lbuf, rbuf,
    wa, ya1, yas, yaq, ra, raq,
    wb, zb1, zbs, zbq, rb, rbq, fin,
    ssem, rsem, lsem, gsem, osem, asem,
):
    t = lax.axis_index("tensor")
    s = lax.axis_index("seq")
    dp = lax.axis_index("dp")
    zh = s // 8
    y = (s // 2) % 4
    core = s % 2
    zz = zh * 2 + dp

    def wrap(value, size):
        return (value + 2 * size) % size

    def x_dev(step):
        return {"tensor": wrap(t + step, 4)}

    def y_dev(step):
        return {"seq": zh * 8 + wrap(y + step, 4) * 2 + core}

    def z_dev(step):
        other = wrap(zz + step, 8)
        return {"seq": (other // 2) * 8 + y * 2 + core, "dp": other % 2}

    core_dev = {"seq": s + 1 - 2 * core}

    def peer_seq(plane, a, k):
        return a * 8 + wrap(plane - zh - y - a, 4) * 2 + k

    barrier = pltpu.get_barrier_semaphore()
    for dev in (x_dev(1), x_dev(-1), z_dev(1), z_dev(-1), z_dev(3), z_dev(-3)):
        pl.semaphore_signal(barrier, inc=1, device_id=dev, device_id_type=MESH)
    for other in range(32):
        pl.semaphore_signal(barrier, inc=1, device_id={"seq": other}, device_id_type=MESH)
    for step in range(1, 4):
        for a in range(4):
            for k in range(2):
                dev = {"seq": peer_seq(t, a, k), "tensor": wrap(t + step, 4)}
                pl.semaphore_signal(barrier, inc=1, device_id=dev, device_id_type=MESH)

    loads = [
        pltpu.make_async_copy(src, dst, lsem.at[i])
        for i, (src, dst) in enumerate(((hid, hl), (wq_h, wq), (wo_h, wo.at[t]), (w2_h, w2), (w1_h, w1)))
    ]
    for load in loads:
        load.start()

    g1 = gain1[...].reshape(1, D)
    loads[0].wait()

    def norm_rows(i, carry):
        x_hat, _ = normalize(hl[pl.ds(i * 8, 8)].astype(F32).reshape(64, D))
        na[i] = (x_hat * g1).astype(BF16)
        return carry

    lax.fori_loop(0, 4, norm_rows, 0)
    loads[1].wait()
    qkv[...] = nt(na[...].reshape(256, D), wq[...]).reshape(32, 8, 3 * QC).astype(BF16)
    pl.semaphore_wait(barrier, 62)

    count = [0]
    started = []

    def fresh(n=1):
        first = count[0]
        count[0] += n
        return first

    def send(src, dst, dev):
        i = fresh()
        copy = pltpu.make_async_remote_copy(
            src_ref=src, dst_ref=dst, send_sem=ssem.at[i], recv_sem=rsem.at[i], device_id=dev, device_id_type=MESH
        )
        copy.start()
        started.append(copy)
        return copy

    base_h, base_m = fresh(32), fresh(32)

    def to_patches(other):
        return pltpu.make_async_remote_copy(
            src_ref=qkv.at[other], dst_ref=qrec.at[s], send_sem=ssem.at[base_h + other], recv_sem=rsem.at[base_h + s],
            device_id={"seq": other}, device_id_type=MESH,
        )

    for other in range(32):

        @pl.when(s != other)
        def _():
            to_patches(other).start()

        @pl.when(s == other)
        def _():
            pltpu.make_async_copy(qkv.at[other], qrec.at[other], rsem.at[base_h + other]).start()

    turned = [
        pltpu.make_async_copy(
            og.at[pl.ds(peer_seq(plane, a, 0), 2)], gs.at[plane, pl.ds(a * 2, 2)], gsem.at[plane * 4 + a]
        )
        for plane in range(4)
        for a in range(4)
    ] + [
        pltpu.make_async_copy(hid.at[pl.ds(peer_seq(t, a, 0), 2)], hres.at[pl.ds(a * 2, 2)], gsem.at[16 + a])
        for a in range(4)
    ]
    for copy in turned:
        copy.start()

    def gather_first(view, own):
        return [(send(own(a), view(t, a), x_dev(1)), send(own(a), view(t, a), x_dev(-1))) for a in range(4)]

    def gather_second(view, copies):
        left, right = wrap(t - 1, 4), wrap(t + 1, 4)
        further = []
        for a in range(2):
            copies[a][0].wait_recv()
            further.append(send(view(left, a), view(left, a), x_dev(1)))
            copies[a + 2][1].wait_recv()
            further.append(send(view(right, a + 2), view(right, a + 2), x_dev(-1)))
        for a in range(2):
            copies[a + 2][0].wait_recv()
            copies[a][1].wait_recv()
        return further

    def gather_third(further):
        for copy in further:
            copy.wait_recv()

    def wo_part(plane, first, size):
        return wo.at[plane, pl.ds(pl.multiple_of(core * 144 + first, 16), size)]

    def wo_send(first, size):
        src = wo_part(t, first, size)
        return send(src, src, x_dev(1)), send(src, src, x_dev(-1))

    loads[2].wait()
    wo_first = wo_send(0, 144)

    def make_perm(i, carry):
        first = pl.multiple_of(i * 128, 128)
        wanted = slab_sources(first, 128)
        perm[pl.ds(first, 128), :] = jnp.where(
            lax.broadcasted_iota(jnp.int32, (128, D), 1) == wanted, 1.0, 0.0
        ).astype(BF16)
        return carry

    lax.fori_loop(0, ROWS // 128, make_perm, 0)

    wo_first[0].wait_recv()
    wo_first[1].wait_recv()
    left, right, far = wrap(t - 1, 4), wrap(t + 1, 4), wrap(t + 2, 4)
    wo_further = [
        send(wo_part(left, 0, 80), wo_part(left, 0, 80), x_dev(1)),
        send(wo_part(right, 80, 64), wo_part(right, 80, 64), x_dev(-1)),
    ]
    wo_swapped = [send(wo_part(plane, 0, 144), wo_part(plane, 0, 144), core_dev) for plane in (left, right)]

    for other in range(32):
        slab = qrec.at[other]
        pltpu.make_async_copy(slab, slab, rsem.at[base_h + other]).wait()
    q = qrec[:, :, 0:QC].reshape(256, QC)
    k_ = qrec[:, :, QC : 2 * QC].reshape(256, QC)
    v = qrec[:, :, 2 * QC : 3 * QC].reshape(256, QC)
    col = lax.broadcasted_iota(jnp.int32, (1, QC), 1)
    same = (lax.broadcasted_iota(jnp.int32, (256, 256), 0) & 7) == (lax.broadcasted_iota(jnp.int32, (256, 256), 1) & 7)
    total = jnp.zeros((256, QC), F32)
    for h in range(QC // HDIM):
        mine = (col >= h * HDIM) & (col < (h + 1) * HDIM)
        qh = jnp.where(mine, q, jnp.zeros_like(q))
        scores = nt(qh, k_) * HDIM ** (-0.5)
        scores = jnp.where(same, scores, -1e30)
        weights = jnp.exp(scores - jnp.max(scores, -1, keepdims=True))
        probs = (weights * (1.0 / jnp.sum(weights, -1, keepdims=True))).astype(BF16)
        total = jnp.where(mine, nn(probs, v), total)
    att[...] = total.reshape(32, 8, QC).astype(BF16)

    def plane_of(frame):
        return lax.rem(frame // 8 + frame // 2 % 4 + zh + y, 4)

    def to_frame(frame):
        return pltpu.make_async_remote_copy(
            src_ref=att.at[frame], dst_ref=arec.at[t, zh * 2 + core],
            send_sem=ssem.at[base_m + frame], recv_sem=rsem.at[base_m + t * 8 + zh * 2 + core],
            device_id={"seq": frame, "tensor": plane_of(frame)}, device_id_type=MESH,
        )

    for frame in range(32):
        stays = jnp.logical_and(s == frame, plane_of(frame) == t)

        @pl.when(jnp.logical_not(stays))
        def _():
            to_frame(frame).start()

        @pl.when(stays)
        def _():
            here = arec.at[t, zh * 2 + core]
            pltpu.make_async_copy(att.at[frame], here, rsem.at[base_m + t * 8 + zh * 2 + core]).start()

    for copy in wo_further:
        copy.wait_recv()
    wo_swapped.append(send(wo_part(far, 0, 144), wo_part(far, 0, 144), core_dev))

    def partial_sums(u, product):
        for n in range(3):
            value = product(n)
            pf[u, :, :, n * 384 : n * 384 + 384] = value.reshape(4, 64, 384)
            pb[u, :, :, n * 384 : n * 384 + 384] = value.astype(BF16).reshape(4, 64, 384)

    def reduce_first(u):
        far, right, left = wrap(t + 2, 4), wrap(t + 1, 4), wrap(t - 1, 4)
        lo, hi = pl.ds(0, 32), pl.ds(32, 32)
        r1 = send(pb.at[u, far, lo], xr1.at[u, 0], x_dev(1))
        l1 = send(pb.at[u, far, hi], xr1.at[u, 1], x_dev(-1))
        r2 = send(pb.at[u, right, hi], xq.at[u, 0, hi], x_dev(1))
        l2 = send(pb.at[u, left, lo], xq.at[u, 1, lo], x_dev(-1))
        return r1, l1, r2, l2

    def reduce_second(u, copies):
        right, left = wrap(t + 1, 4), wrap(t - 1, 4)
        lo, hi = pl.ds(0, 32), pl.ds(32, 32)
        r1, l1, r2, l2 = copies
        r1.wait_recv()
        xs2[u, 0] = (pf[u, right, 0:32, :] + xr1[u, 0].astype(F32)).astype(BF16)
        r3 = send(xs2.at[u, 0], xq.at[u, 0, lo], x_dev(1))
        l1.wait_recv()
        xs2[u, 1] = (pf[u, left, 32:64, :] + xr1[u, 1].astype(F32)).astype(BF16)
        l3 = send(xs2.at[u, 1], xq.at[u, 1, hi], x_dev(-1))
        return r2, l2, r3, l3

    def reduce_third(u, copies):
        for copy in copies:
            copy.wait_recv()
        return pf[u, t] + xq[u, 0].astype(F32) + xq[u, 1].astype(F32)

    for copy in turned:
        copy.wait()
    for plane in range(4):
        gflat[plane] = gs[plane].astype(F32).reshape(64, D).astype(BF16)
    loads[3].wait()
    loads[4].wait()
    g_all = gflat[...].reshape(256, D)
    for n in range(3):
        c = slice(n * 384, n * 384 + 384)
        ga[:, c] = nn(g_all, w2[:, c])
    for copy in wo_swapped:
        copy.wait_recv()
    for plane in range(4):
        for j in range(8):
            slab = arec.at[plane, j]
            pltpu.make_async_copy(slab, slab, rsem.at[base_m + plane * 8 + j]).wait()

    proj = sum(nn(arec[plane].astype(F32).reshape(64, QC).astype(BF16), wo[plane]) for plane in range(4))
    mid_rows = (hres[...].astype(F32).reshape(64, D) + proj).astype(BF16)
    mid[...] = mid_rows
    x_hat2, inv_std2 = normalize(mid_rows.astype(F32))
    xhat[...] = x_hat2
    inv2[...] = inv_std2
    g2 = gain2[...].reshape(1, D)
    nb[t] = (x_hat2 * g2).astype(BF16)

    def quarter(ref):
        return lambda plane, a: ref.at[plane, pl.ds(a * 16, 16)]

    n_first = gather_first(quarter(nb), lambda a: quarter(nb)(t, a))

    for n in range(2):
        c = slice(n * 640, n * 640 + 640)
        lbuf[0, c, :] = nt(perm[c, :], g_all).astype(BF16)
    n_further = gather_second(quarter(nb), n_first)
    gather_third(n_further)
    nb_all = nb[...].reshape(256, D)
    for n in range(2):
        c = slice(n * 640, n * 640 + 640)
        lbuf[1, c, :] = nt(perm[c, :], nb_all).astype(BF16)

    swapped = [send(lbuf.at[core], lbuf.at[2], core_dev)]
    kept = 1 - core

    root = (2.0 / np.pi) ** 0.5
    for n in range(3):
        c = slice(n * 384, n * 384 + 384)
        pre = nn(nb_all, w1[:, c])
        square = pre * pre
        th = jnp.tanh(root * (pre + 0.044715 * (square * pre)))
        half = 0.5 * (1.0 + th)
        rbuf[0, :, c] = (pre * half).astype(BF16)
        slope = half + 0.5 * pre * (1.0 - th * th) * (root * (1.0 + 3 * 0.044715 * square))
        rbuf[1, :, c] = (ga[:, c] * slope).astype(BF16)
        part = pl.ds(n * 384, 384)
        swapped.append(send(rbuf.at[core, :, part], rbuf.at[2, :, part], core_dev))

    partial_sums(0, lambda n: nt(rbuf[0], w2[n * 384 : n * 384 + 384, :]))
    d_first = reduce_first(0)
    for copy in swapped:
        copy.wait_recv()

    def grad_b(i, carry):
        rows = pl.ds(pl.multiple_of(i * 320, 320), 320)
        value = nn(lbuf[kept, rows, :], rbuf[kept, :, CA:]) + nn(lbuf[2, rows, :], rbuf[2, :, CA:])
        for m in range(8):
            wb[i * 2 + m // 4, m % 4] = value[m * SLAB : (m + 1) * SLAB].astype(BF16)
        return carry

    def grad_a(i, carry):
        rows = pl.ds(pl.multiple_of(i * 320, 320), 320)
        value = nn(lbuf[kept, rows, :], rbuf[kept, :, :CA]) + nn(lbuf[2, rows, :], rbuf[2, :, :CA])
        for m in range(8):
            wa[m % 4, i * 2 + m // 4] = value[m * SLAB : (m + 1) * SLAB].astype(BF16)
        return carry

    def add(a, b):
        return (a.astype(F32) + b.astype(F32)).astype(BF16)

    HALF = 384
    halves = (pl.ds(0, HALF), pl.ds(HALF, CB - HALF))

    def b_first(u):
        far = wrap(zz + 4, 8)
        return [
            send(wb.at[far, u, :, halves[d]], zb1.at[u, d, :, halves[d]], z_dev(1 - 2 * d)) for d in range(2)
        ]

    def b_step(n, u, copies):
        result = []
        for d in range(2):
            sign = 1 - 2 * d
            chunk = wrap(zz + sign * (3 - n), 8)
            copies[d].wait_recv()
            if n == 0:
                taken, other = (slice(0, HALF), slice(HALF, CB))[:: 1 - 2 * d]
                zbs[n, u, d, :, taken] = add(wb[chunk, u, :, taken], zb1[u, d, :, taken])
                zbs[n, u, d, :, other] = wb[chunk, u, :, other]
            else:
                zbs[n, u, d] = add(wb[chunk, u], zbq[n - 1, u, d])
            result.append(send(zbs.at[n, u, d], zbq.at[n, u, d], z_dev(sign)))
        return result

    def b_last(u, copies):
        for copy in copies:
            copy.wait_recv()
        rb[u] = (wb[zz, u].astype(F32) + zbq[2, u, 0].astype(F32) + zbq[2, u, 1].astype(F32)).astype(BF16)

    def a_first():
        far, up, down = wrap(y + 2, 4), wrap(y + 1, 4), wrap(y - 1, 4)
        lo, hi = pl.ds(0, 4), pl.ds(4, 4)
        u1 = send(wa.at[far, lo], ya1.at[0], y_dev(1))
        d1 = send(wa.at[far, hi], ya1.at[1], y_dev(-1))
        u2 = send(wa.at[up, hi], yaq.at[0, hi], y_dev(1))
        d2 = send(wa.at[down, lo], yaq.at[1, lo], y_dev(-1))
        return u1, d1, u2, d2

    def a_second(copies):
        up, down = wrap(y + 1, 4), wrap(y - 1, 4)
        u1, d1, u2, d2 = copies
        u1.wait_recv()

        def body_up(i, carry):
            yas[0, i] = add(wa[up, i], ya1[0, i])
            return carry

        lax.fori_loop(0, 4, body_up, 0)
        u3 = send(yas.at[0], yaq.at[0, pl.ds(0, 4)], y_dev(1))
        d1.wait_recv()

        def body_down(i, carry):
            yas[1, i] = add(wa[down, i + 4], ya1[1, i])
            return carry

        lax.fori_loop(0, 4, body_down, 0)
        d3 = send(yas.at[1], yaq.at[1, pl.ds(4, 4)], y_dev(-1))
        return u2, d2, u3, d3

    def a_last(copies):
        for copy in copies:
            copy.wait_recv()

        def body(i, carry):
            ra[i] = (wa[y, i].astype(F32) + yaq[0, i].astype(F32) + yaq[1, i].astype(F32)).astype(BF16)
            return carry

        lax.fori_loop(0, 8, body, 0)

    def straight(rows, place, dev_of, n):
        return [send(rows.at[place(step)], dev_of[1].at[step - 1], dev_of[0](step)) for step in range(1, n)]

    def straight_sum(rows, here, received, copies):
        total = rows[here].astype(F32)
        for i, copy in enumerate(copies):
            copy.wait_recv()
            total = total + received[i].astype(F32)
        return total

    lax.fori_loop(0, 4, grad_b, 0)
    b1 = [b_first(u) for u in range(4)]
    lax.fori_loop(0, 4, grad_a, 0)
    a1 = a_first()
    partial_sums(1, lambda n: nt(rbuf[1], w1[n * 384 : n * 384 + 384, :]))
    e_first = reduce_first(1)
    d_second = reduce_second(0, d_first)
    b2 = [b_step(0, u, b1[u]) for u in range(4)]
    e_second = reduce_second(1, e_first)
    b3 = [b_step(1, u, b2[u]) for u in range(4)]
    a2 = a_second(a1)

    def out_view(ref):
        return lambda plane, a: ref.at[pl.ds(peer_seq(plane, a, 0), 2)]

    def give(rows, ref, base):
        for a in range(4):
            copy = pltpu.make_async_copy(rows.at[pl.ds(a * 2, 2)], out_view(ref)(t, a), osem.at[base + a])
            copy.start()
            placed.append(copy)
        return gather_first(out_view(ref), lambda a: rows.at[pl.ds(a * 2, 2)])

    placed = []
    down_rows = reduce_third(0, d_second)
    bo[...] = (mid[...].astype(F32) + down_rows).reshape(8, 8, D).astype(BF16)
    o_first = give(bo, out_b, 0)
    b4 = [b_step(2, u, b3[u]) for u in range(4)]

    scaled = reduce_third(1, e_second) * g2
    x_hat2 = xhat[...]
    plain = jnp.mean(scaled, -1, keepdims=True)
    cross = jnp.mean(scaled * x_hat2, -1, keepdims=True)
    upstream = gs[t].astype(F32).reshape(64, D)
    go[...] = (upstream + inv2[...] * (scaled - plain - x_hat2 * cross)).reshape(8, 8, D).astype(BF16)
    m_first = give(go, out_g, 4)

    a_last(a2)
    a3 = straight(ra, lambda step: wrap(zz + step, 8), (z_dev, raq), 8)
    o_further = gather_second(out_view(out_b), o_first)
    for u in range(4):
        b_last(u, b4[u])
    b5 = straight(rb, lambda step: wrap(y + step, 4), (y_dev, rbq), 4)
    m_further = gather_second(out_view(out_g), m_first)
    fin_b = straight_sum(rb, y, rbq, b5)
    fin_a = straight_sum(ra, zz, raq, a3)
    for c in range(2):
        fin[c, :, 0:CA] = fin_a[c * 18 : c * 18 + 18]
        fin[c, :, CA:] = fin_b[c * 18 : c * 18 + 18]
    sf = fresh()

    def hand_over(src, dst):
        return pltpu.make_async_remote_copy(
            src_ref=src, dst_ref=dst, send_sem=ssem.at[sf], recv_sem=rsem.at[sf], device_id=core_dev, device_id_type=MESH
        )

    @pl.when(core == 0)
    def _():
        hand_over(fin.at[1], out_1).start()
        own = pltpu.make_async_copy(fin.at[0], out_1, asem)
        own.start()
        own.wait()
        hand_over(fin.at[1], out_2).wait()

    @pl.when(core == 1)
    def _():
        hand_over(fin.at[0], out_2).start()
        own = pltpu.make_async_copy(fin.at[1], out_2, asem)
        own.start()
        own.wait()
        hand_over(fin.at[0], out_1).wait()

    gather_third(o_further)
    gather_third(m_further)
    for copy in placed:
        copy.wait()

    for other in range(32):

        @pl.when(s != other)
        def _():
            to_patches(other).wait_send()

        @pl.when(jnp.logical_not(jnp.logical_and(s == other, plane_of(other) == t)))
        def _():
            to_frame(other).wait_send()

    for copy in started:
        copy.wait_send()


def place(*refs):
    sources, results, (buf_b, buf_g, buf_1, buf_2, sems) = refs[:4], refs[4:8], refs[8:]
    copies = []
    for src, dst, buf, parts in zip(sources, results, (buf_b, buf_g, buf_1, buf_2), (4, 4, 1, 1)):
        step = src.shape[0] // parts
        for i in range(parts):
            rows = pl.ds(i * step, step)
            n = len(copies)
            copies.append(
                (
                    pltpu.make_async_copy(src.at[rows], buf.at[rows], sems.at[0, n]),
                    pltpu.make_async_copy(buf.at[rows], dst.at[rows], sems.at[1, n]),
                )
            )
    for read, _ in copies:
        read.start()
    for read, write in copies:
        read.wait()
        write.start()
    for _, write in copies:
        write.wait()


def local(hidden_in, norm1_gain, qkv_weight, out_weight, norm2_gain, fc1_weight, fc2_weight, out_grad):
    anywhere = pl.BlockSpec(memory_space=pl.ANY)
    vmem = pl.BlockSpec(memory_space=pltpu.VMEM)
    shapes = [
        ((32, 8, D), BF16), ((4, 8, 8, D), BF16), ((8, 8, D), BF16),
        ((3 * QC, D), BF16), ((4, QC, D), BF16), ((D, FQ), BF16), ((D, FQ), BF16),
        ((4, 64, D), BF16), ((32, 8, 3 * QC), BF16), ((32, 8, 3 * QC), BF16),
        ((32, 8, QC), BF16), ((4, 8, 8, QC), BF16),
        ((4, 64, D), BF16), ((256, FQ), F32), ((4, 64, D), BF16),
        ((2, 4, 64, D), F32), ((2, 4, 64, D), BF16),
        ((2, 2, 32, D), BF16), ((2, 2, 32, D), BF16), ((2, 2, 64, D), BF16),
        ((64, D), BF16), ((64, D), F32), ((64, 1), F32), ((8, 8, D), BF16), ((8, 8, D), BF16),
        ((ROWS, D), BF16), ((3, ROWS, 256), BF16), ((3, 256, FQ), BF16),
        ((4, 8, SLAB, CA), BF16), ((2, 4, SLAB, CA), BF16), ((2, 4, SLAB, CA), BF16), ((2, 8, SLAB, CA), BF16),
        ((8, SLAB, CA), BF16), ((7, SLAB, CA), BF16),
        ((8, 4, SLAB, CB), BF16), ((4, 2, SLAB, CB), BF16), ((3, 4, 2, SLAB, CB), BF16), ((3, 4, 2, SLAB, CB), BF16),
        ((4, SLAB, CB), BF16), ((3, SLAB, CB), BF16),
        ((2, 18, FQ), F32),
    ]
    scratch = [pltpu.VMEM(shape, kind) for shape, kind in shapes]
    scratch += [
        pltpu.SemaphoreType.DMA((N_SEM,)), pltpu.SemaphoreType.DMA((N_SEM,)),
        pltpu.SemaphoreType.DMA((5,)), pltpu.SemaphoreType.DMA((20,)), pltpu.SemaphoreType.DMA((8,)),
        pltpu.SemaphoreType.DMA,
    ]
    results = [
        jax.ShapeDtypeStruct((32, 8, D), BF16),
        jax.ShapeDtypeStruct((32, 8, D), BF16),
        jax.ShapeDtypeStruct((18, FQ), F32),
        jax.ShapeDtypeStruct((18, FQ), F32),
    ]
    made = pl.pallas_call(
        kernel,
        out_shape=results,
        in_specs=[anywhere, vmem, anywhere, anywhere, vmem, anywhere, anywhere, anywhere],
        out_specs=[anywhere] * 4,
        scratch_shapes=scratch,
        compiler_params=pltpu.CompilerParams(
            collective_id=0, has_side_effects=True, vmem_limit_bytes=60 * 1024 * 1024
        ),
    )(
        hidden_in.reshape(32, 8, D),
        norm1_gain,
        qkv_weight.transpose(1, 2, 0).reshape(3 * QC, D),
        out_weight,
        norm2_gain,
        fc1_weight,
        fc2_weight,
        out_grad.reshape(32, 8, D),
    )
    block, grad_mid, grad_fc1, grad_fc2 = pl.pallas_call(
        place,
        out_shape=results,
        in_specs=[anywhere] * 4,
        out_specs=[anywhere] * 4,
        scratch_shapes=[pltpu.VMEM(made_one.shape, made_one.dtype) for made_one in results]
        + [pltpu.SemaphoreType.DMA((2, 10))],
        compiler_params=pltpu.CompilerParams(vmem_limit_bytes=60 * 1024 * 1024),
    )(*made)
    shape = hidden_in.shape
    return block.reshape(shape), grad_mid.reshape(shape), grad_fc1, grad_fc2


def solution(mesh):
    return jax.shard_map(
        local,
        mesh=mesh,
        in_specs=(
            P("dp", "seq", None, None),
            P(),
            P(None, None, "tensor"),
            P("tensor", None),
            P(),
            P(None, "tensor"),
            P(None, "tensor"),
            P("dp", "seq", None, None),
        ),
        out_specs=(
            P("dp", "seq", None, None),
            P("dp", "seq", None, None),
            P(("seq", "dp"), "tensor"),
            P(("seq", "dp"), "tensor"),
        ),
        check_vma=False,
    )
```

```python
import functools

import jax
import jax.numpy as jnp
import numpy as np
from jax import lax
from jax.experimental import pallas as pl
from jax.experimental.pallas import tpu as pltpu
from jax.sharding import PartitionSpec as P

MESH = pl.DeviceIdType.MESH
BF16 = jnp.bfloat16
F32 = jnp.float32

HDIM = 72
D = 1152
FQ = 1152
QC = 288
SLAB = 36
ROWS = 32 * SLAB
CA = 512
CB = 640
CA2 = CA // 2
NB = CB // 128
EPS = 1e-06
N_SEM = 224


def slab_sources(first, count):
    n = lax.broadcasted_iota(jnp.int32, (count, 1), 0) + first
    slab = (n * 1821) >> 16
    within = n - slab * SLAB
    core = jnp.where(within >= 18, 1, 0)
    z, y = slab >> 2, slab & 3
    return (((z >> 1) * 4 + y) * 2 + core) * 36 + (z & 1) * 18 + within - core * 18


def nn(a, b):
    return jnp.dot(a, b, preferred_element_type=F32)


def nt(a, b):
    return lax.dot_general(a, b, (((1,), (1,)), ((), ())), preferred_element_type=F32)


def normalize(values):
    center = values - jnp.mean(values, -1, keepdims=True)
    inv_std = lax.rsqrt(jnp.mean(center * center, -1, keepdims=True) + EPS)
    return center * inv_std, inv_std


def kernel(
    hid, gain1, wq_h, wo_h, gain2, w1_h, w2_h, og,
    out_b, out_g, out_1, out_2,
    hl, gs, hres, wq, wo, w1, w2, na, qkv, qrec, att, arec, gflat, ga, nb,
    pf, pb, xr1, xs2, xq, mid, xhat, inv2, bo, go,
    perm, lbuf, rbuf,
    wa, ya1, yas, yaq, ra, raq,
    wb, zb1, zbs, zbq, rb, rbq, fin,
    ssem, rsem, lsem, gsem, osem, asem,
):
    t = lax.axis_index("tensor")
    s = lax.axis_index("seq")
    dp = lax.axis_index("dp")
    zh = s // 8
    y = (s // 2) % 4
    core = s % 2
    zz = zh * 2 + dp

    def wrap(value, size):
        return (value + 2 * size) % size

    def x_dev(step):
        return {"tensor": wrap(t + step, 4)}

    def y_dev(step):
        return {"seq": zh * 8 + wrap(y + step, 4) * 2 + core}

    def z_dev(step):
        other = wrap(zz + step, 8)
        return {"seq": (other // 2) * 8 + y * 2 + core, "dp": other % 2}

    core_dev = {"seq": s + 1 - 2 * core}

    def peer_seq(plane, a, k):
        return a * 8 + wrap(plane - zh - y - a, 4) * 2 + k

    barrier = pltpu.get_barrier_semaphore()
    for dev in (x_dev(1), x_dev(-1), z_dev(1), z_dev(-1), z_dev(3), z_dev(-3)):
        pl.semaphore_signal(barrier, inc=1, device_id=dev, device_id_type=MESH)
    for other in range(32):
        pl.semaphore_signal(barrier, inc=1, device_id={"seq": other}, device_id_type=MESH)
    for step in range(1, 4):
        for a in range(4):
            for k in range(2):
                dev = {"seq": peer_seq(t, a, k), "tensor": wrap(t + step, 4)}
                pl.semaphore_signal(barrier, inc=1, device_id=dev, device_id_type=MESH)

    loads = [
        pltpu.make_async_copy(src, dst, lsem.at[i])
        for i, (src, dst) in enumerate(((hid, hl), (wq_h, wq), (wo_h, wo.at[t]), (w2_h, w2), (w1_h, w1)))
    ]
    for load in loads[:2]:
        load.start()

    g1 = gain1[...].reshape(1, D)
    loads[0].wait()

    def norm_rows(i, carry):
        x_hat, _ = normalize(hl[pl.ds(i * 8, 8)].astype(F32).reshape(64, D))
        na[i] = (x_hat * g1).astype(BF16)
        return carry

    lax.fori_loop(0, 4, norm_rows, 0)
    loads[1].wait()
    for load in loads[2:]:
        load.start()
    qkv[...] = nt(na[...].reshape(256, D), wq[...]).reshape(32, 8, 3 * QC).astype(BF16)
    pl.semaphore_wait(barrier, 62)

    count = [0]
    started = []

    def fresh(n=1):
        first = count[0]
        count[0] += n
        return first

    def send(src, dst, dev):
        i = fresh()
        copy = pltpu.make_async_remote_copy(
            src_ref=src, dst_ref=dst, send_sem=ssem.at[i], recv_sem=rsem.at[i], device_id=dev, device_id_type=MESH
        )
        copy.start()
        started.append(copy)
        return copy

    base_h, base_m = fresh(32), fresh(32)

    def to_patches(other):
        return pltpu.make_async_remote_copy(
            src_ref=qkv.at[other], dst_ref=qrec.at[s], send_sem=ssem.at[base_h + other], recv_sem=rsem.at[base_h + s],
            device_id={"seq": other}, device_id_type=MESH,
        )

    for other in range(32):

        @pl.when(s != other)
        def _():
            to_patches(other).start()

        @pl.when(s == other)
        def _():
            pltpu.make_async_copy(qkv.at[other], qrec.at[other], rsem.at[base_h + other]).start()

    turned = [
        pltpu.make_async_copy(
            og.at[pl.ds(peer_seq(plane, a, 0), 2)], gs.at[plane, pl.ds(a * 2, 2)], gsem.at[plane * 4 + a]
        )
        for plane in range(4)
        for a in range(4)
    ] + [
        pltpu.make_async_copy(hid.at[pl.ds(peer_seq(t, a, 0), 2)], hres.at[pl.ds(a * 2, 2)], gsem.at[16 + a])
        for a in range(4)
    ]
    for copy in turned:
        copy.start()

    def gather_first(view, own):
        ups, downs = [None] * 4, [None] * 4
        for up, down in ((0, 2), (1, 3), (2, 0), (3, 1)):
            ups[up] = send(own(up), view(t, up), x_dev(1))
            downs[down] = send(own(down), view(t, down), x_dev(-1))
        return list(zip(ups, downs))

    def gather_second(view, copies):
        left, right = wrap(t - 1, 4), wrap(t + 1, 4)
        further = []
        for a in range(2):
            copies[a][0].wait_recv()
            further.append(send(view(left, a), view(left, a), x_dev(1)))
            copies[a + 2][1].wait_recv()
            further.append(send(view(right, a + 2), view(right, a + 2), x_dev(-1)))
        for a in range(2):
            copies[a + 2][0].wait_recv()
            copies[a][1].wait_recv()
        return further

    def gather_third(further):
        for copy in further:
            copy.wait_recv()

    def wo_part(plane, first, size):
        return wo.at[plane, pl.ds(pl.multiple_of(core * 144 + first, 16), size)]

    def wo_send(first, size):
        src = wo_part(t, first, size)
        return send(src, src, x_dev(1)), send(src, src, x_dev(-1))

    loads[2].wait()
    wo_first = wo_send(0, 144)

    def make_perm(i, carry):
        first = pl.multiple_of(i * 128, 128)
        wanted = slab_sources(first, 128)
        perm[pl.ds(first, 128), :] = jnp.where(
            lax.broadcasted_iota(jnp.int32, (128, D), 1) == wanted, 1.0, 0.0
        ).astype(BF16)
        return carry

    lax.fori_loop(0, ROWS // 128, make_perm, 0)

    wo_first[0].wait_recv()
    wo_first[1].wait_recv()
    left, right, far = wrap(t - 1, 4), wrap(t + 1, 4), wrap(t + 2, 4)
    wo_further = [
        send(wo_part(left, 0, 80), wo_part(left, 0, 80), x_dev(1)),
        send(wo_part(right, 80, 64), wo_part(right, 80, 64), x_dev(-1)),
    ]
    wo_swapped = [send(wo_part(plane, 0, 144), wo_part(plane, 0, 144), core_dev) for plane in (left, right)]

    for other in range(32):
        slab = qrec.at[other]
        pltpu.make_async_copy(slab, slab, rsem.at[base_h + other]).wait()
    q = qrec[:, :, 0:QC].reshape(256, QC)
    k_ = qrec[:, :, QC : 2 * QC].reshape(256, QC)
    v = qrec[:, :, 2 * QC : 3 * QC].reshape(256, QC)
    col = lax.broadcasted_iota(jnp.int32, (1, QC), 1)
    same = (lax.broadcasted_iota(jnp.int32, (256, 256), 0) & 7) == (lax.broadcasted_iota(jnp.int32, (256, 256), 1) & 7)
    total = jnp.zeros((256, QC), F32)
    for h in range(QC // HDIM):
        mine = (col >= h * HDIM) & (col < (h + 1) * HDIM)
        qh = jnp.where(mine, q, jnp.zeros_like(q))
        scores = nt(qh, k_) * HDIM ** (-0.5)
        scores = jnp.where(same, scores, -1e30)
        weights = jnp.exp(scores - jnp.max(scores, -1, keepdims=True))
        probs = (weights * (1.0 / jnp.sum(weights, -1, keepdims=True))).astype(BF16)
        total = jnp.where(mine, nn(probs, v), total)
    att[...] = total.reshape(32, 8, QC).astype(BF16)

    def plane_of(frame):
        return lax.rem(frame // 8 + frame // 2 % 4 + zh + y, 4)

    def to_frame(frame):
        return pltpu.make_async_remote_copy(
            src_ref=att.at[frame], dst_ref=arec.at[t, zh * 2 + core],
            send_sem=ssem.at[base_m + frame], recv_sem=rsem.at[base_m + t * 8 + zh * 2 + core],
            device_id={"seq": frame, "tensor": plane_of(frame)}, device_id_type=MESH,
        )

    for frame in range(32):
        stays = jnp.logical_and(s == frame, plane_of(frame) == t)

        @pl.when(jnp.logical_not(stays))
        def _():
            to_frame(frame).start()

        @pl.when(stays)
        def _():
            here = arec.at[t, zh * 2 + core]
            pltpu.make_async_copy(att.at[frame], here, rsem.at[base_m + t * 8 + zh * 2 + core]).start()

    for copy in wo_further:
        copy.wait_recv()
    wo_swapped.append(send(wo_part(far, 0, 144), wo_part(far, 0, 144), core_dev))

    def partial_sums(u, product):
        for n in range(3):
            value = product(n)
            pf[u, :, :, n * 384 : n * 384 + 384] = value.reshape(4, 64, 384)
            pb[u, :, :, n * 384 : n * 384 + 384] = value.astype(BF16).reshape(4, 64, 384)

    def reduce_first(u):
        far, right, left = wrap(t + 2, 4), wrap(t + 1, 4), wrap(t - 1, 4)
        lo, hi = pl.ds(0, 32), pl.ds(32, 32)
        r1 = send(pb.at[u, far, lo], xr1.at[u, 0], x_dev(1))
        l1 = send(pb.at[u, far, hi], xr1.at[u, 1], x_dev(-1))
        r2 = send(pb.at[u, right, hi], xq.at[u, 0, hi], x_dev(1))
        l2 = send(pb.at[u, left, lo], xq.at[u, 1, lo], x_dev(-1))
        return r1, l1, r2, l2

    def reduce_second(u, copies):
        right, left = wrap(t + 1, 4), wrap(t - 1, 4)
        lo, hi = pl.ds(0, 32), pl.ds(32, 32)
        r1, l1, r2, l2 = copies
        r1.wait_recv()
        xs2[u, 0] = (pf[u, right, 0:32, :] + xr1[u, 0].astype(F32)).astype(BF16)
        r3 = send(xs2.at[u, 0], xq.at[u, 0, lo], x_dev(1))
        l1.wait_recv()
        xs2[u, 1] = (pf[u, left, 32:64, :] + xr1[u, 1].astype(F32)).astype(BF16)
        l3 = send(xs2.at[u, 1], xq.at[u, 1, hi], x_dev(-1))
        return r2, l2, r3, l3

    def reduce_third(u, copies):
        for copy in copies:
            copy.wait_recv()
        return pf[u, t] + xq[u, 0].astype(F32) + xq[u, 1].astype(F32)

    for copy in turned:
        copy.wait()
    for plane in range(4):
        gflat[plane] = gs[plane].astype(F32).reshape(64, D).astype(BF16)
    loads[3].wait()
    loads[4].wait()
    g_all = gflat[...].reshape(256, D)
    for n in range(3):
        c = slice(n * 384, n * 384 + 384)
        ga[:, c] = nn(g_all, w2[:, c])
    for copy in wo_swapped:
        copy.wait_recv()
    for plane in range(4):
        for j in range(8):
            slab = arec.at[plane, j]
            pltpu.make_async_copy(slab, slab, rsem.at[base_m + plane * 8 + j]).wait()

    proj = sum(nn(arec[plane].astype(F32).reshape(64, QC).astype(BF16), wo[plane]) for plane in range(4))
    mid_rows = (hres[...].astype(F32).reshape(64, D) + proj).astype(BF16)
    mid[...] = mid_rows
    x_hat2, inv_std2 = normalize(mid_rows.astype(F32))
    xhat[...] = x_hat2
    inv2[...] = inv_std2
    g2 = gain2[...].reshape(1, D)
    nb[t] = (x_hat2 * g2).astype(BF16)

    def quarter(ref):
        return lambda plane, a: ref.at[plane, pl.ds(a * 16, 16)]

    n_first = gather_first(quarter(nb), lambda a: quarter(nb)(t, a))

    for n in range(3):
        c = slice(n * 384, n * 384 + 384)
        lbuf[0, c, :] = nt(perm[c, :], g_all).astype(BF16)
    n_further = gather_second(quarter(nb), n_first)
    gather_third(n_further)
    nb_all = nb[...].reshape(256, D)
    for n in range(3):
        c = slice(n * 384, n * 384 + 384)
        lbuf[1, c, :] = nt(perm[c, :], nb_all).astype(BF16)

    swapped = [send(lbuf.at[core], lbuf.at[2], core_dev)]
    kept = 1 - core

    root = (2.0 / np.pi) ** 0.5
    for n in range(3):
        c = slice(n * 384, n * 384 + 384)
        pre = nn(nb_all, w1[:, c])
        square = pre * pre
        th = jnp.tanh(root * (pre + 0.044715 * (square * pre)))
        half = 0.5 * (1.0 + th)
        rbuf[0, :, c] = (pre * half).astype(BF16)
        slope = half + 0.5 * pre * (1.0 - th * th) * (root * (1.0 + 3 * 0.044715 * square))
        rbuf[1, :, c] = (ga[:, c] * slope).astype(BF16)
        part = pl.ds(n * 384, 384)
        swapped.append(send(rbuf.at[core, :, part], rbuf.at[2, :, part], core_dev))

    partial_sums(0, lambda n: nt(rbuf[0], w2[n * 384 : n * 384 + 384, :]))
    d_first = reduce_first(0)
    for copy in swapped:
        copy.wait_recv()

    def grad_b(i, carry):
        rows = pl.ds(pl.multiple_of(i * 288, 32), 288)
        value = nn(lbuf[kept, rows, :], rbuf[kept, :, CA:]) + nn(lbuf[2, rows, :], rbuf[2, :, CA:])
        for m in range(2):
            for u in range(NB):
                wb[u, i * 2 + m] = value[m * 144 : (m + 1) * 144, u * 128 : (u + 1) * 128].astype(BF16)
        return carry

    def grad_a(i, carry):
        rows = pl.ds(pl.multiple_of(i * 288, 32), 288)
        value = nn(lbuf[kept, rows, :], rbuf[kept, :, :CA]) + nn(lbuf[2, rows, :], rbuf[2, :, :CA])
        for m in range(8):
            for u in range(2):
                part = value[m * SLAB : (m + 1) * SLAB, u * CA2 : (u + 1) * CA2]
                wa[u, m % 4, i * 2 + m // 4] = part.astype(BF16)
        return carry

    def add(a, b):
        return (a.astype(F32) + b.astype(F32)).astype(BF16)

    halves = (pl.ds(0, 80), pl.ds(80, 64))

    def b_first(u):
        far = wrap(zz + 4, 8)
        return [
            send(wb.at[u, far, halves[d]], zb1.at[u, d, halves[d]], z_dev(1 - 2 * d)) for d in range(2)
        ]

    def b_step(n, u, copies):
        result = []
        for d in range(2):
            sign = 1 - 2 * d
            chunk = wrap(zz + sign * (3 - n), 8)
            copies[d].wait_recv()
            if n == 0:
                taken, other = (slice(0, 80), slice(80, 144))[:: 1 - 2 * d]
                zbs[n, u, d, taken, :] = add(wb[u, chunk, taken, :], zb1[u, d, taken, :])
                zbs[n, u, d, other, :] = wb[u, chunk, other, :]
            else:
                zbs[n, u, d] = add(wb[u, chunk], zbq[n - 1, u, d])
            result.append(send(zbs.at[n, u, d], zbq.at[n, u, d], z_dev(sign)))
        return result

    def b_last(u, copies):
        for copy in copies:
            copy.wait_recv()
        total = wb[u, zz].astype(F32) + zbq[2, u, 0].astype(F32) + zbq[2, u, 1].astype(F32)
        for i in range(4):
            rb[u, i] = total[i * SLAB : (i + 1) * SLAB].astype(BF16)

    def a_first(u):
        far, up, down = wrap(y + 2, 4), wrap(y + 1, 4), wrap(y - 1, 4)
        lo, hi = pl.ds(0, 4), pl.ds(4, 4)
        u1 = send(wa.at[u, far, lo], ya1.at[u, 0], y_dev(1))
        d1 = send(wa.at[u, far, hi], ya1.at[u, 1], y_dev(-1))
        u2 = send(wa.at[u, up, hi], yaq.at[u, 0, hi], y_dev(1))
        d2 = send(wa.at[u, down, lo], yaq.at[u, 1, lo], y_dev(-1))
        return u1, d1, u2, d2

    def a_second(u, copies):
        up, down = wrap(y + 1, 4), wrap(y - 1, 4)
        u1, d1, u2, d2 = copies
        u1.wait_recv()

        def body_up(i, carry):
            yas[u, 0, i] = add(wa[u, up, i], ya1[u, 0, i])
            return carry

        lax.fori_loop(0, 4, body_up, 0)
        u3 = send(yas.at[u, 0], yaq.at[u, 0, pl.ds(0, 4)], y_dev(1))
        d1.wait_recv()

        def body_down(i, carry):
            yas[u, 1, i] = add(wa[u, down, i + 4], ya1[u, 1, i])
            return carry

        lax.fori_loop(0, 4, body_down, 0)
        d3 = send(yas.at[u, 1], yaq.at[u, 1, pl.ds(4, 4)], y_dev(-1))
        return u2, d2, u3, d3

    def a_last(u, copies):
        for copy in copies:
            copy.wait_recv()

        def body(i, carry):
            total = wa[u, y, i].astype(F32) + yaq[u, 0, i].astype(F32) + yaq[u, 1, i].astype(F32)
            ra[u, i] = total.astype(BF16)
            return carry

        lax.fori_loop(0, 8, body, 0)

    def straight(rows, received, dev_of, here, n):
        return [
            send(rows.at[wrap(here + step, n)], received.at[step - 1], dev_of(step)) for step in (n // 2, *range(1, n // 2), *range(n // 2 + 1, n))
        ]

    def straight_sum(rows, received, here, copies):
        for copy in copies:
            copy.wait_recv()
        total = rows[here].astype(F32)
        for i in range(len(copies)):
            total = total + received[i].astype(F32)
        return total

    lax.fori_loop(0, 4, grad_a, 0)
    a1 = [a_first(u) for u in range(2)]
    lax.fori_loop(0, 4, grad_b, 0)
    b1 = [b_first(u) for u in range(NB)]
    partial_sums(1, lambda n: nt(rbuf[1], w1[n * 384 : n * 384 + 384, :]))
    e_first = reduce_first(1)
    d_second = reduce_second(0, d_first)
    b2 = [b_step(0, u, b1[u]) for u in range(NB)]
    a2 = [a_second(0, a1[0])]
    e_second = reduce_second(1, e_first)
    a2.append(a_second(1, a1[1]))
    b3 = [b_step(1, u, b2[u]) for u in range(NB)]

    def out_view(ref):
        return lambda plane, a: ref.at[pl.ds(peer_seq(plane, a, 0), 2)]

    def give(rows, ref, base):
        for a in range(4):
            copy = pltpu.make_async_copy(rows.at[pl.ds(a * 2, 2)], out_view(ref)(t, a), osem.at[base + a])
            copy.start()
            placed.append(copy)
        return gather_first(out_view(ref), lambda a: rows.at[pl.ds(a * 2, 2)])

    placed = []
    down_rows = reduce_third(0, d_second)
    bo[...] = (mid[...].astype(F32) + down_rows).reshape(8, 8, D).astype(BF16)
    o_first = give(bo, out_b, 0)
    b4 = [b_step(2, u, b3[u]) for u in range(NB)]

    scaled = reduce_third(1, e_second) * g2
    x_hat2 = xhat[...]
    plain = jnp.mean(scaled, -1, keepdims=True)
    cross = jnp.mean(scaled * x_hat2, -1, keepdims=True)
    upstream = gs[t].astype(F32).reshape(64, D)
    go[...] = (upstream + inv2[...] * (scaled - plain - x_hat2 * cross)).reshape(8, 8, D).astype(BF16)
    m_first = give(go, out_g, 4)

    a3 = []
    for u in range(2):
        a_last(u, a2[u])
        a3.append(straight(ra.at[u], raq.at[u], z_dev, zz, 8))
    o_further = gather_second(out_view(out_b), o_first)
    b5 = []
    for u in range(NB):
        b_last(u, b4[u])
        b5.append(straight(rb.at[u], rbq.at[u], y_dev, y, 4))
    m_further = gather_second(out_view(out_g), m_first)
    sums = [
        *(((u * CA2, CA2), straight_sum(ra.at[u], raq.at[u], zz, a3[u])) for u in range(2)),
        *(((CA + u * 128, 128), straight_sum(rb.at[u], rbq.at[u], y, b5[u])) for u in range(NB)),
    ]
    for c in range(2):
        for (first, width), total in sums:
            fin[c, :, first : first + width] = total[c * 18 : c * 18 + 18]
    sf = fresh()

    def hand_over(src, dst):
        return pltpu.make_async_remote_copy(
            src_ref=src, dst_ref=dst, send_sem=ssem.at[sf], recv_sem=rsem.at[sf], device_id=core_dev, device_id_type=MESH
        )

    @pl.when(core == 0)
    def _():
        hand_over(fin.at[1], out_1).start()
        own = pltpu.make_async_copy(fin.at[0], out_1, asem)
        own.start()
        own.wait()
        hand_over(fin.at[1], out_2).wait()

    @pl.when(core == 1)
    def _():
        hand_over(fin.at[0], out_2).start()
        own = pltpu.make_async_copy(fin.at[1], out_2, asem)
        own.start()
        own.wait()
        hand_over(fin.at[0], out_1).wait()

    gather_third(o_further)
    gather_third(m_further)
    for copy in placed:
        copy.wait()

    for other in range(32):

        @pl.when(s != other)
        def _():
            to_patches(other).wait_send()

        @pl.when(jnp.logical_not(jnp.logical_and(s == other, plane_of(other) == t)))
        def _():
            to_frame(other).wait_send()

    for copy in started:
        copy.wait_send()


def place(*refs):
    sources, results, (buf_b, buf_g, buf_1, buf_2, sems) = refs[:4], refs[4:8], refs[8:]
    copies = []
    for src, dst, buf, parts in zip(sources, results, (buf_b, buf_g, buf_1, buf_2), (4, 4, 1, 1)):
        step = src.shape[0] // parts
        for i in range(parts):
            rows = pl.ds(i * step, step)
            n = len(copies)
            copies.append(
                (
                    pltpu.make_async_copy(src.at[rows], buf.at[rows], sems.at[0, n]),
                    pltpu.make_async_copy(buf.at[rows], dst.at[rows], sems.at[1, n]),
                )
            )
    for read, _ in copies:
        read.start()
    for read, write in copies:
        read.wait()
        write.start()
    for _, write in copies:
        write.wait()


def local(hidden_in, norm1_gain, qkv_weight, out_weight, norm2_gain, fc1_weight, fc2_weight, out_grad):
    anywhere = pl.BlockSpec(memory_space=pl.ANY)
    vmem = pl.BlockSpec(memory_space=pltpu.VMEM)
    shapes = [
        ((32, 8, D), BF16), ((4, 8, 8, D), BF16), ((8, 8, D), BF16),
        ((3 * QC, D), BF16), ((4, QC, D), BF16), ((D, FQ), BF16), ((D, FQ), BF16),
        ((4, 64, D), BF16), ((32, 8, 3 * QC), BF16), ((32, 8, 3 * QC), BF16),
        ((32, 8, QC), BF16), ((4, 8, 8, QC), BF16),
        ((4, 64, D), BF16), ((256, FQ), F32), ((4, 64, D), BF16),
        ((2, 4, 64, D), F32), ((2, 4, 64, D), BF16),
        ((2, 2, 32, D), BF16), ((2, 2, 32, D), BF16), ((2, 2, 64, D), BF16),
        ((64, D), BF16), ((64, D), F32), ((64, 1), F32), ((8, 8, D), BF16), ((8, 8, D), BF16),
        ((ROWS, D), BF16), ((3, ROWS, 256), BF16), ((3, 256, FQ), BF16),
        ((2, 4, 8, SLAB, CA2), BF16), ((2, 2, 4, SLAB, CA2), BF16), ((2, 2, 4, SLAB, CA2), BF16), ((2, 2, 8, SLAB, CA2), BF16),
        ((2, 8, SLAB, CA2), BF16), ((2, 7, SLAB, CA2), BF16),
        ((NB, 8, 144, 128), BF16), ((NB, 2, 144, 128), BF16), ((3, NB, 2, 144, 128), BF16), ((3, NB, 2, 144, 128), BF16),
        ((NB, 4, SLAB, 128), BF16), ((NB, 3, SLAB, 128), BF16),
        ((2, 18, FQ), F32),
    ]
    scratch = [pltpu.VMEM(shape, kind) for shape, kind in shapes]
    scratch += [
        pltpu.SemaphoreType.DMA((N_SEM,)), pltpu.SemaphoreType.DMA((N_SEM,)),
        pltpu.SemaphoreType.DMA((5,)), pltpu.SemaphoreType.DMA((20,)), pltpu.SemaphoreType.DMA((8,)),
        pltpu.SemaphoreType.DMA,
    ]
    results = [
        jax.ShapeDtypeStruct((32, 8, D), BF16),
        jax.ShapeDtypeStruct((32, 8, D), BF16),
        jax.ShapeDtypeStruct((18, FQ), F32),
        jax.ShapeDtypeStruct((18, FQ), F32),
    ]
    made = pl.pallas_call(
        kernel,
        out_shape=results,
        in_specs=[anywhere, vmem, anywhere, anywhere, vmem, anywhere, anywhere, anywhere],
        out_specs=[anywhere] * 4,
        scratch_shapes=scratch,
        compiler_params=pltpu.CompilerParams(
            collective_id=0, has_side_effects=True, vmem_limit_bytes=60 * 1024 * 1024
        ),
    )(
        hidden_in.reshape(32, 8, D),
        norm1_gain,
        qkv_weight.transpose(1, 2, 0).reshape(3 * QC, D),
        out_weight,
        norm2_gain,
        fc1_weight,
        fc2_weight,
        out_grad.reshape(32, 8, D),
    )
    block, grad_mid, grad_fc1, grad_fc2 = pl.pallas_call(
        place,
        out_shape=results,
        in_specs=[anywhere] * 4,
        out_specs=[anywhere] * 4,
        scratch_shapes=[pltpu.VMEM(made_one.shape, made_one.dtype) for made_one in results]
        + [pltpu.SemaphoreType.DMA((2, 10))],
        compiler_params=pltpu.CompilerParams(vmem_limit_bytes=60 * 1024 * 1024),
    )(*made)
    shape = hidden_in.shape
    return block.reshape(shape), grad_mid.reshape(shape), grad_fc1, grad_fc2


def solution(mesh):
    return jax.shard_map(
        local,
        mesh=mesh,
        in_specs=(
            P("dp", "seq", None, None),
            P(),
            P(None, None, "tensor"),
            P("tensor", None),
            P(),
            P(None, "tensor"),
            P(None, "tensor"),
            P("dp", "seq", None, None),
        ),
        out_specs=(
            P("dp", "seq", None, None),
            P("dp", "seq", None, None),
            P(("seq", "dp"), "tensor"),
            P(("seq", "dp"), "tensor"),
        ),
        check_vma=False,
    )
```

```python
import functools

import jax
import jax.numpy as jnp
import numpy as np
from jax import lax
from jax.experimental import pallas as pl
from jax.experimental.pallas import tpu as pltpu
from jax.sharding import PartitionSpec as P

MESH = pl.DeviceIdType.MESH
BF16 = jnp.bfloat16
F32 = jnp.float32

HDIM = 72
D = 1152
FQ = 1152
QC = 288
SLAB = 36
ROWS = 32 * SLAB
CA = 640
CB = 512
NA = CA // 128
NB = CB // 128
EPS = 1e-06
N_SEM = 256


def slab_sources(first, count):
    n = lax.broadcasted_iota(jnp.int32, (count, 1), 0) + first
    slab = (n * 1821) >> 16
    within = n - slab * SLAB
    core = jnp.where(within >= 18, 1, 0)
    z, y = slab >> 2, slab & 3
    return (((z >> 1) * 4 + y) * 2 + core) * 36 + (z & 1) * 18 + within - core * 18


def nn(a, b):
    return jnp.dot(a, b, preferred_element_type=F32)


def nt(a, b):
    return lax.dot_general(a, b, (((1,), (1,)), ((), ())), preferred_element_type=F32)


def normalize(values):
    center = values - jnp.mean(values, -1, keepdims=True)
    inv_std = lax.rsqrt(jnp.mean(center * center, -1, keepdims=True) + EPS)
    return center * inv_std, inv_std


def kernel(
    hid, gain1, wq_h, wo_h, gain2, w1_h, w2_h, og,
    out_b, out_g, out_1, out_2,
    hl, gs, hres, wq, wo, w1, w2, na, qkv, qrec, att, arec, gflat, ga, nb,
    pf, pb, xr1, xs2, xq, mid, xhat, inv2, bo, go,
    perm, lbuf, rbuf,
    wa, ya1, yas, yaq, rp, zp1, zps, zpq, ra, raq,
    wb, zb1, zbs, zbq, rb, rbq, fin,
    ssem, rsem, lsem, gsem, osem, asem,
):
    t = lax.axis_index("tensor")
    s = lax.axis_index("seq")
    dp = lax.axis_index("dp")
    zh = s // 8
    y = (s // 2) % 4
    core = s % 2
    zz = zh * 2 + dp

    def wrap(value, size):
        return (value + 2 * size) % size

    def x_dev(step):
        return {"tensor": wrap(t + step, 4)}

    def y_dev(step):
        return {"seq": zh * 8 + wrap(y + step, 4) * 2 + core}

    def z_dev(step):
        other = wrap(zz + step, 8)
        return {"seq": (other // 2) * 8 + y * 2 + core, "dp": other % 2}

    core_dev = {"seq": s + 1 - 2 * core}

    def peer_seq(plane, a, k):
        return a * 8 + wrap(plane - zh - y - a, 4) * 2 + k

    barrier = pltpu.get_barrier_semaphore()
    for dev in (x_dev(1), x_dev(-1), z_dev(1), z_dev(-1), z_dev(3), z_dev(-3)):
        pl.semaphore_signal(barrier, inc=1, device_id=dev, device_id_type=MESH)
    for other in range(32):
        pl.semaphore_signal(barrier, inc=1, device_id={"seq": other}, device_id_type=MESH)
    for step in range(1, 4):
        for a in range(4):
            for k in range(2):
                dev = {"seq": peer_seq(t, a, k), "tensor": wrap(t + step, 4)}
                pl.semaphore_signal(barrier, inc=1, device_id=dev, device_id_type=MESH)

    loads = [
        pltpu.make_async_copy(src, dst, lsem.at[i])
        for i, (src, dst) in enumerate(((hid, hl), (wq_h, wq), (wo_h, wo.at[t]), (w2_h, w2), (w1_h, w1)))
    ]
    for load in loads[:2]:
        load.start()

    g1 = gain1[...].reshape(1, D)
    loads[0].wait()

    def norm_rows(i, carry):
        x_hat, _ = normalize(hl[pl.ds(i * 8, 8)].astype(F32).reshape(64, D))
        na[i] = (x_hat * g1).astype(BF16)
        return carry

    lax.fori_loop(0, 4, norm_rows, 0)
    loads[1].wait()
    for load in loads[2:]:
        load.start()
    qkv[...] = nt(na[...].reshape(256, D), wq[...]).reshape(32, 8, 3 * QC).astype(BF16)
    pl.semaphore_wait(barrier, 62)

    count = [0]
    started = []

    def fresh(n=1):
        first = count[0]
        count[0] += n
        return first

    def send(src, dst, dev):
        i = fresh()
        copy = pltpu.make_async_remote_copy(
            src_ref=src, dst_ref=dst, send_sem=ssem.at[i], recv_sem=rsem.at[i], device_id=dev, device_id_type=MESH
        )
        copy.start()
        started.append(copy)
        return copy

    base_h, base_m = fresh(32), fresh(32)

    def to_patches(other):
        return pltpu.make_async_remote_copy(
            src_ref=qkv.at[other], dst_ref=qrec.at[s], send_sem=ssem.at[base_h + other], recv_sem=rsem.at[base_h + s],
            device_id={"seq": other}, device_id_type=MESH,
        )

    for other in range(32):

        @pl.when(s != other)
        def _():
            to_patches(other).start()

        @pl.when(s == other)
        def _():
            pltpu.make_async_copy(qkv.at[other], qrec.at[other], rsem.at[base_h + other]).start()

    turned = [
        pltpu.make_async_copy(
            og.at[pl.ds(peer_seq(plane, a, 0), 2)], gs.at[plane, pl.ds(a * 2, 2)], gsem.at[plane * 4 + a]
        )
        for plane in range(4)
        for a in range(4)
    ] + [
        pltpu.make_async_copy(hid.at[pl.ds(peer_seq(t, a, 0), 2)], hres.at[pl.ds(a * 2, 2)], gsem.at[16 + a])
        for a in range(4)
    ]
    for copy in turned:
        copy.start()

    def gather_first(view, own):
        ups, downs = [None] * 4, [None] * 4
        for up, down in ((0, 2), (1, 3), (2, 0), (3, 1)):
            ups[up] = send(own(up), view(t, up), x_dev(1))
            downs[down] = send(own(down), view(t, down), x_dev(-1))
        return list(zip(ups, downs))

    def gather_second(view, copies):
        left, right = wrap(t - 1, 4), wrap(t + 1, 4)
        further = []
        for a in range(2):
            copies[a][0].wait_recv()
            further.append(send(view(left, a), view(left, a), x_dev(1)))
            copies[a + 2][1].wait_recv()
            further.append(send(view(right, a + 2), view(right, a + 2), x_dev(-1)))
        for a in range(2):
            copies[a + 2][0].wait_recv()
            copies[a][1].wait_recv()
        return further

    def gather_third(further):
        for copy in further:
            copy.wait_recv()

    def wo_part(plane, first, size):
        return wo.at[plane, pl.ds(pl.multiple_of(core * 144 + first, 16), size)]

    def wo_send(first, size):
        src = wo_part(t, first, size)
        return send(src, src, x_dev(1)), send(src, src, x_dev(-1))

    loads[2].wait()
    wo_first = wo_send(0, 144)

    def make_perm(i, carry):
        first = pl.multiple_of(i * 128, 128)
        wanted = slab_sources(first, 128)
        perm[pl.ds(first, 128), :] = jnp.where(
            lax.broadcasted_iota(jnp.int32, (128, D), 1) == wanted, 1.0, 0.0
        ).astype(BF16)
        return carry

    lax.fori_loop(0, ROWS // 128, make_perm, 0)

    wo_first[0].wait_recv()
    wo_first[1].wait_recv()
    left, right, far = wrap(t - 1, 4), wrap(t + 1, 4), wrap(t + 2, 4)
    wo_further = [
        send(wo_part(left, 0, 80), wo_part(left, 0, 80), x_dev(1)),
        send(wo_part(right, 80, 64), wo_part(right, 80, 64), x_dev(-1)),
    ]
    wo_swapped = [send(wo_part(plane, 0, 144), wo_part(plane, 0, 144), core_dev) for plane in (left, right)]

    for other in range(32):
        slab = qrec.at[other]
        pltpu.make_async_copy(slab, slab, rsem.at[base_h + other]).wait()
    q = qrec[:, :, 0:QC].reshape(256, QC)
    k_ = qrec[:, :, QC : 2 * QC].reshape(256, QC)
    v = qrec[:, :, 2 * QC : 3 * QC].reshape(256, QC)
    col = lax.broadcasted_iota(jnp.int32, (1, QC), 1)
    same = (lax.broadcasted_iota(jnp.int32, (256, 256), 0) & 7) == (lax.broadcasted_iota(jnp.int32, (256, 256), 1) & 7)
    total = jnp.zeros((256, QC), F32)
    for h in range(QC // HDIM):
        mine = (col >= h * HDIM) & (col < (h + 1) * HDIM)
        qh = jnp.where(mine, q, jnp.zeros_like(q))
        scores = nt(qh, k_) * HDIM ** (-0.5)
        scores = jnp.where(same, scores, -1e30)
        weights = jnp.exp(scores - jnp.max(scores, -1, keepdims=True))
        probs = (weights * (1.0 / jnp.sum(weights, -1, keepdims=True))).astype(BF16)
        total = jnp.where(mine, nn(probs, v), total)
    att[...] = total.reshape(32, 8, QC).astype(BF16)

    def plane_of(frame):
        return lax.rem(frame // 8 + frame // 2 % 4 + zh + y, 4)

    def to_frame(frame):
        return pltpu.make_async_remote_copy(
            src_ref=att.at[frame], dst_ref=arec.at[t, zh * 2 + core],
            send_sem=ssem.at[base_m + frame], recv_sem=rsem.at[base_m + t * 8 + zh * 2 + core],
            device_id={"seq": frame, "tensor": plane_of(frame)}, device_id_type=MESH,
        )

    for frame in range(32):
        stays = jnp.logical_and(s == frame, plane_of(frame) == t)

        @pl.when(jnp.logical_not(stays))
        def _():
            to_frame(frame).start()

        @pl.when(stays)
        def _():
            here = arec.at[t, zh * 2 + core]
            pltpu.make_async_copy(att.at[frame], here, rsem.at[base_m + t * 8 + zh * 2 + core]).start()

    for copy in wo_further:
        copy.wait_recv()
    wo_swapped.append(send(wo_part(far, 0, 144), wo_part(far, 0, 144), core_dev))

    def partial_sums(u, product):
        for n in range(3):
            value = product(n)
            pf[u, :, :, n * 384 : n * 384 + 384] = value.reshape(4, 64, 384)
            pb[u, :, :, n * 384 : n * 384 + 384] = value.astype(BF16).reshape(4, 64, 384)

    def reduce_first(u):
        far, right, left = wrap(t + 2, 4), wrap(t + 1, 4), wrap(t - 1, 4)
        lo, hi = pl.ds(0, 32), pl.ds(32, 32)
        r1 = send(pb.at[u, far, lo], xr1.at[u, 0], x_dev(1))
        l1 = send(pb.at[u, far, hi], xr1.at[u, 1], x_dev(-1))
        r2 = send(pb.at[u, right, hi], xq.at[u, 0, hi], x_dev(1))
        l2 = send(pb.at[u, left, lo], xq.at[u, 1, lo], x_dev(-1))
        return r1, l1, r2, l2

    def reduce_second(u, copies):
        right, left = wrap(t + 1, 4), wrap(t - 1, 4)
        lo, hi = pl.ds(0, 32), pl.ds(32, 32)
        r1, l1, r2, l2 = copies
        r1.wait_recv()
        xs2[u, 0] = (pf[u, right, 0:32, :] + xr1[u, 0].astype(F32)).astype(BF16)
        r3 = send(xs2.at[u, 0], xq.at[u, 0, lo], x_dev(1))
        l1.wait_recv()
        xs2[u, 1] = (pf[u, left, 32:64, :] + xr1[u, 1].astype(F32)).astype(BF16)
        l3 = send(xs2.at[u, 1], xq.at[u, 1, hi], x_dev(-1))
        return r2, l2, r3, l3

    def reduce_third(u, copies):
        for copy in copies:
            copy.wait_recv()
        return pf[u, t] + xq[u, 0].astype(F32) + xq[u, 1].astype(F32)

    for copy in turned:
        copy.wait()
    for plane in range(4):
        gflat[plane] = gs[plane].astype(F32).reshape(64, D).astype(BF16)
    loads[3].wait()
    loads[4].wait()
    g_all = gflat[...].reshape(256, D)
    for n in range(3):
        c = slice(n * 384, n * 384 + 384)
        ga[:, c] = nn(g_all, w2[:, c])
    for copy in wo_swapped:
        copy.wait_recv()
    for plane in range(4):
        for j in range(8):
            slab = arec.at[plane, j]
            pltpu.make_async_copy(slab, slab, rsem.at[base_m + plane * 8 + j]).wait()

    proj = sum(nn(arec[plane].astype(F32).reshape(64, QC).astype(BF16), wo[plane]) for plane in range(4))
    mid_rows = (hres[...].astype(F32).reshape(64, D) + proj).astype(BF16)
    mid[...] = mid_rows
    x_hat2, inv_std2 = normalize(mid_rows.astype(F32))
    xhat[...] = x_hat2
    inv2[...] = inv_std2
    g2 = gain2[...].reshape(1, D)
    nb[t] = (x_hat2 * g2).astype(BF16)

    def quarter(ref):
        return lambda plane, a: ref.at[plane, pl.ds(a * 16, 16)]

    n_first = gather_first(quarter(nb), lambda a: quarter(nb)(t, a))

    for n in range(3):
        c = slice(n * 384, n * 384 + 384)
        lbuf[0, c, :] = nt(perm[c, :], g_all).astype(BF16)
    n_further = gather_second(quarter(nb), n_first)
    gather_third(n_further)
    nb_all = nb[...].reshape(256, D)
    for n in range(3):
        c = slice(n * 384, n * 384 + 384)
        lbuf[1, c, :] = nt(perm[c, :], nb_all).astype(BF16)

    swapped = [send(lbuf.at[core], lbuf.at[2], core_dev)]
    kept = 1 - core

    root = (2.0 / np.pi) ** 0.5
    for n in range(3):
        c = slice(n * 384, n * 384 + 384)
        pre = nn(nb_all, w1[:, c])
        square = pre * pre
        th = jnp.tanh(root * (pre + 0.044715 * (square * pre)))
        half = 0.5 * (1.0 + th)
        rbuf[0, :, c] = (pre * half).astype(BF16)
        slope = half + 0.5 * pre * (1.0 - th * th) * (root * (1.0 + 3 * 0.044715 * square))
        rbuf[1, :, c] = (ga[:, c] * slope).astype(BF16)
        part = pl.ds(n * 384, 384)
        swapped.append(send(rbuf.at[core, :, part], rbuf.at[2, :, part], core_dev))

    partial_sums(0, lambda n: nt(rbuf[0], w2[n * 384 : n * 384 + 384, :]))
    d_first = reduce_first(0)
    for copy in swapped:
        copy.wait_recv()

    def grad_b(i, carry):
        rows = pl.ds(pl.multiple_of(i * 288, 32), 288)
        value = nn(lbuf[kept, rows, :], rbuf[kept, :, CA:]) + nn(lbuf[2, rows, :], rbuf[2, :, CA:])
        for m in range(2):
            for u in range(NB):
                wb[u, i * 2 + m] = value[m * 144 : (m + 1) * 144, u * 128 : (u + 1) * 128].astype(BF16)
        return carry

    def grad_a(i, carry):
        rows = pl.ds(pl.multiple_of(i * 288, 32), 288)
        value = nn(lbuf[kept, rows, :], rbuf[kept, :, :CA]) + nn(lbuf[2, rows, :], rbuf[2, :, :CA])
        for m in range(8):
            for u in range(NA):
                part = value[m * SLAB : (m + 1) * SLAB, u * 128 : (u + 1) * 128]
                wa[u, m % 4, i * 2 + m // 4] = part.astype(BF16)
        return carry

    def add(a, b):
        return (a.astype(F32) + b.astype(F32)).astype(BF16)

    def ring_first(rows, halves, first):
        far = rows(wrap(zz + 4, 8))
        return [send(far.at[halves[d]], first.at[d, halves[d]], z_dev(1 - 2 * d)) for d in range(2)]

    def ring_step(n, rows, halves, buffers, copies):
        first, passed, got = buffers
        result = []
        for d in range(2):
            sign = 1 - 2 * d
            chunk = rows(wrap(zz + sign * (3 - n), 8))
            copies[d].wait_recv()
            if n == 0:
                taken, other = halves[d], halves[1 - d]
                passed[0, d, taken] = add(chunk[taken], first[d, taken])
                passed[0, d, other] = chunk[other]
            else:
                passed[n, d] = add(chunk[...], got[n - 1, d])
            result.append(send(passed.at[n, d], got.at[n, d], z_dev(sign)))
        return result

    def ring_last(rows, buffers, copies):
        for copy in copies:
            copy.wait_recv()
        got = buffers[2]
        return rows(zz)[...].astype(F32) + got[2, 0].astype(F32) + got[2, 1].astype(F32)

    b_halves = (pl.ds(0, 80), pl.ds(80, 64))

    def b_rows(u):
        return lambda chunk: wb.at[u, chunk]

    def b_buffers(u):
        return zb1.at[u], zbs.at[u], zbq.at[u]

    def b_steps(n, copies):
        return [ring_step(n, b_rows(u), b_halves, b_buffers(u), copies[u]) for u in range(NB)]

    def b_last(u, copies):
        total = ring_last(b_rows(u), b_buffers(u), copies)
        for i in range(4):
            rb[u, i] = total[i * SLAB : (i + 1) * SLAB].astype(BF16)

    p_halves = (pl.ds(0, 1), pl.ds(1, 1))
    p_rows = lambda chunk: rp.at[chunk]
    p_buffers = zp1, zps, zpq

    def a_first(u):
        far, up, down = wrap(y + 2, 4), wrap(y + 1, 4), wrap(y - 1, 4)
        lo, hi = pl.ds(0, 4), pl.ds(4, 4)
        u1 = send(wa.at[u, far, lo], ya1.at[u, 0], y_dev(1))
        d1 = send(wa.at[u, far, hi], ya1.at[u, 1], y_dev(-1))
        u2 = send(wa.at[u, up, hi], yaq.at[u, 0, hi], y_dev(1))
        d2 = send(wa.at[u, down, lo], yaq.at[u, 1, lo], y_dev(-1))
        return u1, d1, u2, d2

    def a_second(u, copies):
        up, down = wrap(y + 1, 4), wrap(y - 1, 4)
        u1, d1, u2, d2 = copies
        u1.wait_recv()

        def body_up(i, carry):
            yas[u, 0, i] = add(wa[u, up, i], ya1[u, 0, i])
            return carry

        lax.fori_loop(0, 4, body_up, 0)
        u3 = send(yas.at[u, 0], yaq.at[u, 0, pl.ds(0, 4)], y_dev(1))
        d1.wait_recv()

        def body_down(i, carry):
            yas[u, 1, i] = add(wa[u, down, i + 4], ya1[u, 1, i])
            return carry

        lax.fori_loop(0, 4, body_down, 0)
        d3 = send(yas.at[u, 1], yaq.at[u, 1, pl.ds(4, 4)], y_dev(-1))
        return u2, d2, u3, d3

    def a_last(u, copies):
        for copy in copies:
            copy.wait_recv()

        def body(i, carry):
            total = wa[u, y, i].astype(F32) + yaq[u, 0, i].astype(F32) + yaq[u, 1, i].astype(F32)
            if u < 2:
                rp[i, u] = total.astype(BF16)
            else:
                ra[u - 2, i] = total.astype(BF16)
            return carry

        lax.fori_loop(0, 8, body, 0)

    def straight(rows, received, dev_of, here, n):
        return [
            send(rows.at[wrap(here + step, n)], received.at[step - 1], dev_of(step)) for step in (n // 2, *range(1, n // 2), *range(n // 2 + 1, n))
        ]

    def straight_sum(rows, received, here, copies):
        for copy in copies:
            copy.wait_recv()
        total = rows[here].astype(F32)
        for i in range(len(copies)):
            total = total + received[i].astype(F32)
        return total

    lax.fori_loop(0, 4, grad_a, 0)
    a1 = [a_first(u) for u in range(3)]
    lax.fori_loop(0, 4, grad_b, 0)
    b1 = [ring_first(b_rows(u), b_halves, zb1.at[u]) for u in range(NB)]
    partial_sums(1, lambda n: nt(rbuf[1], w1[n * 384 : n * 384 + 384, :]))
    e_first = reduce_first(1)
    d_second = reduce_second(0, d_first)
    a2 = [a_second(0, a1[0])]
    a1.append(a_first(3))
    b2 = b_steps(0, b1)
    a2.append(a_second(1, a1[1]))
    a1.append(a_first(4))
    e_second = reduce_second(1, e_first)
    b3 = b_steps(1, b2)
    a2.append(a_second(2, a1[2]))
    a_last(0, a2[0])

    def out_view(ref):
        return lambda plane, a: ref.at[pl.ds(peer_seq(plane, a, 0), 2)]

    def give(rows, ref, base):
        for a in range(4):
            copy = pltpu.make_async_copy(rows.at[pl.ds(a * 2, 2)], out_view(ref)(t, a), osem.at[base + a])
            copy.start()
            placed.append(copy)
        return gather_first(out_view(ref), lambda a: rows.at[pl.ds(a * 2, 2)])

    placed = []
    down_rows = reduce_third(0, d_second)
    bo[...] = (mid[...].astype(F32) + down_rows).reshape(8, 8, D).astype(BF16)
    o_first = give(bo, out_b, 0)
    b4 = b_steps(2, b3)
    a2.append(a_second(3, a1[3]))
    a_last(1, a2[1])
    p1 = ring_first(p_rows, p_halves, zp1)

    scaled = reduce_third(1, e_second) * g2
    x_hat2 = xhat[...]
    plain = jnp.mean(scaled, -1, keepdims=True)
    cross = jnp.mean(scaled * x_hat2, -1, keepdims=True)
    upstream = gs[t].astype(F32).reshape(64, D)
    go[...] = (upstream + inv2[...] * (scaled - plain - x_hat2 * cross)).reshape(8, 8, D).astype(BF16)
    m_first = give(go, out_g, 4)

    a2.append(a_second(4, a1[4]))
    p2 = ring_step(0, p_rows, p_halves, p_buffers, p1)
    a3 = {}

    def a_finish(u):
        a_last(u, a2[u])
        a3[u] = straight(ra.at[u - 2], raq.at[u - 2], z_dev, zz, 8)

    a_finish(2)
    o_further = gather_second(out_view(out_b), o_first)
    a_finish(3)
    p3 = ring_step(1, p_rows, p_halves, p_buffers, p2)
    a_finish(4)
    b5 = []
    for u in range(NB):
        b_last(u, b4[u])
        b5.append(straight(rb.at[u], rbq.at[u], y_dev, y, 4))
    p4 = ring_step(2, p_rows, p_halves, p_buffers, p3)
    m_further = gather_second(out_view(out_g), m_first)
    sums = [(CA + u * 128, straight_sum(rb.at[u], rbq.at[u], y, b5[u])) for u in range(NB)]
    sums += [(u * 128, straight_sum(ra.at[u - 2], raq.at[u - 2], zz, a3[u])) for u in range(2, NA)]
    pair = ring_last(p_rows, p_buffers, p4)
    sums += [(u * 128, pair[u]) for u in range(2)]
    for c in range(2):
        for first, total in sums:
            fin[c, :, first : first + 128] = total[c * 18 : c * 18 + 18]
    sf = fresh()

    def hand_over(src, dst):
        return pltpu.make_async_remote_copy(
            src_ref=src, dst_ref=dst, send_sem=ssem.at[sf], recv_sem=rsem.at[sf], device_id=core_dev, device_id_type=MESH
        )

    @pl.when(core == 0)
    def _():
        hand_over(fin.at[1], out_1).start()
        own = pltpu.make_async_copy(fin.at[0], out_1, asem)
        own.start()
        own.wait()
        hand_over(fin.at[1], out_2).wait()

    @pl.when(core == 1)
    def _():
        hand_over(fin.at[0], out_2).start()
        own = pltpu.make_async_copy(fin.at[1], out_2, asem)
        own.start()
        own.wait()
        hand_over(fin.at[0], out_1).wait()

    gather_third(o_further)
    gather_third(m_further)
    for copy in placed:
        copy.wait()

    for other in range(32):

        @pl.when(s != other)
        def _():
            to_patches(other).wait_send()

        @pl.when(jnp.logical_not(jnp.logical_and(s == other, plane_of(other) == t)))
        def _():
            to_frame(other).wait_send()

    for copy in started:
        copy.wait_send()


def place(*refs):
    sources, results, (buf_b, buf_g, buf_1, buf_2, sems) = refs[:4], refs[4:8], refs[8:]
    copies = []
    for src, dst, buf, parts in zip(sources, results, (buf_b, buf_g, buf_1, buf_2), (4, 4, 1, 1)):
        step = src.shape[0] // parts
        for i in range(parts):
            rows = pl.ds(i * step, step)
            n = len(copies)
            copies.append(
                (
                    pltpu.make_async_copy(src.at[rows], buf.at[rows], sems.at[0, n]),
                    pltpu.make_async_copy(buf.at[rows], dst.at[rows], sems.at[1, n]),
                )
            )
    for read, _ in copies:
        read.start()
    for read, write in copies:
        read.wait()
        write.start()
    for _, write in copies:
        write.wait()


def local(hidden_in, norm1_gain, qkv_weight, out_weight, norm2_gain, fc1_weight, fc2_weight, out_grad):
    anywhere = pl.BlockSpec(memory_space=pl.ANY)
    vmem = pl.BlockSpec(memory_space=pltpu.VMEM)
    shapes = [
        ((32, 8, D), BF16), ((4, 8, 8, D), BF16), ((8, 8, D), BF16),
        ((3 * QC, D), BF16), ((4, QC, D), BF16), ((D, FQ), BF16), ((D, FQ), BF16),
        ((4, 64, D), BF16), ((32, 8, 3 * QC), BF16), ((32, 8, 3 * QC), BF16),
        ((32, 8, QC), BF16), ((4, 8, 8, QC), BF16),
        ((4, 64, D), BF16), ((256, FQ), F32), ((4, 64, D), BF16),
        ((2, 4, 64, D), F32), ((2, 4, 64, D), BF16),
        ((2, 2, 32, D), BF16), ((2, 2, 32, D), BF16), ((2, 2, 64, D), BF16),
        ((64, D), BF16), ((64, D), F32), ((64, 1), F32), ((8, 8, D), BF16), ((8, 8, D), BF16),
        ((ROWS, D), BF16), ((3, ROWS, 256), BF16), ((3, 256, FQ), BF16),
        ((NA, 4, 8, SLAB, 128), BF16), ((NA, 2, 4, SLAB, 128), BF16),
        ((NA, 2, 4, SLAB, 128), BF16), ((NA, 2, 8, SLAB, 128), BF16),
        ((8, 2, SLAB, 128), BF16), ((2, 2, SLAB, 128), BF16),
        ((3, 2, 2, SLAB, 128), BF16), ((3, 2, 2, SLAB, 128), BF16),
        ((NA - 2, 8, SLAB, 128), BF16), ((NA - 2, 7, SLAB, 128), BF16),
        ((NB, 8, 144, 128), BF16), ((NB, 2, 144, 128), BF16),
        ((NB, 3, 2, 144, 128), BF16), ((NB, 3, 2, 144, 128), BF16),
        ((NB, 4, SLAB, 128), BF16), ((NB, 3, SLAB, 128), BF16),
        ((2, 18, FQ), F32),
    ]
    scratch = [pltpu.VMEM(shape, kind) for shape, kind in shapes]
    scratch += [
        pltpu.SemaphoreType.DMA((N_SEM,)), pltpu.SemaphoreType.DMA((N_SEM,)),
        pltpu.SemaphoreType.DMA((5,)), pltpu.SemaphoreType.DMA((20,)), pltpu.SemaphoreType.DMA((8,)),
        pltpu.SemaphoreType.DMA,
    ]
    results = [
        jax.ShapeDtypeStruct((32, 8, D), BF16),
        jax.ShapeDtypeStruct((32, 8, D), BF16),
        jax.ShapeDtypeStruct((18, FQ), F32),
        jax.ShapeDtypeStruct((18, FQ), F32),
    ]
    made = pl.pallas_call(
        kernel,
        out_shape=results,
        in_specs=[anywhere, vmem, anywhere, anywhere, vmem, anywhere, anywhere, anywhere],
        out_specs=[anywhere] * 4,
        scratch_shapes=scratch,
        compiler_params=pltpu.CompilerParams(
            collective_id=0, has_side_effects=True, vmem_limit_bytes=60 * 1024 * 1024
        ),
    )(
        hidden_in.reshape(32, 8, D),
        norm1_gain,
        qkv_weight.transpose(1, 2, 0).reshape(3 * QC, D),
        out_weight,
        norm2_gain,
        fc1_weight,
        fc2_weight,
        out_grad.reshape(32, 8, D),
    )
    block, grad_mid, grad_fc1, grad_fc2 = pl.pallas_call(
        place,
        out_shape=results,
        in_specs=[anywhere] * 4,
        out_specs=[anywhere] * 4,
        scratch_shapes=[pltpu.VMEM(made_one.shape, made_one.dtype) for made_one in results]
        + [pltpu.SemaphoreType.DMA((2, 10))],
        compiler_params=pltpu.CompilerParams(vmem_limit_bytes=60 * 1024 * 1024),
    )(*made)
    shape = hidden_in.shape
    return block.reshape(shape), grad_mid.reshape(shape), grad_fc1, grad_fc2


def solution(mesh):
    return jax.shard_map(
        local,
        mesh=mesh,
        in_specs=(
            P("dp", "seq", None, None),
            P(),
            P(None, None, "tensor"),
            P("tensor", None),
            P(),
            P(None, "tensor"),
            P(None, "tensor"),
            P("dp", "seq", None, None),
        ),
        out_specs=(
            P("dp", "seq", None, None),
            P("dp", "seq", None, None),
            P(("seq", "dp"), "tensor"),
            P(("seq", "dp"), "tensor"),
        ),
        check_vma=False,
    )
```

```python
import functools

import jax
import jax.numpy as jnp
import numpy as np
from jax import lax
from jax.experimental import pallas as pl
from jax.experimental.pallas import tpu as pltpu
from jax.sharding import PartitionSpec as P

MESH = pl.DeviceIdType.MESH
BF16 = jnp.bfloat16
F32 = jnp.float32

HDIM = 72
D = 1152
FQ = 1152
QC = 288
SLAB = 36
ROWS = 32 * SLAB
CA = 512
CB = 640
CA2 = CA // 2
NB = CB // 128
EPS = 1e-06
N_SEM = 224


def slab_sources(first, count):
    n = lax.broadcasted_iota(jnp.int32, (count, 1), 0) + first
    slab = (n * 1821) >> 16
    within = n - slab * SLAB
    core = jnp.where(within >= 18, 1, 0)
    z, y = slab >> 2, slab & 3
    return (((z >> 1) * 4 + y) * 2 + core) * 36 + (z & 1) * 18 + within - core * 18


def nn(a, b):
    return jnp.dot(a, b, preferred_element_type=F32)


def nt(a, b):
    return lax.dot_general(a, b, (((1,), (1,)), ((), ())), preferred_element_type=F32)


def normalize(values):
    center = values - jnp.mean(values, -1, keepdims=True)
    inv_std = lax.rsqrt(jnp.mean(center * center, -1, keepdims=True) + EPS)
    return center * inv_std, inv_std


def kernel(
    hid, gain1, wq_h, wo_h, gain2, w1_h, w2_h, og,
    out_b, out_g, out_1, out_2,
    hl, gs, hres, wq, wo, w1, w2, na, qkv, qrec, att, arec, gflat, ga, nb,
    pf, pb, xr1, xs2, xq, mid, xhat, inv2, bo, go,
    perm, lbuf, rbuf,
    wa, ya1, yas, yaq, ra, raq,
    wb, zb1, zbs, zbq, rb, rbq, fin,
    ssem, rsem, lsem, gsem, osem, asem,
):
    t = lax.axis_index("tensor")
    s = lax.axis_index("seq")
    dp = lax.axis_index("dp")
    zh = s // 8
    y = (s // 2) % 4
    core = s % 2
    zz = zh * 2 + dp

    def wrap(value, size):
        return (value + 2 * size) % size

    def x_dev(step):
        return {"tensor": wrap(t + step, 4)}

    def y_dev(step):
        return {"seq": zh * 8 + wrap(y + step, 4) * 2 + core}

    def z_dev(step):
        other = wrap(zz + step, 8)
        return {"seq": (other // 2) * 8 + y * 2 + core, "dp": other % 2}

    core_dev = {"seq": s + 1 - 2 * core}

    def peer_seq(plane, a, k):
        return a * 8 + wrap(plane - zh - y - a, 4) * 2 + k

    barrier = pltpu.get_barrier_semaphore()
    for dev in (x_dev(1), x_dev(-1), z_dev(1), z_dev(-1), z_dev(3), z_dev(-3)):
        pl.semaphore_signal(barrier, inc=1, device_id=dev, device_id_type=MESH)
    for other in range(32):
        pl.semaphore_signal(barrier, inc=1, device_id={"seq": other}, device_id_type=MESH)
    for step in range(1, 4):
        for a in range(4):
            for k in range(2):
                dev = {"seq": peer_seq(t, a, k), "tensor": wrap(t + step, 4)}
                pl.semaphore_signal(barrier, inc=1, device_id=dev, device_id_type=MESH)

    loads = [
        pltpu.make_async_copy(src, dst, lsem.at[i])
        for i, (src, dst) in enumerate(((hid, hl), (wq_h, wq), (wo_h, wo.at[t]), (w2_h, w2), (w1_h, w1)))
    ]
    for load in loads[:2]:
        load.start()

    g1 = gain1[...].reshape(1, D)
    loads[0].wait()

    def norm_rows(i, carry):
        x_hat, _ = normalize(hl[pl.ds(i * 8, 8)].astype(F32).reshape(64, D))
        na[i] = (x_hat * g1).astype(BF16)
        return carry

    lax.fori_loop(0, 4, norm_rows, 0)
    loads[1].wait()
    for load in loads[2:]:
        load.start()
    qkv[...] = nt(na[...].reshape(256, D), wq[...]).reshape(32, 8, 3 * QC).astype(BF16)
    pl.semaphore_wait(barrier, 62)

    count = [0]
    started = []

    def fresh(n=1):
        first = count[0]
        count[0] += n
        return first

    def send(src, dst, dev):
        i = fresh()
        copy = pltpu.make_async_remote_copy(
            src_ref=src, dst_ref=dst, send_sem=ssem.at[i], recv_sem=rsem.at[i], device_id=dev, device_id_type=MESH
        )
        copy.start()
        started.append(copy)
        return copy

    def sent():
        for copy in started:
            copy.wait_send()
        started.clear()

    base_h, base_m = fresh(32), fresh(32)

    def to_patches(other):
        return pltpu.make_async_remote_copy(
            src_ref=qkv.at[other], dst_ref=qrec.at[s], send_sem=ssem.at[base_h + other], recv_sem=rsem.at[base_h + s],
            device_id={"seq": other}, device_id_type=MESH,
        )

    for other in range(32):

        @pl.when(s != other)
        def _():
            to_patches(other).start()

        @pl.when(s == other)
        def _():
            pltpu.make_async_copy(qkv.at[other], qrec.at[other], rsem.at[base_h + other]).start()

    turned = [
        pltpu.make_async_copy(
            og.at[pl.ds(peer_seq(plane, a, 0), 2)], gs.at[plane, pl.ds(a * 2, 2)], gsem.at[plane * 4 + a]
        )
        for plane in range(4)
        for a in range(4)
    ] + [
        pltpu.make_async_copy(hid.at[pl.ds(peer_seq(t, a, 0), 2)], hres.at[pl.ds(a * 2, 2)], gsem.at[16 + a])
        for a in range(4)
    ]
    for copy in turned:
        copy.start()

    def gather_first(view, own):
        ups, downs = [None] * 4, [None] * 4
        for up, down in ((0, 2), (1, 3), (2, 0), (3, 1)):
            ups[up] = send(own(up), view(t, up), x_dev(1))
            downs[down] = send(own(down), view(t, down), x_dev(-1))
        return list(zip(ups, downs))

    def gather_second(view, copies):
        left, right = wrap(t - 1, 4), wrap(t + 1, 4)
        further = []
        for a in range(2):
            copies[a][0].wait_recv()
            further.append(send(view(left, a), view(left, a), x_dev(1)))
            copies[a + 2][1].wait_recv()
            further.append(send(view(right, a + 2), view(right, a + 2), x_dev(-1)))
        for a in range(2):
            copies[a + 2][0].wait_recv()
            copies[a][1].wait_recv()
        return further

    def gather_third(further):
        for copy in further:
            copy.wait_recv()

    def wo_part(plane, first, size):
        return wo.at[plane, pl.ds(pl.multiple_of(core * 144 + first, 16), size)]

    def wo_send(first, size):
        src = wo_part(t, first, size)
        return send(src, src, x_dev(1)), send(src, src, x_dev(-1))

    loads[2].wait()
    wo_first = wo_send(0, 144)

    def make_perm(i, carry):
        first = pl.multiple_of(i * 128, 128)
        wanted = slab_sources(first, 128)
        perm[pl.ds(first, 128), :] = jnp.where(
            lax.broadcasted_iota(jnp.int32, (128, D), 1) == wanted, 1.0, 0.0
        ).astype(BF16)
        return carry

    lax.fori_loop(0, ROWS // 128, make_perm, 0)

    wo_first[0].wait_recv()
    wo_first[1].wait_recv()
    left, right, far = wrap(t - 1, 4), wrap(t + 1, 4), wrap(t + 2, 4)
    wo_further = [
        send(wo_part(left, 0, 80), wo_part(left, 0, 80), x_dev(1)),
        send(wo_part(right, 80, 64), wo_part(right, 80, 64), x_dev(-1)),
    ]
    wo_swapped = [send(wo_part(plane, 0, 144), wo_part(plane, 0, 144), core_dev) for plane in (left, right)]

    for other in range(32):
        slab = qrec.at[other]
        pltpu.make_async_copy(slab, slab, rsem.at[base_h + other]).wait()
    q = qrec[:, :, 0:QC].reshape(256, QC)
    k_ = qrec[:, :, QC : 2 * QC].reshape(256, QC)
    v = qrec[:, :, 2 * QC : 3 * QC].reshape(256, QC)
    col = lax.broadcasted_iota(jnp.int32, (1, QC), 1)
    same = (lax.broadcasted_iota(jnp.int32, (256, 256), 0) & 7) == (lax.broadcasted_iota(jnp.int32, (256, 256), 1) & 7)
    total = jnp.zeros((256, QC), F32)
    for h in range(QC // HDIM):
        mine = (col >= h * HDIM) & (col < (h + 1) * HDIM)
        qh = jnp.where(mine, q, jnp.zeros_like(q))
        scores = nt(qh, k_) * HDIM ** (-0.5)
        scores = jnp.where(same, scores, -1e30)
        weights = jnp.exp(scores - jnp.max(scores, -1, keepdims=True))
        probs = (weights * (1.0 / jnp.sum(weights, -1, keepdims=True))).astype(BF16)
        total = jnp.where(mine, nn(probs, v), total)
    att[...] = total.reshape(32, 8, QC).astype(BF16)

    def plane_of(frame):
        return lax.rem(frame // 8 + frame // 2 % 4 + zh + y, 4)

    def to_frame(frame):
        return pltpu.make_async_remote_copy(
            src_ref=att.at[frame], dst_ref=arec.at[t, zh * 2 + core],
            send_sem=ssem.at[base_m + frame], recv_sem=rsem.at[base_m + t * 8 + zh * 2 + core],
            device_id={"seq": frame, "tensor": plane_of(frame)}, device_id_type=MESH,
        )

    for frame in range(32):
        stays = jnp.logical_and(s == frame, plane_of(frame) == t)

        @pl.when(jnp.logical_not(stays))
        def _():
            to_frame(frame).start()

        @pl.when(stays)
        def _():
            here = arec.at[t, zh * 2 + core]
            pltpu.make_async_copy(att.at[frame], here, rsem.at[base_m + t * 8 + zh * 2 + core]).start()

    for copy in wo_further:
        copy.wait_recv()
    wo_swapped.append(send(wo_part(far, 0, 144), wo_part(far, 0, 144), core_dev))

    def partial_sums(u, product):
        for n in range(3):
            value = product(n)
            pf[u, :, :, n * 384 : n * 384 + 384] = value.reshape(4, 64, 384)
            pb[u, :, :, n * 384 : n * 384 + 384] = value.astype(BF16).reshape(4, 64, 384)

    def reduce_first(u):
        far, right, left = wrap(t + 2, 4), wrap(t + 1, 4), wrap(t - 1, 4)
        lo, hi = pl.ds(0, 32), pl.ds(32, 32)
        r1 = send(pb.at[u, far, lo], xr1.at[u, 0], x_dev(1))
        l1 = send(pb.at[u, far, hi], xr1.at[u, 1], x_dev(-1))
        r2 = send(pb.at[u, right, hi], xq.at[u, 0, hi], x_dev(1))
        l2 = send(pb.at[u, left, lo], xq.at[u, 1, lo], x_dev(-1))
        return r1, l1, r2, l2

    def reduce_second(u, copies):
        right, left = wrap(t + 1, 4), wrap(t - 1, 4)
        lo, hi = pl.ds(0, 32), pl.ds(32, 32)
        r1, l1, r2, l2 = copies
        r1.wait_recv()
        xs2[u, 0] = (pf[u, right, 0:32, :] + xr1[u, 0].astype(F32)).astype(BF16)
        r3 = send(xs2.at[u, 0], xq.at[u, 0, lo], x_dev(1))
        l1.wait_recv()
        xs2[u, 1] = (pf[u, left, 32:64, :] + xr1[u, 1].astype(F32)).astype(BF16)
        l3 = send(xs2.at[u, 1], xq.at[u, 1, hi], x_dev(-1))
        return r2, l2, r3, l3

    def reduce_third(u, copies):
        for copy in copies:
            copy.wait_recv()
        return pf[u, t] + xq[u, 0].astype(F32) + xq[u, 1].astype(F32)

    for copy in turned:
        copy.wait()
    for plane in range(4):
        gflat[plane] = gs[plane].astype(F32).reshape(64, D).astype(BF16)
    loads[3].wait()
    loads[4].wait()
    g_all = gflat[...].reshape(256, D)
    for n in range(3):
        c = slice(n * 384, n * 384 + 384)
        ga[:, c] = nn(g_all, w2[:, c])
    for copy in wo_swapped:
        copy.wait_recv()
    for plane in range(4):
        for j in range(8):
            slab = arec.at[plane, j]
            pltpu.make_async_copy(slab, slab, rsem.at[base_m + plane * 8 + j]).wait()

    proj = sum(nn(arec[plane].astype(F32).reshape(64, QC).astype(BF16), wo[plane]) for plane in range(4))
    mid_rows = (hres[...].astype(F32).reshape(64, D) + proj).astype(BF16)
    mid[...] = mid_rows
    x_hat2, inv_std2 = normalize(mid_rows.astype(F32))
    xhat[...] = x_hat2
    inv2[...] = inv_std2
    g2 = gain2[...].reshape(1, D)
    nb[t] = (x_hat2 * g2).astype(BF16)

    def quarter(ref):
        return lambda plane, a: ref.at[plane, pl.ds(a * 16, 16)]

    early = list(started)
    started.clear()
    n_first = gather_first(quarter(nb), lambda a: quarter(nb)(t, a))

    for n in range(3):
        c = slice(n * 384, n * 384 + 384)
        lbuf[0, c, :] = nt(perm[c, :], g_all).astype(BF16)
    for other in range(32):

        @pl.when(s != other)
        def _():
            to_patches(other).wait_send()

        @pl.when(jnp.logical_not(jnp.logical_and(s == other, plane_of(other) == t)))
        def _():
            to_frame(other).wait_send()
    n_further = gather_second(quarter(nb), n_first)
    for copy in early:
        copy.wait_send()
    gather_third(n_further)
    nb_all = nb[...].reshape(256, D)
    for n in range(3):
        c = slice(n * 384, n * 384 + 384)
        lbuf[1, c, :] = nt(perm[c, :], nb_all).astype(BF16)

    swapped = [send(lbuf.at[core], lbuf.at[2], core_dev)]
    kept = 1 - core

    root = (2.0 / np.pi) ** 0.5
    for n in range(3):
        c = slice(n * 384, n * 384 + 384)
        pre = nn(nb_all, w1[:, c])
        square = pre * pre
        th = jnp.tanh(root * (pre + 0.044715 * (square * pre)))
        half = 0.5 * (1.0 + th)
        rbuf[0, :, c] = (pre * half).astype(BF16)
        slope = half + 0.5 * pre * (1.0 - th * th) * (root * (1.0 + 3 * 0.044715 * square))
        rbuf[1, :, c] = (ga[:, c] * slope).astype(BF16)
        part = pl.ds(n * 384, 384)
        swapped.append(send(rbuf.at[core, :, part], rbuf.at[2, :, part], core_dev))

    partial_sums(0, lambda n: nt(rbuf[0], w2[n * 384 : n * 384 + 384, :]))
    d_first = reduce_first(0)
    for copy in swapped:
        copy.wait_recv()

    def grad_b(i, carry):
        rows = pl.ds(pl.multiple_of(i * 288, 32), 288)
        value = nn(lbuf[kept, rows, :], rbuf[kept, :, CA:]) + nn(lbuf[2, rows, :], rbuf[2, :, CA:])
        for m in range(2):
            for u in range(NB):
                wb[u, i * 2 + m] = value[m * 144 : (m + 1) * 144, u * 128 : (u + 1) * 128].astype(BF16)
        return carry

    def grad_a(i, carry):
        rows = pl.ds(pl.multiple_of(i * 288, 32), 288)
        value = nn(lbuf[kept, rows, :], rbuf[kept, :, :CA]) + nn(lbuf[2, rows, :], rbuf[2, :, :CA])
        for m in range(8):
            for u in range(2):
                part = value[m * SLAB : (m + 1) * SLAB, u * CA2 : (u + 1) * CA2]
                wa[u, m % 4, i * 2 + m // 4] = part.astype(BF16)
        return carry

    def add(a, b):
        return (a.astype(F32) + b.astype(F32)).astype(BF16)

    halves = (pl.ds(0, 80), pl.ds(80, 64))

    def b_first(u):
        far = wrap(zz + 4, 8)
        return [
            send(wb.at[u, far, halves[d]], zb1.at[u, d, halves[d]], z_dev(1 - 2 * d)) for d in range(2)
        ]

    def b_step(n, u, copies):
        result = []
        for d in range(2):
            sign = 1 - 2 * d
            chunk = wrap(zz + sign * (3 - n), 8)
            copies[d].wait_recv()
            if n == 0:
                taken, other = (slice(0, 80), slice(80, 144))[:: 1 - 2 * d]
                zbs[n, u, d, taken, :] = add(wb[u, chunk, taken, :], zb1[u, d, taken, :])
                zbs[n, u, d, other, :] = wb[u, chunk, other, :]
            else:
                zbs[n, u, d] = add(wb[u, chunk], zbq[n - 1, u, d])
            result.append(send(zbs.at[n, u, d], zbq.at[n, u, d], z_dev(sign)))
        return result

    def b_last(u, copies):
        for copy in copies:
            copy.wait_recv()
        total = wb[u, zz].astype(F32) + zbq[2, u, 0].astype(F32) + zbq[2, u, 1].astype(F32)
        for i in range(4):
            rb[u, i] = total[i * SLAB : (i + 1) * SLAB].astype(BF16)

    def a_first(u):
        far, up, down = wrap(y + 2, 4), wrap(y + 1, 4), wrap(y - 1, 4)
        lo, hi = pl.ds(0, 4), pl.ds(4, 4)
        u1 = send(wa.at[u, far, lo], ya1.at[u, 0], y_dev(1))
        d1 = send(wa.at[u, far, hi], ya1.at[u, 1], y_dev(-1))
        u2 = send(wa.at[u, up, hi], yaq.at[u, 0, hi], y_dev(1))
        d2 = send(wa.at[u, down, lo], yaq.at[u, 1, lo], y_dev(-1))
        return u1, d1, u2, d2

    def a_second(u, copies):
        up, down = wrap(y + 1, 4), wrap(y - 1, 4)
        u1, d1, u2, d2 = copies
        u1.wait_recv()

        def body_up(i, carry):
            yas[u, 0, i] = add(wa[u, up, i], ya1[u, 0, i])
            return carry

        lax.fori_loop(0, 4, body_up, 0)
        u3 = send(yas.at[u, 0], yaq.at[u, 0, pl.ds(0, 4)], y_dev(1))
        d1.wait_recv()

        def body_down(i, carry):
            yas[u, 1, i] = add(wa[u, down, i + 4], ya1[u, 1, i])
            return carry

        lax.fori_loop(0, 4, body_down, 0)
        d3 = send(yas.at[u, 1], yaq.at[u, 1, pl.ds(4, 4)], y_dev(-1))
        return u2, d2, u3, d3

    def a_last(u, copies):
        for copy in copies:
            copy.wait_recv()

        def body(i, carry):
            total = wa[u, y, i].astype(F32) + yaq[u, 0, i].astype(F32) + yaq[u, 1, i].astype(F32)
            ra[u, i] = total.astype(BF16)
            return carry

        lax.fori_loop(0, 8, body, 0)

    def straight(rows, received, dev_of, here, n):
        return [
            send(rows.at[wrap(here + step, n)], received.at[step - 1], dev_of(step)) for step in (n // 2, *range(1, n // 2), *range(n // 2 + 1, n))
        ]

    def straight_sum(rows, received, here, copies):
        for copy in copies:
            copy.wait_recv()
        total = rows[here].astype(F32)
        for i in range(len(copies)):
            total = total + received[i].astype(F32)
        return total

    lax.fori_loop(0, 4, grad_a, 0)
    a1 = [a_first(u) for u in range(2)]
    lax.fori_loop(0, 4, grad_b, 0)
    b1 = [b_first(u) for u in range(NB)]
    partial_sums(1, lambda n: nt(rbuf[1], w1[n * 384 : n * 384 + 384, :]))
    e_first = reduce_first(1)
    d_second = reduce_second(0, d_first)
    b2 = [b_step(0, u, b1[u]) for u in range(NB)]
    a2 = [a_second(0, a1[0])]
    e_second = reduce_second(1, e_first)
    a2.append(a_second(1, a1[1]))
    b3 = [b_step(1, u, b2[u]) for u in range(NB)]

    def out_view(ref):
        return lambda plane, a: ref.at[pl.ds(peer_seq(plane, a, 0), 2)]

    def give(rows, ref, base):
        for a in range(4):
            copy = pltpu.make_async_copy(rows.at[pl.ds(a * 2, 2)], out_view(ref)(t, a), osem.at[base + a])
            copy.start()
            placed.append(copy)
        return gather_first(out_view(ref), lambda a: rows.at[pl.ds(a * 2, 2)])

    placed = []
    down_rows = reduce_third(0, d_second)
    bo[...] = (mid[...].astype(F32) + down_rows).reshape(8, 8, D).astype(BF16)
    o_first = give(bo, out_b, 0)
    a3 = []
    a_last(0, a2[0])
    a3.append(straight(ra.at[0], raq.at[0], z_dev, zz, 8))
    b4 = [b_step(2, u, b3[u]) for u in range(NB)]

    scaled = reduce_third(1, e_second) * g2
    x_hat2 = xhat[...]
    plain = jnp.mean(scaled, -1, keepdims=True)
    cross = jnp.mean(scaled * x_hat2, -1, keepdims=True)
    upstream = gs[t].astype(F32).reshape(64, D)
    go[...] = (upstream + inv2[...] * (scaled - plain - x_hat2 * cross)).reshape(8, 8, D).astype(BF16)
    m_first = give(go, out_g, 4)

    a_last(1, a2[1])
    a3.append(straight(ra.at[1], raq.at[1], z_dev, zz, 8))
    o_further = gather_second(out_view(out_b), o_first)
    b5 = []
    for u in range(NB):
        b_last(u, b4[u])
        b5.append(straight(rb.at[u], rbq.at[u], y_dev, y, 4))
    m_further = gather_second(out_view(out_g), m_first)
    sent()
    sums = [
        *(((u * CA2, CA2), straight_sum(ra.at[u], raq.at[u], zz, a3[u])) for u in range(2)),
        *(((CA + u * 128, 128), straight_sum(rb.at[u], rbq.at[u], y, b5[u])) for u in range(NB)),
    ]
    for c in range(2):
        for (first, width), total in sums:
            fin[c, :, first : first + width] = total[c * 18 : c * 18 + 18]
    sf = fresh()

    def hand_over(src, dst):
        return pltpu.make_async_remote_copy(
            src_ref=src, dst_ref=dst, send_sem=ssem.at[sf], recv_sem=rsem.at[sf], device_id=core_dev, device_id_type=MESH
        )

    @pl.when(core == 0)
    def _():
        hand_over(fin.at[1], out_1).start()
        own = pltpu.make_async_copy(fin.at[0], out_1, asem)
        own.start()
        own.wait()
        hand_over(fin.at[1], out_2).wait()

    @pl.when(core == 1)
    def _():
        hand_over(fin.at[0], out_2).start()
        own = pltpu.make_async_copy(fin.at[1], out_2, asem)
        own.start()
        own.wait()
        hand_over(fin.at[0], out_1).wait()

    gather_third(o_further)
    gather_third(m_further)
    for copy in placed:
        copy.wait()

    sent()


def place(*refs):
    sources, results, (buf_b, buf_g, buf_1, buf_2, sems) = refs[:4], refs[4:8], refs[8:]
    copies = []
    for src, dst, buf, parts in zip(sources, results, (buf_b, buf_g, buf_1, buf_2), (4, 4, 1, 1)):
        step = src.shape[0] // parts
        for i in range(parts):
            rows = pl.ds(i * step, step)
            n = len(copies)
            copies.append(
                (
                    pltpu.make_async_copy(src.at[rows], buf.at[rows], sems.at[0, n]),
                    pltpu.make_async_copy(buf.at[rows], dst.at[rows], sems.at[1, n]),
                )
            )
    for read, _ in copies:
        read.start()
    for read, write in copies:
        read.wait()
        write.start()
    for _, write in copies:
        write.wait()


def local(hidden_in, norm1_gain, qkv_weight, out_weight, norm2_gain, fc1_weight, fc2_weight, out_grad):
    anywhere = pl.BlockSpec(memory_space=pl.ANY)
    vmem = pl.BlockSpec(memory_space=pltpu.VMEM)
    shapes = [
        ((32, 8, D), BF16), ((4, 8, 8, D), BF16), ((8, 8, D), BF16),
        ((3 * QC, D), BF16), ((4, QC, D), BF16), ((D, FQ), BF16), ((D, FQ), BF16),
        ((4, 64, D), BF16), ((32, 8, 3 * QC), BF16), ((32, 8, 3 * QC), BF16),
        ((32, 8, QC), BF16), ((4, 8, 8, QC), BF16),
        ((4, 64, D), BF16), ((256, FQ), F32), ((4, 64, D), BF16),
        ((2, 4, 64, D), F32), ((2, 4, 64, D), BF16),
        ((2, 2, 32, D), BF16), ((2, 2, 32, D), BF16), ((2, 2, 64, D), BF16),
        ((64, D), BF16), ((64, D), F32), ((64, 1), F32), ((8, 8, D), BF16), ((8, 8, D), BF16),
        ((ROWS, D), BF16), ((3, ROWS, 256), BF16), ((3, 256, FQ), BF16),
        ((2, 4, 8, SLAB, CA2), BF16), ((2, 2, 4, SLAB, CA2), BF16), ((2, 2, 4, SLAB, CA2), BF16), ((2, 2, 8, SLAB, CA2), BF16),
        ((2, 8, SLAB, CA2), BF16), ((2, 7, SLAB, CA2), BF16),
        ((NB, 8, 144, 128), BF16), ((NB, 2, 144, 128), BF16), ((3, NB, 2, 144, 128), BF16), ((3, NB, 2, 144, 128), BF16),
        ((NB, 4, SLAB, 128), BF16), ((NB, 3, SLAB, 128), BF16),
        ((2, 18, FQ), F32),
    ]
    scratch = [pltpu.VMEM(shape, kind) for shape, kind in shapes]
    scratch += [
        pltpu.SemaphoreType.DMA((N_SEM,)), pltpu.SemaphoreType.DMA((N_SEM,)),
        pltpu.SemaphoreType.DMA((5,)), pltpu.SemaphoreType.DMA((20,)), pltpu.SemaphoreType.DMA((8,)),
        pltpu.SemaphoreType.DMA,
    ]
    results = [
        jax.ShapeDtypeStruct((32, 8, D), BF16),
        jax.ShapeDtypeStruct((32, 8, D), BF16),
        jax.ShapeDtypeStruct((18, FQ), F32),
        jax.ShapeDtypeStruct((18, FQ), F32),
    ]
    made = pl.pallas_call(
        kernel,
        out_shape=results,
        in_specs=[anywhere, vmem, anywhere, anywhere, vmem, anywhere, anywhere, anywhere],
        out_specs=[anywhere] * 4,
        scratch_shapes=scratch,
        compiler_params=pltpu.CompilerParams(
            collective_id=0, has_side_effects=True, vmem_limit_bytes=60 * 1024 * 1024
        ),
    )(
        hidden_in.reshape(32, 8, D),
        norm1_gain,
        qkv_weight.transpose(1, 2, 0).reshape(3 * QC, D),
        out_weight,
        norm2_gain,
        fc1_weight,
        fc2_weight,
        out_grad.reshape(32, 8, D),
    )
    block, grad_mid, grad_fc1, grad_fc2 = pl.pallas_call(
        place,
        out_shape=results,
        in_specs=[anywhere] * 4,
        out_specs=[anywhere] * 4,
        scratch_shapes=[pltpu.VMEM(made_one.shape, made_one.dtype) for made_one in results]
        + [pltpu.SemaphoreType.DMA((2, 10))],
        compiler_params=pltpu.CompilerParams(vmem_limit_bytes=60 * 1024 * 1024),
    )(*made)
    shape = hidden_in.shape
    return block.reshape(shape), grad_mid.reshape(shape), grad_fc1, grad_fc2


def solution(mesh):
    return jax.shard_map(
        local,
        mesh=mesh,
        in_specs=(
            P("dp", "seq", None, None),
            P(),
            P(None, None, "tensor"),
            P("tensor", None),
            P(),
            P(None, "tensor"),
            P(None, "tensor"),
            P("dp", "seq", None, None),
        ),
        out_specs=(
            P("dp", "seq", None, None),
            P("dp", "seq", None, None),
            P(("seq", "dp"), "tensor"),
            P(("seq", "dp"), "tensor"),
        ),
        check_vma=False,
    )
```

```python
import functools

import jax
import jax.numpy as jnp
import numpy as np
from jax import lax
from jax.experimental import pallas as pl
from jax.experimental.pallas import tpu as pltpu
from jax.sharding import PartitionSpec as P

MESH = pl.DeviceIdType.MESH
BF16 = jnp.bfloat16
F32 = jnp.float32

HDIM = 72
D = 1152
FQ = 1152
QC = 288
SLAB = 36
ROWS = 32 * SLAB
CA = 512
CB = 640
CA2 = CA // 2
NB = CB // 128
EPS = 1e-06
N_SEM = 224


def slab_sources(first, count):
    n = lax.broadcasted_iota(jnp.int32, (count, 1), 0) + first
    slab = (n * 1821) >> 16
    within = n - slab * SLAB
    core = jnp.where(within >= 18, 1, 0)
    z, y = slab >> 2, slab & 3
    return (((z >> 1) * 4 + y) * 2 + core) * 36 + (z & 1) * 18 + within - core * 18


def nn(a, b):
    return jnp.dot(a, b, preferred_element_type=F32)


def nt(a, b):
    return lax.dot_general(a, b, (((1,), (1,)), ((), ())), preferred_element_type=F32)


def normalize(values):
    center = values - jnp.mean(values, -1, keepdims=True)
    inv_std = lax.rsqrt(jnp.mean(center * center, -1, keepdims=True) + EPS)
    return center * inv_std, inv_std


def kernel(
    hid, gain1, wq_h, wo_h, gain2, w1_h, w2_h, og,
    out_b, out_g, out_1, out_2,
    hl, gs, hres, wq, wo, w1, w2, na, qkv, qrec, att, arec, gflat, ga, nb,
    pf, pb, xr1, xs2, xq, mid, xhat, inv2, bo, go,
    perm, lbuf, rbuf,
    wa, ya1, yas, yaq, ra, raq,
    wb, zb1, zbs, zbq, rb, rbq, fin,
    ssem, rsem, lsem, gsem, osem, asem,
):
    t = lax.axis_index("tensor")
    s = lax.axis_index("seq")
    dp = lax.axis_index("dp")
    zh = s // 8
    y = (s // 2) % 4
    core = s % 2
    zz = zh * 2 + dp

    def wrap(value, size):
        return (value + 2 * size) % size

    def x_dev(step):
        return {"tensor": wrap(t + step, 4)}

    def y_dev(step):
        return {"seq": zh * 8 + wrap(y + step, 4) * 2 + core}

    def z_dev(step):
        other = wrap(zz + step, 8)
        return {"seq": (other // 2) * 8 + y * 2 + core, "dp": other % 2}

    core_dev = {"seq": s + 1 - 2 * core}

    def peer_seq(plane, a, k):
        return a * 8 + wrap(plane - zh - y - a, 4) * 2 + k

    barrier = pltpu.get_barrier_semaphore()
    for dev in (x_dev(1), x_dev(-1), z_dev(1), z_dev(-1), z_dev(3), z_dev(-3)):
        pl.semaphore_signal(barrier, inc=1, device_id=dev, device_id_type=MESH)
    for other in range(32):
        pl.semaphore_signal(barrier, inc=1, device_id={"seq": other}, device_id_type=MESH)
    for step in range(1, 4):
        for a in range(4):
            for k in range(2):
                dev = {"seq": peer_seq(t, a, k), "tensor": wrap(t + step, 4)}
                pl.semaphore_signal(barrier, inc=1, device_id=dev, device_id_type=MESH)

    loads = [
        pltpu.make_async_copy(src, dst, lsem.at[i])
        for i, (src, dst) in enumerate(((hid, hl), (wq_h, wq), (wo_h, wo.at[t]), (w2_h, w2), (w1_h, w1)))
    ]
    for load in loads[:2]:
        load.start()

    g1 = gain1[...].reshape(1, D)
    loads[0].wait()

    def norm_rows(i, carry):
        x_hat, _ = normalize(hl[pl.ds(i * 8, 8)].astype(F32).reshape(64, D))
        na[i] = (x_hat * g1).astype(BF16)
        return carry

    lax.fori_loop(0, 4, norm_rows, 0)
    loads[1].wait()
    for load in loads[2:]:
        load.start()
    qkv[...] = nt(na[...].reshape(256, D), wq[...]).reshape(32, 8, 3 * QC).astype(BF16)
    pl.semaphore_wait(barrier, 62)

    count = [0]
    started = []

    def fresh(n=1):
        first = count[0]
        count[0] += n
        return first

    def send(src, dst, dev):
        i = fresh()
        copy = pltpu.make_async_remote_copy(
            src_ref=src, dst_ref=dst, send_sem=ssem.at[i], recv_sem=rsem.at[i], device_id=dev, device_id_type=MESH
        )
        copy.start()
        started.append(copy)
        return copy

    base_h, base_m = fresh(32), fresh(32)

    def to_patches(other):
        return pltpu.make_async_remote_copy(
            src_ref=qkv.at[other], dst_ref=qrec.at[s], send_sem=ssem.at[base_h + other], recv_sem=rsem.at[base_h + s],
            device_id={"seq": other}, device_id_type=MESH,
        )

    for other in range(32):

        @pl.when(s != other)
        def _():
            to_patches(other).start()

        @pl.when(s == other)
        def _():
            pltpu.make_async_copy(qkv.at[other], qrec.at[other], rsem.at[base_h + other]).start()

    turned = [
        pltpu.make_async_copy(
            og.at[pl.ds(peer_seq(plane, a, 0), 2)], gs.at[plane, pl.ds(a * 2, 2)], gsem.at[plane * 4 + a]
        )
        for plane in range(4)
        for a in range(4)
    ] + [
        pltpu.make_async_copy(hid.at[pl.ds(peer_seq(t, a, 0), 2)], hres.at[pl.ds(a * 2, 2)], gsem.at[16 + a])
        for a in range(4)
    ]
    for copy in turned:
        copy.start()

    def gather_first(view, own):
        ups, downs = [None] * 4, [None] * 4
        for up, down in ((0, 2), (1, 3), (2, 0), (3, 1)):
            ups[up] = send(own(up), view(t, up), x_dev(1))
            downs[down] = send(own(down), view(t, down), x_dev(-1))
        return list(zip(ups, downs))

    def gather_second(view, copies):
        left, right = wrap(t - 1, 4), wrap(t + 1, 4)
        further = []
        for a in range(2):
            copies[a][0].wait_recv()
            further.append(send(view(left, a), view(left, a), x_dev(1)))
            copies[a + 2][1].wait_recv()
            further.append(send(view(right, a + 2), view(right, a + 2), x_dev(-1)))
        for a in range(2):
            copies[a + 2][0].wait_recv()
            copies[a][1].wait_recv()
        return further

    def gather_third(further):
        for copy in further:
            copy.wait_recv()

    def wo_part(plane, first, size):
        return wo.at[plane, pl.ds(pl.multiple_of(core * 144 + first, 16), size)]

    def wo_send(first, size):
        src = wo_part(t, first, size)
        return send(src, src, x_dev(1)), send(src, src, x_dev(-1))

    loads[2].wait()
    wo_first = wo_send(0, 144)

    def make_perm(i, carry):
        first = pl.multiple_of(i * 128, 128)
        wanted = slab_sources(first, 128)
        perm[pl.ds(first, 128), :] = jnp.where(
            lax.broadcasted_iota(jnp.int32, (128, D), 1) == wanted, 1.0, 0.0
        ).astype(BF16)
        return carry

    lax.fori_loop(0, ROWS // 128, make_perm, 0)

    wo_first[0].wait_recv()
    wo_first[1].wait_recv()
    left, right, far = wrap(t - 1, 4), wrap(t + 1, 4), wrap(t + 2, 4)
    wo_further = [
        send(wo_part(left, 0, 80), wo_part(left, 0, 80), x_dev(1)),
        send(wo_part(right, 80, 64), wo_part(right, 80, 64), x_dev(-1)),
    ]
    wo_swapped = [send(wo_part(plane, 0, 144), wo_part(plane, 0, 144), core_dev) for plane in (left, right)]

    for other in range(32):
        slab = qrec.at[other]
        pltpu.make_async_copy(slab, slab, rsem.at[base_h + other]).wait()
    q = qrec[:, :, 0:QC].reshape(256, QC)
    k_ = qrec[:, :, QC : 2 * QC].reshape(256, QC)
    v = qrec[:, :, 2 * QC : 3 * QC].reshape(256, QC)
    col = lax.broadcasted_iota(jnp.int32, (1, QC), 1)
    same = (lax.broadcasted_iota(jnp.int32, (256, 256), 0) & 7) == (lax.broadcasted_iota(jnp.int32, (256, 256), 1) & 7)
    total = jnp.zeros((256, QC), F32)
    for h in range(QC // HDIM):
        mine = (col >= h * HDIM) & (col < (h + 1) * HDIM)
        qh = jnp.where(mine, q, jnp.zeros_like(q))
        scores = nt(qh, k_) * HDIM ** (-0.5)
        scores = jnp.where(same, scores, -1e30)
        weights = jnp.exp(scores - jnp.max(scores, -1, keepdims=True))
        probs = (weights * (1.0 / jnp.sum(weights, -1, keepdims=True))).astype(BF16)
        total = jnp.where(mine, nn(probs, v), total)
    att[...] = total.reshape(32, 8, QC).astype(BF16)

    def plane_of(frame):
        return lax.rem(frame // 8 + frame // 2 % 4 + zh + y, 4)

    def to_frame(frame):
        return pltpu.make_async_remote_copy(
            src_ref=att.at[frame], dst_ref=arec.at[t, zh * 2 + core],
            send_sem=ssem.at[base_m + frame], recv_sem=rsem.at[base_m + t * 8 + zh * 2 + core],
            device_id={"seq": frame, "tensor": plane_of(frame)}, device_id_type=MESH,
        )

    for frame in range(32):
        stays = jnp.logical_and(s == frame, plane_of(frame) == t)

        @pl.when(jnp.logical_not(stays))
        def _():
            to_frame(frame).start()

        @pl.when(stays)
        def _():
            here = arec.at[t, zh * 2 + core]
            pltpu.make_async_copy(att.at[frame], here, rsem.at[base_m + t * 8 + zh * 2 + core]).start()

    for copy in wo_further:
        copy.wait_recv()
    wo_swapped.append(send(wo_part(far, 0, 144), wo_part(far, 0, 144), core_dev))

    def partial_sums(u, product):
        for n in range(3):
            value = product(n)
            pf[u, :, :, n * 384 : n * 384 + 384] = value.reshape(4, 64, 384)
            pb[u, :, :, n * 384 : n * 384 + 384] = value.astype(BF16).reshape(4, 64, 384)

    def reduce_first(u):
        far, right, left = wrap(t + 2, 4), wrap(t + 1, 4), wrap(t - 1, 4)
        lo, hi = pl.ds(0, 32), pl.ds(32, 32)
        r1 = send(pb.at[u, far, lo], xr1.at[u, 0], x_dev(1))
        l1 = send(pb.at[u, far, hi], xr1.at[u, 1], x_dev(-1))
        r2 = send(pb.at[u, right, hi], xq.at[u, 0, hi], x_dev(1))
        l2 = send(pb.at[u, left, lo], xq.at[u, 1, lo], x_dev(-1))
        return r1, l1, r2, l2

    def reduce_second(u, copies):
        right, left = wrap(t + 1, 4), wrap(t - 1, 4)
        lo, hi = pl.ds(0, 32), pl.ds(32, 32)
        r1, l1, r2, l2 = copies
        r1.wait_recv()
        xs2[u, 0] = (pf[u, right, 0:32, :] + xr1[u, 0].astype(F32)).astype(BF16)
        r3 = send(xs2.at[u, 0], xq.at[u, 0, lo], x_dev(1))
        l1.wait_recv()
        xs2[u, 1] = (pf[u, left, 32:64, :] + xr1[u, 1].astype(F32)).astype(BF16)
        l3 = send(xs2.at[u, 1], xq.at[u, 1, hi], x_dev(-1))
        return r2, l2, r3, l3

    def reduce_third(u, copies):
        for copy in copies:
            copy.wait_recv()
        return pf[u, t] + xq[u, 0].astype(F32) + xq[u, 1].astype(F32)

    for copy in turned:
        copy.wait()
    for plane in range(4):
        gflat[plane] = gs[plane].astype(F32).reshape(64, D).astype(BF16)
    loads[3].wait()
    loads[4].wait()
    g_all = gflat[...].reshape(256, D)
    for n in range(3):
        c = slice(n * 384, n * 384 + 384)
        ga[:, c] = nn(g_all, w2[:, c])
    for copy in wo_swapped:
        copy.wait_recv()
    for plane in range(4):
        for j in range(8):
            slab = arec.at[plane, j]
            pltpu.make_async_copy(slab, slab, rsem.at[base_m + plane * 8 + j]).wait()

    proj = sum(nn(arec[plane].astype(F32).reshape(64, QC).astype(BF16), wo[plane]) for plane in range(4))
    mid_rows = (hres[...].astype(F32).reshape(64, D) + proj).astype(BF16)
    mid[...] = mid_rows
    x_hat2, inv_std2 = normalize(mid_rows.astype(F32))
    xhat[...] = x_hat2
    inv2[...] = inv_std2
    g2 = gain2[...].reshape(1, D)
    nb[t] = (x_hat2 * g2).astype(BF16)

    def quarter(ref):
        return lambda plane, a: ref.at[plane, pl.ds(a * 16, 16)]

    n_first = gather_first(quarter(nb), lambda a: quarter(nb)(t, a))

    for n in range(3):
        c = slice(n * 384, n * 384 + 384)
        lbuf[0, c, :] = nt(perm[c, :], g_all).astype(BF16)
    n_further = gather_second(quarter(nb), n_first)

    swapped = []
    kept = 1 - core
    root = (2.0 / np.pi) ** 0.5
    for part in range(2):
        if part:
            gather_third(n_further)
        pair = lax.rem(t // 2 + part, 2)
        rows = pl.ds(pl.multiple_of(pair * 128, 128), 128)
        nb_pair = nb[pl.ds(pair * 2, 2)].reshape(128, D)
        for n in range(3):
            c = slice(n * 384, n * 384 + 384)
            lbuf[1, c, rows] = nt(perm[c, :], nb_pair).astype(BF16)
        if part:
            swapped.append(send(lbuf.at[core], lbuf.at[2], core_dev))
        for n in range(3):
            c = slice(n * 384, n * 384 + 384)
            pre = nn(nb_pair, w1[:, c])
            square = pre * pre
            th = jnp.tanh(root * (pre + 0.044715 * (square * pre)))
            half = 0.5 * (1.0 + th)
            rbuf[0, rows, c] = (pre * half).astype(BF16)
            slope = half + 0.5 * pre * (1.0 - th * th) * (root * (1.0 + 3 * 0.044715 * square))
            rbuf[1, rows, c] = (ga[rows, c] * slope).astype(BF16)
            lanes = pl.ds(n * 384, 384)
            swapped.append(send(rbuf.at[core, rows, lanes], rbuf.at[2, rows, lanes], core_dev))

    partial_sums(0, lambda n: nt(rbuf[0], w2[n * 384 : n * 384 + 384, :]))
    d_first = reduce_first(0)
    for copy in swapped:
        copy.wait_recv()

    def grad_b(i, carry):
        rows = pl.ds(pl.multiple_of(i * 288, 32), 288)
        value = nn(lbuf[kept, rows, :], rbuf[kept, :, CA:]) + nn(lbuf[2, rows, :], rbuf[2, :, CA:])
        for m in range(2):
            for u in range(NB):
                wb[u, i * 2 + m] = value[m * 144 : (m + 1) * 144, u * 128 : (u + 1) * 128].astype(BF16)
        return carry

    def grad_a(i, carry):
        rows = pl.ds(pl.multiple_of(i * 288, 32), 288)
        value = nn(lbuf[kept, rows, :], rbuf[kept, :, :CA]) + nn(lbuf[2, rows, :], rbuf[2, :, :CA])
        for m in range(8):
            for u in range(2):
                part = value[m * SLAB : (m + 1) * SLAB, u * CA2 : (u + 1) * CA2]
                wa[u, m % 4, i * 2 + m // 4] = part.astype(BF16)
        return carry

    def add(a, b):
        return (a.astype(F32) + b.astype(F32)).astype(BF16)

    halves = (pl.ds(0, 80), pl.ds(80, 64))

    def b_first(u):
        far = wrap(zz + 4, 8)
        return [
            send(wb.at[u, far, halves[d]], zb1.at[u, d, halves[d]], z_dev(1 - 2 * d)) for d in range(2)
        ]

    def b_step(n, u, copies):
        result = []
        for d in range(2):
            sign = 1 - 2 * d
            chunk = wrap(zz + sign * (3 - n), 8)
            copies[d].wait_recv()
            if n == 0:
                taken, other = (slice(0, 80), slice(80, 144))[:: 1 - 2 * d]
                zbs[n, u, d, taken, :] = add(wb[u, chunk, taken, :], zb1[u, d, taken, :])
                zbs[n, u, d, other, :] = wb[u, chunk, other, :]
            else:
                zbs[n, u, d] = add(wb[u, chunk], zbq[n - 1, u, d])
            result.append(send(zbs.at[n, u, d], zbq.at[n, u, d], z_dev(sign)))
        return result

    def b_last(u, copies):
        for copy in copies:
            copy.wait_recv()
        total = wb[u, zz].astype(F32) + zbq[2, u, 0].astype(F32) + zbq[2, u, 1].astype(F32)
        for i in range(4):
            rb[u, i] = total[i * SLAB : (i + 1) * SLAB].astype(BF16)

    def a_first(u):
        far, up, down = wrap(y + 2, 4), wrap(y + 1, 4), wrap(y - 1, 4)
        lo, hi = pl.ds(0, 4), pl.ds(4, 4)
        u1 = send(wa.at[u, far, lo], ya1.at[u, 0], y_dev(1))
        d1 = send(wa.at[u, far, hi], ya1.at[u, 1], y_dev(-1))
        u2 = send(wa.at[u, up, hi], yaq.at[u, 0, hi], y_dev(1))
        d2 = send(wa.at[u, down, lo], yaq.at[u, 1, lo], y_dev(-1))
        return u1, d1, u2, d2

    def a_second(u, copies):
        up, down = wrap(y + 1, 4), wrap(y - 1, 4)
        u1, d1, u2, d2 = copies
        u1.wait_recv()

        def body_up(i, carry):
            yas[u, 0, i] = add(wa[u, up, i], ya1[u, 0, i])
            return carry

        lax.fori_loop(0, 4, body_up, 0)
        u3 = send(yas.at[u, 0], yaq.at[u, 0, pl.ds(0, 4)], y_dev(1))
        d1.wait_recv()

        def body_down(i, carry):
            yas[u, 1, i] = add(wa[u, down, i + 4], ya1[u, 1, i])
            return carry

        lax.fori_loop(0, 4, body_down, 0)
        d3 = send(yas.at[u, 1], yaq.at[u, 1, pl.ds(4, 4)], y_dev(-1))
        return u2, d2, u3, d3

    def a_last(u, copies):
        for copy in copies:
            copy.wait_recv()

        def body(i, carry):
            total = wa[u, y, i].astype(F32) + yaq[u, 0, i].astype(F32) + yaq[u, 1, i].astype(F32)
            ra[u, i] = total.astype(BF16)
            return carry

        lax.fori_loop(0, 8, body, 0)

    def straight(rows, received, dev_of, here, n):
        return [
            send(rows.at[wrap(here + step, n)], received.at[step - 1], dev_of(step)) for step in (n // 2, *range(1, n // 2), *range(n // 2 + 1, n))
        ]

    def straight_sum(rows, received, here, copies):
        for copy in copies:
            copy.wait_recv()
        total = rows[here].astype(F32)
        for i in range(len(copies)):
            total = total + received[i].astype(F32)
        return total

    lax.fori_loop(0, 4, grad_a, 0)
    a1 = [a_first(u) for u in range(2)]
    lax.fori_loop(0, 4, grad_b, 0)
    b1 = [b_first(u) for u in range(NB)]
    partial_sums(1, lambda n: nt(rbuf[1], w1[n * 384 : n * 384 + 384, :]))
    e_first = reduce_first(1)
    d_second = reduce_second(0, d_first)
    b2 = [b_step(0, u, b1[u]) for u in range(NB)]
    a2 = [a_second(0, a1[0])]
    e_second = reduce_second(1, e_first)
    a2.append(a_second(1, a1[1]))
    b3 = [b_step(1, u, b2[u]) for u in range(NB)]

    def out_view(ref):
        return lambda plane, a: ref.at[pl.ds(peer_seq(plane, a, 0), 2)]

    def give(rows, ref, base):
        for a in range(4):
            copy = pltpu.make_async_copy(rows.at[pl.ds(a * 2, 2)], out_view(ref)(t, a), osem.at[base + a])
            copy.start()
            placed.append(copy)
        return gather_first(out_view(ref), lambda a: rows.at[pl.ds(a * 2, 2)])

    placed = []
    down_rows = reduce_third(0, d_second)
    bo[...] = (mid[...].astype(F32) + down_rows).reshape(8, 8, D).astype(BF16)
    o_first = give(bo, out_b, 0)
    b4 = [b_step(2, u, b3[u]) for u in range(NB)]

    scaled = reduce_third(1, e_second) * g2
    x_hat2 = xhat[...]
    plain = jnp.mean(scaled, -1, keepdims=True)
    cross = jnp.mean(scaled * x_hat2, -1, keepdims=True)
    upstream = gs[t].astype(F32).reshape(64, D)
    go[...] = (upstream + inv2[...] * (scaled - plain - x_hat2 * cross)).reshape(8, 8, D).astype(BF16)
    m_first = give(go, out_g, 4)

    a3 = []
    for u in range(2):
        a_last(u, a2[u])
        a3.append(straight(ra.at[u], raq.at[u], z_dev, zz, 8))
    o_further = gather_second(out_view(out_b), o_first)
    b5 = []
    for u in range(NB):
        b_last(u, b4[u])
        b5.append(straight(rb.at[u], rbq.at[u], y_dev, y, 4))
    m_further = gather_second(out_view(out_g), m_first)
    sums = [
        *(((u * CA2, CA2), straight_sum(ra.at[u], raq.at[u], zz, a3[u])) for u in range(2)),
        *(((CA + u * 128, 128), straight_sum(rb.at[u], rbq.at[u], y, b5[u])) for u in range(NB)),
    ]
    for c in range(2):
        for (first, width), total in sums:
            fin[c, :, first : first + width] = total[c * 18 : c * 18 + 18]
    sf = fresh()

    def hand_over(src, dst):
        return pltpu.make_async_remote_copy(
            src_ref=src, dst_ref=dst, send_sem=ssem.at[sf], recv_sem=rsem.at[sf], device_id=core_dev, device_id_type=MESH
        )

    @pl.when(core == 0)
    def _():
        hand_over(fin.at[1], out_1).start()
        own = pltpu.make_async_copy(fin.at[0], out_1, asem)
        own.start()
        own.wait()
        hand_over(fin.at[1], out_2).wait()

    @pl.when(core == 1)
    def _():
        hand_over(fin.at[0], out_2).start()
        own = pltpu.make_async_copy(fin.at[1], out_2, asem)
        own.start()
        own.wait()
        hand_over(fin.at[0], out_1).wait()

    gather_third(o_further)
    gather_third(m_further)
    for copy in placed:
        copy.wait()

    for other in range(32):

        @pl.when(s != other)
        def _():
            to_patches(other).wait_send()

        @pl.when(jnp.logical_not(jnp.logical_and(s == other, plane_of(other) == t)))
        def _():
            to_frame(other).wait_send()

    for copy in started:
        copy.wait_send()


def place(*refs):
    sources, results, (buf_b, buf_g, buf_1, buf_2, sems) = refs[:4], refs[4:8], refs[8:]
    copies = []
    for src, dst, buf, parts in zip(sources, results, (buf_b, buf_g, buf_1, buf_2), (4, 4, 1, 1)):
        step = src.shape[0] // parts
        for i in range(parts):
            rows = pl.ds(i * step, step)
            n = len(copies)
            copies.append(
                (
                    pltpu.make_async_copy(src.at[rows], buf.at[rows], sems.at[0, n]),
                    pltpu.make_async_copy(buf.at[rows], dst.at[rows], sems.at[1, n]),
                )
            )
    for read, _ in copies:
        read.start()
    for read, write in copies:
        read.wait()
        write.start()
    for _, write in copies:
        write.wait()


def local(hidden_in, norm1_gain, qkv_weight, out_weight, norm2_gain, fc1_weight, fc2_weight, out_grad):
    anywhere = pl.BlockSpec(memory_space=pl.ANY)
    vmem = pl.BlockSpec(memory_space=pltpu.VMEM)
    shapes = [
        ((32, 8, D), BF16), ((4, 8, 8, D), BF16), ((8, 8, D), BF16),
        ((3 * QC, D), BF16), ((4, QC, D), BF16), ((D, FQ), BF16), ((D, FQ), BF16),
        ((4, 64, D), BF16), ((32, 8, 3 * QC), BF16), ((32, 8, 3 * QC), BF16),
        ((32, 8, QC), BF16), ((4, 8, 8, QC), BF16),
        ((4, 64, D), BF16), ((256, FQ), F32), ((4, 64, D), BF16),
        ((2, 4, 64, D), F32), ((2, 4, 64, D), BF16),
        ((2, 2, 32, D), BF16), ((2, 2, 32, D), BF16), ((2, 2, 64, D), BF16),
        ((64, D), BF16), ((64, D), F32), ((64, 1), F32), ((8, 8, D), BF16), ((8, 8, D), BF16),
        ((ROWS, D), BF16), ((3, ROWS, 256), BF16), ((3, 256, FQ), BF16),
        ((2, 4, 8, SLAB, CA2), BF16), ((2, 2, 4, SLAB, CA2), BF16), ((2, 2, 4, SLAB, CA2), BF16), ((2, 2, 8, SLAB, CA2), BF16),
        ((2, 8, SLAB, CA2), BF16), ((2, 7, SLAB, CA2), BF16),
        ((NB, 8, 144, 128), BF16), ((NB, 2, 144, 128), BF16), ((3, NB, 2, 144, 128), BF16), ((3, NB, 2, 144, 128), BF16),
        ((NB, 4, SLAB, 128), BF16), ((NB, 3, SLAB, 128), BF16),
        ((2, 18, FQ), F32),
    ]
    scratch = [pltpu.VMEM(shape, kind) for shape, kind in shapes]
    scratch += [
        pltpu.SemaphoreType.DMA((N_SEM,)), pltpu.SemaphoreType.DMA((N_SEM,)),
        pltpu.SemaphoreType.DMA((5,)), pltpu.SemaphoreType.DMA((20,)), pltpu.SemaphoreType.DMA((8,)),
        pltpu.SemaphoreType.DMA,
    ]
    results = [
        jax.ShapeDtypeStruct((32, 8, D), BF16),
        jax.ShapeDtypeStruct((32, 8, D), BF16),
        jax.ShapeDtypeStruct((18, FQ), F32),
        jax.ShapeDtypeStruct((18, FQ), F32),
    ]
    made = pl.pallas_call(
        kernel,
        out_shape=results,
        in_specs=[anywhere, vmem, anywhere, anywhere, vmem, anywhere, anywhere, anywhere],
        out_specs=[anywhere] * 4,
        scratch_shapes=scratch,
        compiler_params=pltpu.CompilerParams(
            collective_id=0, has_side_effects=True, vmem_limit_bytes=60 * 1024 * 1024
        ),
    )(
        hidden_in.reshape(32, 8, D),
        norm1_gain,
        qkv_weight.transpose(1, 2, 0).reshape(3 * QC, D),
        out_weight,
        norm2_gain,
        fc1_weight,
        fc2_weight,
        out_grad.reshape(32, 8, D),
    )
    block, grad_mid, grad_fc1, grad_fc2 = pl.pallas_call(
        place,
        out_shape=results,
        in_specs=[anywhere] * 4,
        out_specs=[anywhere] * 4,
        scratch_shapes=[pltpu.VMEM(made_one.shape, made_one.dtype) for made_one in results]
        + [pltpu.SemaphoreType.DMA((2, 10))],
        compiler_params=pltpu.CompilerParams(vmem_limit_bytes=60 * 1024 * 1024),
    )(*made)
    shape = hidden_in.shape
    return block.reshape(shape), grad_mid.reshape(shape), grad_fc1, grad_fc2


def solution(mesh):
    return jax.shard_map(
        local,
        mesh=mesh,
        in_specs=(
            P("dp", "seq", None, None),
            P(),
            P(None, None, "tensor"),
            P("tensor", None),
            P(),
            P(None, "tensor"),
            P(None, "tensor"),
            P("dp", "seq", None, None),
        ),
        out_specs=(
            P("dp", "seq", None, None),
            P("dp", "seq", None, None),
            P(("seq", "dp"), "tensor"),
            P(("seq", "dp"), "tensor"),
        ),
        check_vma=False,
    )
```

```python
import functools

import jax
import jax.numpy as jnp
import numpy as np
from jax import lax
from jax.experimental import pallas as pl
from jax.experimental.pallas import tpu as pltpu
from jax.sharding import PartitionSpec as P

MESH = pl.DeviceIdType.MESH
BF16 = jnp.bfloat16
F32 = jnp.float32

HDIM = 72
D = 1152
FQ = 1152
QC = 288
SLAB = 36
ROWS = 32 * SLAB
CA = 512
CB = 640
CA2 = CA // 2
NB = CB // 128
EPS = 1e-06
N_SEM = 224


def slab_sources(first, count):
    n = lax.broadcasted_iota(jnp.int32, (count, 1), 0) + first
    slab = (n * 1821) >> 16
    within = n - slab * SLAB
    core = jnp.where(within >= 18, 1, 0)
    z, y = slab >> 2, slab & 3
    return (((z >> 1) * 4 + y) * 2 + core) * 36 + (z & 1) * 18 + within - core * 18


def nn(a, b):
    return jnp.dot(a, b, preferred_element_type=F32)


def nt(a, b):
    return lax.dot_general(a, b, (((1,), (1,)), ((), ())), preferred_element_type=F32)


def normalize(values):
    center = values - jnp.mean(values, -1, keepdims=True)
    inv_std = lax.rsqrt(jnp.mean(center * center, -1, keepdims=True) + EPS)
    return center * inv_std, inv_std


def kernel(
    hid, gain1, wq_h, wo_h, gain2, w1_h, w2_h, og,
    out_b, out_g, out_1, out_2,
    hl, gs, hres, wq, wo, w1, w2, na, qkv, qrec, att, arec, gflat, ga, nb,
    pf, pb, xr1, xs2, xq, mid, xhat, inv2, bo, go,
    perm, lbuf, rbuf,
    wa, ya1, yas, yaq, ra, raq,
    wb, zb1, zbs, zbq, rb, rbq, fin,
    ssem, rsem, lsem, gsem, osem, asem,
):
    t = lax.axis_index("tensor")
    s = lax.axis_index("seq")
    dp = lax.axis_index("dp")
    zh = s // 8
    y = (s // 2) % 4
    core = s % 2
    zz = zh * 2 + dp

    def wrap(value, size):
        return (value + 2 * size) % size

    def x_dev(step):
        return {"tensor": wrap(t + step, 4)}

    def y_dev(step):
        return {"seq": zh * 8 + wrap(y + step, 4) * 2 + core}

    def z_dev(step):
        other = wrap(zz + step, 8)
        return {"seq": (other // 2) * 8 + y * 2 + core, "dp": other % 2}

    core_dev = {"seq": s + 1 - 2 * core}

    def peer_seq(plane, a, k):
        return a * 8 + wrap(plane - zh - y - a, 4) * 2 + k

    barrier = pltpu.get_barrier_semaphore()
    for dev in (x_dev(1), x_dev(-1), z_dev(1), z_dev(-1), z_dev(3), z_dev(-3)):
        pl.semaphore_signal(barrier, inc=1, device_id=dev, device_id_type=MESH)
    for other in range(32):
        pl.semaphore_signal(barrier, inc=1, device_id={"seq": other}, device_id_type=MESH)
    for step in range(1, 4):
        for a in range(4):
            for k in range(2):
                dev = {"seq": peer_seq(t, a, k), "tensor": wrap(t + step, 4)}
                pl.semaphore_signal(barrier, inc=1, device_id=dev, device_id_type=MESH)

    loads = [
        pltpu.make_async_copy(src, dst, lsem.at[i])
        for i, (src, dst) in enumerate(((hid, hl), (wq_h, wq), (wo_h, wo.at[t]), (w2_h, w2), (w1_h, w1)))
    ]
    for load in loads[:2]:
        load.start()

    g1 = gain1[...].reshape(1, D)
    loads[0].wait()

    def norm_rows(i, carry):
        x_hat, _ = normalize(hl[pl.ds(i * 8, 8)].astype(F32).reshape(64, D))
        na[i] = (x_hat * g1).astype(BF16)
        return carry

    lax.fori_loop(0, 4, norm_rows, 0)
    loads[1].wait()
    for load in loads[2:]:
        load.start()
    qkv[...] = nt(na[...].reshape(256, D), wq[...]).reshape(32, 8, 3 * QC).astype(BF16)
    pl.semaphore_wait(barrier, 62)

    count = [0]
    started = []

    def fresh(n=1):
        first = count[0]
        count[0] += n
        return first

    def send(src, dst, dev):
        i = fresh()
        copy = pltpu.make_async_remote_copy(
            src_ref=src, dst_ref=dst, send_sem=ssem.at[i], recv_sem=rsem.at[i], device_id=dev, device_id_type=MESH
        )
        copy.start()
        started.append(copy)
        return copy

    base_h, base_m = fresh(32), fresh(32)

    turns = (*range(16, 24), *range(8, 16), *range(24, 32), *range(1, 8))

    def to_patches(turn):
        other = lax.rem(s + turn, 32)
        return pltpu.make_async_remote_copy(
            src_ref=qkv.at[other], dst_ref=qrec.at[s], send_sem=ssem.at[base_h + turn], recv_sem=rsem.at[base_h + s],
            device_id={"seq": other}, device_id_type=MESH,
        )

    for turn in turns:
        to_patches(turn).start()
    pltpu.make_async_copy(qkv.at[s], qrec.at[s], rsem.at[base_h + s]).start()

    turned = [
        pltpu.make_async_copy(
            og.at[pl.ds(peer_seq(plane, a, 0), 2)], gs.at[plane, pl.ds(a * 2, 2)], gsem.at[plane * 4 + a]
        )
        for plane in range(4)
        for a in range(4)
    ] + [
        pltpu.make_async_copy(hid.at[pl.ds(peer_seq(t, a, 0), 2)], hres.at[pl.ds(a * 2, 2)], gsem.at[16 + a])
        for a in range(4)
    ]
    for copy in turned:
        copy.start()

    def gather_first(view, own):
        ups, downs = [None] * 4, [None] * 4
        for up, down in ((0, 2), (1, 3), (2, 0), (3, 1)):
            ups[up] = send(own(up), view(t, up), x_dev(1))
            downs[down] = send(own(down), view(t, down), x_dev(-1))
        return list(zip(ups, downs))

    def gather_second(view, copies):
        left, right = wrap(t - 1, 4), wrap(t + 1, 4)
        further = []
        for a in range(2):
            copies[a][0].wait_recv()
            further.append(send(view(left, a), view(left, a), x_dev(1)))
            copies[a + 2][1].wait_recv()
            further.append(send(view(right, a + 2), view(right, a + 2), x_dev(-1)))
        for a in range(2):
            copies[a + 2][0].wait_recv()
            copies[a][1].wait_recv()
        return further

    def gather_third(further):
        for copy in further:
            copy.wait_recv()

    def wo_part(plane, first, size):
        return wo.at[plane, pl.ds(pl.multiple_of(core * 144 + first, 16), size)]

    def wo_send(first, size):
        src = wo_part(t, first, size)
        return send(src, src, x_dev(1)), send(src, src, x_dev(-1))

    loads[2].wait()
    wo_first = wo_send(0, 144)

    def make_perm(i, carry):
        first = pl.multiple_of(i * 128, 128)
        wanted = slab_sources(first, 128)
        perm[pl.ds(first, 128), :] = jnp.where(
            lax.broadcasted_iota(jnp.int32, (128, D), 1) == wanted, 1.0, 0.0
        ).astype(BF16)
        return carry

    lax.fori_loop(0, ROWS // 128, make_perm, 0)

    wo_first[0].wait_recv()
    wo_first[1].wait_recv()
    left, right, far = wrap(t - 1, 4), wrap(t + 1, 4), wrap(t + 2, 4)
    wo_further = [
        send(wo_part(left, 0, 80), wo_part(left, 0, 80), x_dev(1)),
        send(wo_part(right, 80, 64), wo_part(right, 80, 64), x_dev(-1)),
    ]
    wo_swapped = [send(wo_part(plane, 0, 144), wo_part(plane, 0, 144), core_dev) for plane in (left, right)]

    for other in range(32):
        slab = qrec.at[other]
        pltpu.make_async_copy(slab, slab, rsem.at[base_h + other]).wait()
    q = qrec[:, :, 0:QC].reshape(256, QC)
    k_ = qrec[:, :, QC : 2 * QC].reshape(256, QC)
    v = qrec[:, :, 2 * QC : 3 * QC].reshape(256, QC)
    col = lax.broadcasted_iota(jnp.int32, (1, QC), 1)
    same = (lax.broadcasted_iota(jnp.int32, (256, 256), 0) & 7) == (lax.broadcasted_iota(jnp.int32, (256, 256), 1) & 7)
    total = jnp.zeros((256, QC), F32)
    for h in range(QC // HDIM):
        mine = (col >= h * HDIM) & (col < (h + 1) * HDIM)
        qh = jnp.where(mine, q, jnp.zeros_like(q))
        scores = nt(qh, k_) * HDIM ** (-0.5)
        scores = jnp.where(same, scores, -1e30)
        weights = jnp.exp(scores - jnp.max(scores, -1, keepdims=True))
        probs = (weights * (1.0 / jnp.sum(weights, -1, keepdims=True))).astype(BF16)
        total = jnp.where(mine, nn(probs, v), total)
    att[...] = total.reshape(32, 8, QC).astype(BF16)

    def plane_of(frame):
        return lax.rem(frame // 8 + frame // 2 % 4 + zh + y, 4)

    def to_frame(turn):
        frame = lax.rem(s + turn, 32)
        return pltpu.make_async_remote_copy(
            src_ref=att.at[frame], dst_ref=arec.at[t, zh * 2 + core],
            send_sem=ssem.at[base_m + turn], recv_sem=rsem.at[base_m + t * 8 + zh * 2 + core],
            device_id={"seq": frame, "tensor": plane_of(frame)}, device_id_type=MESH,
        )

    for turn in turns:
        to_frame(turn).start()
    stays = plane_of(s) == t

    @pl.when(jnp.logical_not(stays))
    def _():
        to_frame(0).start()

    @pl.when(stays)
    def _():
        here = arec.at[t, zh * 2 + core]
        pltpu.make_async_copy(att.at[s], here, rsem.at[base_m + t * 8 + zh * 2 + core]).start()

    for copy in wo_further:
        copy.wait_recv()
    wo_swapped.append(send(wo_part(far, 0, 144), wo_part(far, 0, 144), core_dev))

    def partial_sums(u, product):
        for n in range(3):
            value = product(n)
            pf[u, :, :, n * 384 : n * 384 + 384] = value.reshape(4, 64, 384)
            pb[u, :, :, n * 384 : n * 384 + 384] = value.astype(BF16).reshape(4, 64, 384)

    def reduce_first(u):
        far, right, left = wrap(t + 2, 4), wrap(t + 1, 4), wrap(t - 1, 4)
        lo, hi = pl.ds(0, 32), pl.ds(32, 32)
        r1 = send(pb.at[u, far, lo], xr1.at[u, 0], x_dev(1))
        l1 = send(pb.at[u, far, hi], xr1.at[u, 1], x_dev(-1))
        r2 = send(pb.at[u, right, hi], xq.at[u, 0, hi], x_dev(1))
        l2 = send(pb.at[u, left, lo], xq.at[u, 1, lo], x_dev(-1))
        return r1, l1, r2, l2

    def reduce_second(u, copies):
        right, left = wrap(t + 1, 4), wrap(t - 1, 4)
        lo, hi = pl.ds(0, 32), pl.ds(32, 32)
        r1, l1, r2, l2 = copies
        r1.wait_recv()
        xs2[u, 0] = (pf[u, right, 0:32, :] + xr1[u, 0].astype(F32)).astype(BF16)
        r3 = send(xs2.at[u, 0], xq.at[u, 0, lo], x_dev(1))
        l1.wait_recv()
        xs2[u, 1] = (pf[u, left, 32:64, :] + xr1[u, 1].astype(F32)).astype(BF16)
        l3 = send(xs2.at[u, 1], xq.at[u, 1, hi], x_dev(-1))
        return r2, l2, r3, l3

    def reduce_third(u, copies):
        for copy in copies:
            copy.wait_recv()
        return pf[u, t] + xq[u, 0].astype(F32) + xq[u, 1].astype(F32)

    for copy in turned:
        copy.wait()
    for plane in range(4):
        gflat[plane] = gs[plane].astype(F32).reshape(64, D).astype(BF16)
    loads[3].wait()
    loads[4].wait()
    g_all = gflat[...].reshape(256, D)
    for n in range(3):
        c = slice(n * 384, n * 384 + 384)
        ga[:, c] = nn(g_all, w2[:, c])
    for copy in wo_swapped:
        copy.wait_recv()
    for plane in range(4):
        for j in range(8):
            slab = arec.at[plane, j]
            pltpu.make_async_copy(slab, slab, rsem.at[base_m + plane * 8 + j]).wait()

    proj = sum(nn(arec[plane].astype(F32).reshape(64, QC).astype(BF16), wo[plane]) for plane in range(4))
    mid_rows = (hres[...].astype(F32).reshape(64, D) + proj).astype(BF16)
    mid[...] = mid_rows
    x_hat2, inv_std2 = normalize(mid_rows.astype(F32))
    xhat[...] = x_hat2
    inv2[...] = inv_std2
    g2 = gain2[...].reshape(1, D)
    nb[t] = (x_hat2 * g2).astype(BF16)

    def quarter(ref):
        return lambda plane, a: ref.at[plane, pl.ds(a * 16, 16)]

    n_first = gather_first(quarter(nb), lambda a: quarter(nb)(t, a))

    for n in range(3):
        c = slice(n * 384, n * 384 + 384)
        lbuf[0, c, :] = nt(perm[c, :], g_all).astype(BF16)
    n_further = gather_second(quarter(nb), n_first)

    swapped = []
    kept = 1 - core
    root = (2.0 / np.pi) ** 0.5
    for part in range(2):
        if part:
            gather_third(n_further)
        pair = lax.rem(t // 2 + part, 2)
        rows = pl.ds(pl.multiple_of(pair * 128, 128), 128)
        nb_pair = nb[pl.ds(pair * 2, 2)].reshape(128, D)
        for n in range(3):
            c = slice(n * 384, n * 384 + 384)
            lbuf[1, c, rows] = nt(perm[c, :], nb_pair).astype(BF16)
        if part:
            swapped.append(send(lbuf.at[core], lbuf.at[2], core_dev))
        for n in range(3):
            c = slice(n * 384, n * 384 + 384)
            pre = nn(nb_pair, w1[:, c])
            square = pre * pre
            th = jnp.tanh(root * (pre + 0.044715 * (square * pre)))
            half = 0.5 * (1.0 + th)
            rbuf[0, rows, c] = (pre * half).astype(BF16)
            slope = half + 0.5 * pre * (1.0 - th * th) * (root * (1.0 + 3 * 0.044715 * square))
            rbuf[1, rows, c] = (ga[rows, c] * slope).astype(BF16)
            lanes = pl.ds(n * 384, 384)
            swapped.append(send(rbuf.at[core, rows, lanes], rbuf.at[2, rows, lanes], core_dev))

    partial_sums(0, lambda n: nt(rbuf[0], w2[n * 384 : n * 384 + 384, :]))
    d_first = reduce_first(0)
    for copy in swapped:
        copy.wait_recv()

    def grad_b(i, carry):
        rows = pl.ds(pl.multiple_of(i * 288, 32), 288)
        value = nn(lbuf[kept, rows, :], rbuf[kept, :, CA:]) + nn(lbuf[2, rows, :], rbuf[2, :, CA:])
        for m in range(2):
            for u in range(NB):
                wb[u, i * 2 + m] = value[m * 144 : (m + 1) * 144, u * 128 : (u + 1) * 128].astype(BF16)
        return carry

    def grad_a(i, carry):
        rows = pl.ds(pl.multiple_of(i * 288, 32), 288)
        value = nn(lbuf[kept, rows, :], rbuf[kept, :, :CA]) + nn(lbuf[2, rows, :], rbuf[2, :, :CA])
        for m in range(8):
            for u in range(2):
                part = value[m * SLAB : (m + 1) * SLAB, u * CA2 : (u + 1) * CA2]
                wa[u, m % 4, i * 2 + m // 4] = part.astype(BF16)
        return carry

    def add(a, b):
        return (a.astype(F32) + b.astype(F32)).astype(BF16)

    halves = (pl.ds(0, 80), pl.ds(80, 64))

    def b_first(u):
        far = wrap(zz + 4, 8)
        return [
            send(wb.at[u, far, halves[d]], zb1.at[u, d, halves[d]], z_dev(1 - 2 * d)) for d in range(2)
        ]

    def b_step(n, u, copies):
        result = []
        for d in range(2):
            sign = 1 - 2 * d
            chunk = wrap(zz + sign * (3 - n), 8)
            copies[d].wait_recv()
            if n == 0:
                taken, other = (slice(0, 80), slice(80, 144))[:: 1 - 2 * d]
                zbs[n, u, d, taken, :] = add(wb[u, chunk, taken, :], zb1[u, d, taken, :])
                zbs[n, u, d, other, :] = wb[u, chunk, other, :]
            else:
                zbs[n, u, d] = add(wb[u, chunk], zbq[n - 1, u, d])
            result.append(send(zbs.at[n, u, d], zbq.at[n, u, d], z_dev(sign)))
        return result

    def b_last(u, copies):
        for copy in copies:
            copy.wait_recv()
        total = wb[u, zz].astype(F32) + zbq[2, u, 0].astype(F32) + zbq[2, u, 1].astype(F32)
        for i in range(4):
            rb[u, i] = total[i * SLAB : (i + 1) * SLAB].astype(BF16)

    def a_first(u):
        far, up, down = wrap(y + 2, 4), wrap(y + 1, 4), wrap(y - 1, 4)
        lo, hi = pl.ds(0, 4), pl.ds(4, 4)
        u1 = send(wa.at[u, far, lo], ya1.at[u, 0], y_dev(1))
        d1 = send(wa.at[u, far, hi], ya1.at[u, 1], y_dev(-1))
        u2 = send(wa.at[u, up, hi], yaq.at[u, 0, hi], y_dev(1))
        d2 = send(wa.at[u, down, lo], yaq.at[u, 1, lo], y_dev(-1))
        return u1, d1, u2, d2

    def a_second(u, copies):
        up, down = wrap(y + 1, 4), wrap(y - 1, 4)
        u1, d1, u2, d2 = copies
        u1.wait_recv()

        def body_up(i, carry):
            yas[u, 0, i] = add(wa[u, up, i], ya1[u, 0, i])
            return carry

        lax.fori_loop(0, 4, body_up, 0)
        u3 = send(yas.at[u, 0], yaq.at[u, 0, pl.ds(0, 4)], y_dev(1))
        d1.wait_recv()

        def body_down(i, carry):
            yas[u, 1, i] = add(wa[u, down, i + 4], ya1[u, 1, i])
            return carry

        lax.fori_loop(0, 4, body_down, 0)
        d3 = send(yas.at[u, 1], yaq.at[u, 1, pl.ds(4, 4)], y_dev(-1))
        return u2, d2, u3, d3

    def a_last(u, copies):
        for copy in copies:
            copy.wait_recv()

        def body(i, carry):
            total = wa[u, y, i].astype(F32) + yaq[u, 0, i].astype(F32) + yaq[u, 1, i].astype(F32)
            ra[u, i] = total.astype(BF16)
            return carry

        lax.fori_loop(0, 8, body, 0)

    def straight(rows, received, dev_of, here, n):
        return [
            send(rows.at[wrap(here + step, n)], received.at[step - 1], dev_of(step)) for step in (n // 2, *range(1, n // 2), *range(n // 2 + 1, n))
        ]

    def straight_sum(rows, received, here, copies):
        for copy in copies:
            copy.wait_recv()
        total = rows[here].astype(F32)
        for i in range(len(copies)):
            total = total + received[i].astype(F32)
        return total

    lax.fori_loop(0, 4, grad_a, 0)
    a1 = [a_first(u) for u in range(2)]
    lax.fori_loop(0, 4, grad_b, 0)
    b1 = [b_first(u) for u in range(NB)]
    partial_sums(1, lambda n: nt(rbuf[1], w1[n * 384 : n * 384 + 384, :]))
    e_first = reduce_first(1)
    d_second = reduce_second(0, d_first)
    b2 = [b_step(0, u, b1[u]) for u in range(NB)]
    a2 = [a_second(0, a1[0])]
    e_second = reduce_second(1, e_first)
    a2.append(a_second(1, a1[1]))
    b3 = [b_step(1, u, b2[u]) for u in range(NB)]

    def out_view(ref):
        return lambda plane, a: ref.at[pl.ds(peer_seq(plane, a, 0), 2)]

    def give(rows, ref, base):
        for a in range(4):
            copy = pltpu.make_async_copy(rows.at[pl.ds(a * 2, 2)], out_view(ref)(t, a), osem.at[base + a])
            copy.start()
            placed.append(copy)
        return gather_first(out_view(ref), lambda a: rows.at[pl.ds(a * 2, 2)])

    placed = []
    down_rows = reduce_third(0, d_second)
    bo[...] = (mid[...].astype(F32) + down_rows).reshape(8, 8, D).astype(BF16)
    o_first = give(bo, out_b, 0)
    b4 = [b_step(2, u, b3[u]) for u in range(NB)]

    scaled = reduce_third(1, e_second) * g2
    x_hat2 = xhat[...]
    plain = jnp.mean(scaled, -1, keepdims=True)
    cross = jnp.mean(scaled * x_hat2, -1, keepdims=True)
    upstream = gs[t].astype(F32).reshape(64, D)
    go[...] = (upstream + inv2[...] * (scaled - plain - x_hat2 * cross)).reshape(8, 8, D).astype(BF16)
    m_first = give(go, out_g, 4)

    a3 = []
    for u in range(2):
        a_last(u, a2[u])
        a3.append(straight(ra.at[u], raq.at[u], z_dev, zz, 8))
    o_further = gather_second(out_view(out_b), o_first)
    b5 = []
    for u in range(NB):
        b_last(u, b4[u])
        b5.append(straight(rb.at[u], rbq.at[u], y_dev, y, 4))
    m_further = gather_second(out_view(out_g), m_first)
    sums = [
        *(((u * CA2, CA2), straight_sum(ra.at[u], raq.at[u], zz, a3[u])) for u in range(2)),
        *(((CA + u * 128, 128), straight_sum(rb.at[u], rbq.at[u], y, b5[u])) for u in range(NB)),
    ]
    for c in range(2):
        for (first, width), total in sums:
            fin[c, :, first : first + width] = total[c * 18 : c * 18 + 18]
    sf = fresh()

    def hand_over(src, dst):
        return pltpu.make_async_remote_copy(
            src_ref=src, dst_ref=dst, send_sem=ssem.at[sf], recv_sem=rsem.at[sf], device_id=core_dev, device_id_type=MESH
        )

    @pl.when(core == 0)
    def _():
        hand_over(fin.at[1], out_1).start()
        own = pltpu.make_async_copy(fin.at[0], out_1, asem)
        own.start()
        own.wait()
        hand_over(fin.at[1], out_2).wait()

    @pl.when(core == 1)
    def _():
        hand_over(fin.at[0], out_2).start()
        own = pltpu.make_async_copy(fin.at[1], out_2, asem)
        own.start()
        own.wait()
        hand_over(fin.at[0], out_1).wait()

    gather_third(o_further)
    gather_third(m_further)
    for copy in placed:
        copy.wait()

    for turn in turns:
        to_patches(turn).wait_send()
        to_frame(turn).wait_send()

    @pl.when(jnp.logical_not(stays))
    def _():
        to_frame(0).wait_send()

    for copy in started:
        copy.wait_send()


def place(*refs):
    sources, results, (buf_b, buf_g, buf_1, buf_2, sems) = refs[:4], refs[4:8], refs[8:]
    copies = []
    for src, dst, buf, parts in zip(sources, results, (buf_b, buf_g, buf_1, buf_2), (4, 4, 1, 1)):
        step = src.shape[0] // parts
        for i in range(parts):
            rows = pl.ds(i * step, step)
            n = len(copies)
            copies.append(
                (
                    pltpu.make_async_copy(src.at[rows], buf.at[rows], sems.at[0, n]),
                    pltpu.make_async_copy(buf.at[rows], dst.at[rows], sems.at[1, n]),
                )
            )
    for read, _ in copies:
        read.start()
    for read, write in copies:
        read.wait()
        write.start()
    for _, write in copies:
        write.wait()


def local(hidden_in, norm1_gain, qkv_weight, out_weight, norm2_gain, fc1_weight, fc2_weight, out_grad):
    anywhere = pl.BlockSpec(memory_space=pl.ANY)
    vmem = pl.BlockSpec(memory_space=pltpu.VMEM)
    shapes = [
        ((32, 8, D), BF16), ((4, 8, 8, D), BF16), ((8, 8, D), BF16),
        ((3 * QC, D), BF16), ((4, QC, D), BF16), ((D, FQ), BF16), ((D, FQ), BF16),
        ((4, 64, D), BF16), ((32, 8, 3 * QC), BF16), ((32, 8, 3 * QC), BF16),
        ((32, 8, QC), BF16), ((4, 8, 8, QC), BF16),
        ((4, 64, D), BF16), ((256, FQ), F32), ((4, 64, D), BF16),
        ((2, 4, 64, D), F32), ((2, 4, 64, D), BF16),
        ((2, 2, 32, D), BF16), ((2, 2, 32, D), BF16), ((2, 2, 64, D), BF16),
        ((64, D), BF16), ((64, D), F32), ((64, 1), F32), ((8, 8, D), BF16), ((8, 8, D), BF16),
        ((ROWS, D), BF16), ((3, ROWS, 256), BF16), ((3, 256, FQ), BF16),
        ((2, 4, 8, SLAB, CA2), BF16), ((2, 2, 4, SLAB, CA2), BF16), ((2, 2, 4, SLAB, CA2), BF16), ((2, 2, 8, SLAB, CA2), BF16),
        ((2, 8, SLAB, CA2), BF16), ((2, 7, SLAB, CA2), BF16),
        ((NB, 8, 144, 128), BF16), ((NB, 2, 144, 128), BF16), ((3, NB, 2, 144, 128), BF16), ((3, NB, 2, 144, 128), BF16),
        ((NB, 4, SLAB, 128), BF16), ((NB, 3, SLAB, 128), BF16),
        ((2, 18, FQ), F32),
    ]
    scratch = [pltpu.VMEM(shape, kind) for shape, kind in shapes]
    scratch += [
        pltpu.SemaphoreType.DMA((N_SEM,)), pltpu.SemaphoreType.DMA((N_SEM,)),
        pltpu.SemaphoreType.DMA((5,)), pltpu.SemaphoreType.DMA((20,)), pltpu.SemaphoreType.DMA((8,)),
        pltpu.SemaphoreType.DMA,
    ]
    results = [
        jax.ShapeDtypeStruct((32, 8, D), BF16),
        jax.ShapeDtypeStruct((32, 8, D), BF16),
        jax.ShapeDtypeStruct((18, FQ), F32),
        jax.ShapeDtypeStruct((18, FQ), F32),
    ]
    made = pl.pallas_call(
        kernel,
        out_shape=results,
        in_specs=[anywhere, vmem, anywhere, anywhere, vmem, anywhere, anywhere, anywhere],
        out_specs=[anywhere] * 4,
        scratch_shapes=scratch,
        compiler_params=pltpu.CompilerParams(
            collective_id=0, has_side_effects=True, vmem_limit_bytes=60 * 1024 * 1024
        ),
    )(
        hidden_in.reshape(32, 8, D),
        norm1_gain,
        qkv_weight.transpose(1, 2, 0).reshape(3 * QC, D),
        out_weight,
        norm2_gain,
        fc1_weight,
        fc2_weight,
        out_grad.reshape(32, 8, D),
    )
    block, grad_mid, grad_fc1, grad_fc2 = pl.pallas_call(
        place,
        out_shape=results,
        in_specs=[anywhere] * 4,
        out_specs=[anywhere] * 4,
        scratch_shapes=[pltpu.VMEM(made_one.shape, made_one.dtype) for made_one in results]
        + [pltpu.SemaphoreType.DMA((2, 10))],
        compiler_params=pltpu.CompilerParams(vmem_limit_bytes=60 * 1024 * 1024),
    )(*made)
    shape = hidden_in.shape
    return block.reshape(shape), grad_mid.reshape(shape), grad_fc1, grad_fc2


def solution(mesh):
    return jax.shard_map(
        local,
        mesh=mesh,
        in_specs=(
            P("dp", "seq", None, None),
            P(),
            P(None, None, "tensor"),
            P("tensor", None),
            P(),
            P(None, "tensor"),
            P(None, "tensor"),
            P("dp", "seq", None, None),
        ),
        out_specs=(
            P("dp", "seq", None, None),
            P("dp", "seq", None, None),
            P(("seq", "dp"), "tensor"),
            P(("seq", "dp"), "tensor"),
        ),
        check_vma=False,
    )
```

```python
import functools

import jax
import jax.numpy as jnp
import numpy as np
from jax import lax
from jax.experimental import pallas as pl
from jax.experimental.pallas import tpu as pltpu
from jax.sharding import PartitionSpec as P

MESH = pl.DeviceIdType.MESH
BF16 = jnp.bfloat16
F32 = jnp.float32

HDIM = 72
D = 1152
FQ = 1152
QC = 288
SLAB = 36
ROWS = 32 * SLAB
CA = 512
CB = 640
CA2 = CA // 2
NB = CB // 128
EPS = 1e-06
N_SEM = 224


def slab_sources(first, count):
    n = lax.broadcasted_iota(jnp.int32, (count, 1), 0) + first
    slab = (n * 1821) >> 16
    within = n - slab * SLAB
    core = jnp.where(within >= 18, 1, 0)
    z, y = slab >> 2, slab & 3
    return (((z >> 1) * 4 + y) * 2 + core) * 36 + (z & 1) * 18 + within - core * 18


def nn(a, b):
    return jnp.dot(a, b, preferred_element_type=F32)


def nt(a, b):
    return lax.dot_general(a, b, (((1,), (1,)), ((), ())), preferred_element_type=F32)


def normalize(values):
    center = values - jnp.mean(values, -1, keepdims=True)
    inv_std = lax.rsqrt(jnp.mean(center * center, -1, keepdims=True) + EPS)
    return center * inv_std, inv_std


def kernel(
    hid, gain1, wq_h, wo_h, gain2, w1_h, w2_h, og,
    out_b, out_g, out_1, out_2,
    hl, gs, hres, wq, wo, w1, w2, na, qkv, qrec, att, arec, gflat, ga, nb,
    pf, pb, xr1, xs2, xq, mid, xhat, inv2, bo, go,
    perm, lbuf, rbuf,
    wa, ya1, yas, yaq, ra, raq,
    wb, zb1, zbs, zbq, rb, rbq, fin,
    ssem, rsem, lsem, gsem, osem, asem,
):
    t = lax.axis_index("tensor")
    s = lax.axis_index("seq")
    dp = lax.axis_index("dp")
    zh = s // 8
    y = (s // 2) % 4
    core = s % 2
    zz = zh * 2 + dp

    def wrap(value, size):
        return (value + 2 * size) % size

    def x_dev(step):
        return {"tensor": wrap(t + step, 4)}

    def y_dev(step):
        return {"seq": zh * 8 + wrap(y + step, 4) * 2 + core}

    def z_dev(step):
        other = wrap(zz + step, 8)
        return {"seq": (other // 2) * 8 + y * 2 + core, "dp": other % 2}

    core_dev = {"seq": s + 1 - 2 * core}

    def peer_seq(plane, a, k):
        return a * 8 + wrap(plane - zh - y - a, 4) * 2 + k

    barrier = pltpu.get_barrier_semaphore()
    for dev in (x_dev(1), x_dev(-1), z_dev(1), z_dev(-1), z_dev(3), z_dev(-3)):
        pl.semaphore_signal(barrier, inc=1, device_id=dev, device_id_type=MESH)
    for other in range(32):
        pl.semaphore_signal(barrier, inc=1, device_id={"seq": other}, device_id_type=MESH)
    for step in range(1, 4):
        for a in range(4):
            for k in range(2):
                dev = {"seq": peer_seq(t, a, k), "tensor": wrap(t + step, 4)}
                pl.semaphore_signal(barrier, inc=1, device_id=dev, device_id_type=MESH)

    loads = [
        pltpu.make_async_copy(src, dst, lsem.at[i])
        for i, (src, dst) in enumerate(((hid, hl), (wq_h, wq), (wo_h, wo.at[t]), (w2_h, w2), (w1_h, w1)))
    ]
    for load in loads[:2]:
        load.start()

    g1 = gain1[...].reshape(1, D)
    loads[0].wait()

    def norm_rows(i, carry):
        x_hat, _ = normalize(hl[pl.ds(i * 8, 8)].astype(F32).reshape(64, D))
        na[i] = (x_hat * g1).astype(BF16)
        return carry

    lax.fori_loop(0, 4, norm_rows, 0)
    loads[1].wait()
    for load in loads[2:]:
        load.start()
    qkv[...] = nt(na[...].reshape(256, D), wq[...]).reshape(32, 8, 3 * QC).astype(BF16)
    pl.semaphore_wait(barrier, 62)

    count = [0]
    started = []

    def fresh(n=1):
        first = count[0]
        count[0] += n
        return first

    def send(src, dst, dev):
        i = fresh()
        copy = pltpu.make_async_remote_copy(
            src_ref=src, dst_ref=dst, send_sem=ssem.at[i], recv_sem=rsem.at[i], device_id=dev, device_id_type=MESH
        )
        copy.start()
        started.append(copy)
        return copy

    base_h, base_m = fresh(32), fresh(32)

    turns = (*range(16, 24), *range(8, 16), *range(24, 32), *range(1, 8))

    def to_patches(turn):
        other = lax.rem(s + turn, 32)
        return pltpu.make_async_remote_copy(
            src_ref=qkv.at[other], dst_ref=qrec.at[s], send_sem=ssem.at[base_h + turn], recv_sem=rsem.at[base_h + s],
            device_id={"seq": other}, device_id_type=MESH,
        )

    for turn in turns:
        to_patches(turn).start()
    pltpu.make_async_copy(qkv.at[s], qrec.at[s], rsem.at[base_h + s]).start()

    turned = [
        pltpu.make_async_copy(
            og.at[pl.ds(peer_seq(plane, a, 0), 2)], gs.at[plane, pl.ds(a * 2, 2)], gsem.at[plane * 4 + a]
        )
        for plane in range(4)
        for a in range(4)
    ] + [
        pltpu.make_async_copy(hid.at[pl.ds(peer_seq(t, a, 0), 2)], hres.at[pl.ds(a * 2, 2)], gsem.at[16 + a])
        for a in range(4)
    ]
    for copy in turned:
        copy.start()

    def gather_first(view, own):
        ups, downs = [None] * 4, [None] * 4
        for up, down in ((0, 2), (1, 3), (2, 0), (3, 1)):
            ups[up] = send(own(up), view(t, up), x_dev(1))
            downs[down] = send(own(down), view(t, down), x_dev(-1))
        return list(zip(ups, downs))

    def gather_second(view, copies):
        left, right = wrap(t - 1, 4), wrap(t + 1, 4)
        further = []
        for a in range(2):
            copies[a][0].wait_recv()
            further.append(send(view(left, a), view(left, a), x_dev(1)))
            copies[a + 2][1].wait_recv()
            further.append(send(view(right, a + 2), view(right, a + 2), x_dev(-1)))
        for a in range(2):
            copies[a + 2][0].wait_recv()
            copies[a][1].wait_recv()
        return further

    def gather_third(further):
        for copy in further:
            copy.wait_recv()

    def wo_part(plane, first, size):
        return wo.at[plane, pl.ds(pl.multiple_of(core * 144 + first, 16), size)]

    def wo_send(first, size):
        src = wo_part(t, first, size)
        return send(src, src, x_dev(1)), send(src, src, x_dev(-1))

    loads[2].wait()
    wo_first = wo_send(0, 144)

    def make_perm(i, carry):
        first = pl.multiple_of(i * 128, 128)
        wanted = slab_sources(first, 128)
        perm[pl.ds(first, 128), :] = jnp.where(
            lax.broadcasted_iota(jnp.int32, (128, D), 1) == wanted, 1.0, 0.0
        ).astype(BF16)
        return carry

    lax.fori_loop(0, ROWS // 128, make_perm, 0)

    wo_first[0].wait_recv()
    wo_first[1].wait_recv()
    left, right, far = wrap(t - 1, 4), wrap(t + 1, 4), wrap(t + 2, 4)
    wo_further = [
        send(wo_part(left, 0, 80), wo_part(left, 0, 80), x_dev(1)),
        send(wo_part(right, 80, 64), wo_part(right, 80, 64), x_dev(-1)),
    ]
    wo_swapped = [send(wo_part(plane, 0, 144), wo_part(plane, 0, 144), core_dev) for plane in (left, right)]

    for other in range(32):
        slab = qrec.at[other]
        pltpu.make_async_copy(slab, slab, rsem.at[base_h + other]).wait()
    q = qrec[:, :, 0:QC].reshape(256, QC)
    k_ = qrec[:, :, QC : 2 * QC].reshape(256, QC)
    v = qrec[:, :, 2 * QC : 3 * QC].reshape(256, QC)
    col = lax.broadcasted_iota(jnp.int32, (1, QC), 1)
    same = (lax.broadcasted_iota(jnp.int32, (256, 256), 0) & 7) == (lax.broadcasted_iota(jnp.int32, (256, 256), 1) & 7)
    total = jnp.zeros((256, QC), F32)
    for h in range(QC // HDIM):
        mine = (col >= h * HDIM) & (col < (h + 1) * HDIM)
        qh = jnp.where(mine, q, jnp.zeros_like(q))
        scores = nt(qh, k_) * HDIM ** (-0.5)
        scores = jnp.where(same, scores, -1e30)
        weights = jnp.exp(scores - jnp.max(scores, -1, keepdims=True))
        probs = (weights * (1.0 / jnp.sum(weights, -1, keepdims=True))).astype(BF16)
        total = jnp.where(mine, nn(probs, v), total)
    att[...] = total.reshape(32, 8, QC).astype(BF16)

    def plane_of(frame):
        return lax.rem(frame // 8 + frame // 2 % 4 + zh + y, 4)

    def to_frame(turn):
        frame = lax.rem(s + turn, 32)
        return pltpu.make_async_remote_copy(
            src_ref=att.at[frame], dst_ref=arec.at[t, zh * 2 + core],
            send_sem=ssem.at[base_m + turn], recv_sem=rsem.at[base_m + t * 8 + zh * 2 + core],
            device_id={"seq": frame, "tensor": plane_of(frame)}, device_id_type=MESH,
        )

    for turn in turns:
        to_frame(turn).start()
    stays = plane_of(s) == t

    @pl.when(jnp.logical_not(stays))
    def _():
        to_frame(0).start()

    @pl.when(stays)
    def _():
        here = arec.at[t, zh * 2 + core]
        pltpu.make_async_copy(att.at[s], here, rsem.at[base_m + t * 8 + zh * 2 + core]).start()

    for copy in wo_further:
        copy.wait_recv()
    wo_swapped.append(send(wo_part(far, 0, 144), wo_part(far, 0, 144), core_dev))

    def partial_sums(u, product):
        for n in range(3):
            value = product(n)
            pf[u, :, :, n * 384 : n * 384 + 384] = value.reshape(4, 64, 384)
            pb[u, :, :, n * 384 : n * 384 + 384] = value.astype(BF16).reshape(4, 64, 384)

    def reduce_first(u):
        far, right, left = wrap(t + 2, 4), wrap(t + 1, 4), wrap(t - 1, 4)
        lo, hi = pl.ds(0, 32), pl.ds(32, 32)
        r1 = send(pb.at[u, far, lo], xr1.at[u, 0], x_dev(1))
        l1 = send(pb.at[u, far, hi], xr1.at[u, 1], x_dev(-1))
        r2 = send(pb.at[u, right, hi], xq.at[u, 0, hi], x_dev(1))
        l2 = send(pb.at[u, left, lo], xq.at[u, 1, lo], x_dev(-1))
        return r1, l1, r2, l2

    def reduce_second(u, copies):
        right, left = wrap(t + 1, 4), wrap(t - 1, 4)
        lo, hi = pl.ds(0, 32), pl.ds(32, 32)
        r1, l1, r2, l2 = copies
        r1.wait_recv()
        xs2[u, 0] = (pf[u, right, 0:32, :] + xr1[u, 0].astype(F32)).astype(BF16)
        r3 = send(xs2.at[u, 0], xq.at[u, 0, lo], x_dev(1))
        l1.wait_recv()
        xs2[u, 1] = (pf[u, left, 32:64, :] + xr1[u, 1].astype(F32)).astype(BF16)
        l3 = send(xs2.at[u, 1], xq.at[u, 1, hi], x_dev(-1))
        return r2, l2, r3, l3

    def reduce_third(u, copies):
        for copy in copies:
            copy.wait_recv()
        return pf[u, t] + xq[u, 0].astype(F32) + xq[u, 1].astype(F32)

    for copy in turned:
        copy.wait()
    for plane in range(4):
        gflat[plane] = gs[plane].astype(F32).reshape(64, D).astype(BF16)
    loads[3].wait()
    loads[4].wait()
    g_all = gflat[...].reshape(256, D)
    for n in range(3):
        c = slice(n * 384, n * 384 + 384)
        ga[:, c] = nn(g_all, w2[:, c])
    for copy in wo_swapped:
        copy.wait_recv()
    for plane in range(4):
        for j in range(8):
            slab = arec.at[plane, j]
            pltpu.make_async_copy(slab, slab, rsem.at[base_m + plane * 8 + j]).wait()

    proj = sum(nn(arec[plane].astype(F32).reshape(64, QC).astype(BF16), wo[plane]) for plane in range(4))
    mid_rows = (hres[...].astype(F32).reshape(64, D) + proj).astype(BF16)
    mid[...] = mid_rows
    x_hat2, inv_std2 = normalize(mid_rows.astype(F32))
    xhat[...] = x_hat2
    inv2[...] = inv_std2
    g2 = gain2[...].reshape(1, D)
    nb[t] = (x_hat2 * g2).astype(BF16)

    def quarter(ref):
        return lambda plane, a: ref.at[plane, pl.ds(a * 16, 16)]

    n_first = gather_first(quarter(nb), lambda a: quarter(nb)(t, a))

    for n in range(3):
        c = slice(n * 384, n * 384 + 384)
        lbuf[0, c, :] = nt(perm[c, :], g_all).astype(BF16)
    n_further = gather_second(quarter(nb), n_first)

    swapped = []
    kept = 1 - core
    root = (2.0 / np.pi) ** 0.5
    for part in range(2):
        if part:
            gather_third(n_further)
        pair = lax.rem(t // 2 + part, 2)
        rows = pl.ds(pl.multiple_of(pair * 128, 128), 128)
        nb_pair = nb[pl.ds(pair * 2, 2)].reshape(128, D)
        for n in range(3):
            c = slice(n * 384, n * 384 + 384)
            lbuf[1, c, rows] = nt(perm[c, :], nb_pair).astype(BF16)
        if part:
            swapped.append(send(lbuf.at[core], lbuf.at[2], core_dev))
        for n in range(3):
            c = slice(n * 384, n * 384 + 384)
            pre = nn(nb_pair, w1[:, c])
            square = pre * pre
            th = jnp.tanh(root * (pre + 0.044715 * (square * pre)))
            half = 0.5 * (1.0 + th)
            rbuf[0, rows, c] = (pre * half).astype(BF16)
            slope = half + 0.5 * pre * (1.0 - th * th) * (root * (1.0 + 3 * 0.044715 * square))
            rbuf[1, rows, c] = (ga[rows, c] * slope).astype(BF16)
            lanes = pl.ds(n * 384, 384)
            swapped.append(send(rbuf.at[core, rows, lanes], rbuf.at[2, rows, lanes], core_dev))

    partial_sums(0, lambda n: nt(rbuf[0], w2[n * 384 : n * 384 + 384, :]))
    d_first = reduce_first(0)
    for copy in swapped:
        copy.wait_recv()

    def grad_b(i, carry):
        rows = pl.ds(pl.multiple_of(i * 288, 32), 288)
        value = nn(lbuf[kept, rows, :], rbuf[kept, :, CA:]) + nn(lbuf[2, rows, :], rbuf[2, :, CA:])
        for m in range(2):
            for u in range(NB):
                wb[u, i * 2 + m] = value[m * 144 : (m + 1) * 144, u * 128 : (u + 1) * 128].astype(BF16)
        return carry

    def grad_a(i, carry):
        rows = pl.ds(pl.multiple_of(i * 288, 32), 288)
        value = nn(lbuf[kept, rows, :], rbuf[kept, :, :CA]) + nn(lbuf[2, rows, :], rbuf[2, :, :CA])
        for m in range(8):
            for u in range(2):
                part = value[m * SLAB : (m + 1) * SLAB, u * CA2 : (u + 1) * CA2]
                wa[u, m % 4, i * 2 + m // 4] = part.astype(BF16)
        return carry

    def add(a, b):
        return (a.astype(F32) + b.astype(F32)).astype(BF16)

    halves = (pl.ds(0, 80), pl.ds(80, 64))

    def b_first(u):
        far = wrap(zz + 4, 8)
        return [
            send(wb.at[u, far, halves[d]], zb1.at[u, d, halves[d]], z_dev(1 - 2 * d)) for d in range(2)
        ]

    def b_step(n, u, copies):
        result = []
        for d in range(2):
            sign = 1 - 2 * d
            chunk = wrap(zz + sign * (3 - n), 8)
            copies[d].wait_recv()
            if n == 0:
                taken, other = (slice(0, 80), slice(80, 144))[:: 1 - 2 * d]
                zbs[n, u, d, taken, :] = add(wb[u, chunk, taken, :], zb1[u, d, taken, :])
                zbs[n, u, d, other, :] = wb[u, chunk, other, :]
            else:
                zbs[n, u, d] = add(wb[u, chunk], zbq[n - 1, u, d])
            result.append(send(zbs.at[n, u, d], zbq.at[n, u, d], z_dev(sign)))
        return result

    def b_last(u, copies):
        for copy in copies:
            copy.wait_recv()
        total = wb[u, zz].astype(F32) + zbq[2, u, 0].astype(F32) + zbq[2, u, 1].astype(F32)
        for i in range(4):
            rb[u, i] = total[i * SLAB : (i + 1) * SLAB].astype(BF16)

    def a_first(u):
        far, up, down = wrap(y + 2, 4), wrap(y + 1, 4), wrap(y - 1, 4)
        lo, hi = pl.ds(0, 4), pl.ds(4, 4)
        u1 = send(wa.at[u, far, lo], ya1.at[u, 0], y_dev(1))
        d1 = send(wa.at[u, far, hi], ya1.at[u, 1], y_dev(-1))
        u2 = send(wa.at[u, up, hi], yaq.at[u, 0, hi], y_dev(1))
        d2 = send(wa.at[u, down, lo], yaq.at[u, 1, lo], y_dev(-1))
        return u1, d1, u2, d2

    def a_second(u, copies):
        up, down = wrap(y + 1, 4), wrap(y - 1, 4)
        u1, d1, u2, d2 = copies
        u1.wait_recv()

        def body_up(i, carry):
            yas[u, 0, i] = add(wa[u, up, i], ya1[u, 0, i])
            return carry

        lax.fori_loop(0, 4, body_up, 0)
        u3 = send(yas.at[u, 0], yaq.at[u, 0, pl.ds(0, 4)], y_dev(1))
        d1.wait_recv()

        def body_down(i, carry):
            yas[u, 1, i] = add(wa[u, down, i + 4], ya1[u, 1, i])
            return carry

        lax.fori_loop(0, 4, body_down, 0)
        d3 = send(yas.at[u, 1], yaq.at[u, 1, pl.ds(4, 4)], y_dev(-1))
        return u2, d2, u3, d3

    def a_last(u, copies):
        for copy in copies:
            copy.wait_recv()

        def body(i, carry):
            total = wa[u, y, i].astype(F32) + yaq[u, 0, i].astype(F32) + yaq[u, 1, i].astype(F32)
            ra[u, i] = total.astype(BF16)
            return carry

        lax.fori_loop(0, 8, body, 0)

    def straight(rows, received, dev_of, here, n):
        return [
            send(rows.at[wrap(here + step, n)], received.at[step - 1], dev_of(step)) for step in (n // 2, *range(1, n // 2), *range(n // 2 + 1, n))
        ]

    def straight_sum(rows, received, here, copies):
        for copy in copies:
            copy.wait_recv()
        total = rows[here].astype(F32)
        for i in range(len(copies)):
            total = total + received[i].astype(F32)
        return total

    lax.fori_loop(0, 4, grad_b, 0)
    b1 = [b_first(u) for u in range(NB)]
    lax.fori_loop(0, 4, grad_a, 0)
    a1 = [a_first(u) for u in range(2)]
    partial_sums(1, lambda n: nt(rbuf[1], w1[n * 384 : n * 384 + 384, :]))
    e_first = reduce_first(1)
    d_second = reduce_second(0, d_first)
    b2 = [b_step(0, u, b1[u]) for u in range(NB)]
    a2 = [a_second(0, a1[0])]
    e_second = reduce_second(1, e_first)
    a2.append(a_second(1, a1[1]))
    b3 = [b_step(1, u, b2[u]) for u in range(NB)]

    def out_view(ref):
        return lambda plane, a: ref.at[pl.ds(peer_seq(plane, a, 0), 2)]

    def give(rows, ref, base):
        for a in range(4):
            copy = pltpu.make_async_copy(rows.at[pl.ds(a * 2, 2)], out_view(ref)(t, a), osem.at[base + a])
            copy.start()
            placed.append(copy)
        return gather_first(out_view(ref), lambda a: rows.at[pl.ds(a * 2, 2)])

    placed = []
    down_rows = reduce_third(0, d_second)
    bo[...] = (mid[...].astype(F32) + down_rows).reshape(8, 8, D).astype(BF16)
    o_first = give(bo, out_b, 0)
    b4 = [b_step(2, u, b3[u]) for u in range(NB)]

    scaled = reduce_third(1, e_second) * g2
    x_hat2 = xhat[...]
    plain = jnp.mean(scaled, -1, keepdims=True)
    cross = jnp.mean(scaled * x_hat2, -1, keepdims=True)
    upstream = gs[t].astype(F32).reshape(64, D)
    go[...] = (upstream + inv2[...] * (scaled - plain - x_hat2 * cross)).reshape(8, 8, D).astype(BF16)
    m_first = give(go, out_g, 4)

    a3 = []
    for u in range(2):
        a_last(u, a2[u])
        a3.append(straight(ra.at[u], raq.at[u], z_dev, zz, 8))
    o_further = gather_second(out_view(out_b), o_first)
    b5 = []
    for u in range(NB):
        b_last(u, b4[u])
        b5.append(straight(rb.at[u], rbq.at[u], y_dev, y, 4))
    m_further = gather_second(out_view(out_g), m_first)
    sums = [
        *(((u * CA2, CA2), straight_sum(ra.at[u], raq.at[u], zz, a3[u])) for u in range(2)),
        *(((CA + u * 128, 128), straight_sum(rb.at[u], rbq.at[u], y, b5[u])) for u in range(NB)),
    ]
    for c in range(2):
        for (first, width), total in sums:
            fin[c, :, first : first + width] = total[c * 18 : c * 18 + 18]
    sf = fresh()

    def hand_over(src, dst):
        return pltpu.make_async_remote_copy(
            src_ref=src, dst_ref=dst, send_sem=ssem.at[sf], recv_sem=rsem.at[sf], device_id=core_dev, device_id_type=MESH
        )

    @pl.when(core == 0)
    def _():
        hand_over(fin.at[1], out_1).start()
        own = pltpu.make_async_copy(fin.at[0], out_1, asem)
        own.start()
        own.wait()
        hand_over(fin.at[1], out_2).wait()

    @pl.when(core == 1)
    def _():
        hand_over(fin.at[0], out_2).start()
        own = pltpu.make_async_copy(fin.at[1], out_2, asem)
        own.start()
        own.wait()
        hand_over(fin.at[0], out_1).wait()

    gather_third(o_further)
    gather_third(m_further)
    for copy in placed:
        copy.wait()

    for turn in turns:
        to_patches(turn).wait_send()
        to_frame(turn).wait_send()

    @pl.when(jnp.logical_not(stays))
    def _():
        to_frame(0).wait_send()

    for copy in started:
        copy.wait_send()


def place(*refs):
    sources, results, (buf_b, buf_g, buf_1, buf_2, sems) = refs[:4], refs[4:8], refs[8:]
    copies = []
    for src, dst, buf, parts in zip(sources, results, (buf_b, buf_g, buf_1, buf_2), (4, 4, 1, 1)):
        step = src.shape[0] // parts
        for i in range(parts):
            rows = pl.ds(i * step, step)
            n = len(copies)
            copies.append(
                (
                    pltpu.make_async_copy(src.at[rows], buf.at[rows], sems.at[0, n]),
                    pltpu.make_async_copy(buf.at[rows], dst.at[rows], sems.at[1, n]),
                )
            )
    for read, _ in copies:
        read.start()
    for read, write in copies:
        read.wait()
        write.start()
    for _, write in copies:
        write.wait()


def local(hidden_in, norm1_gain, qkv_weight, out_weight, norm2_gain, fc1_weight, fc2_weight, out_grad):
    anywhere = pl.BlockSpec(memory_space=pl.ANY)
    vmem = pl.BlockSpec(memory_space=pltpu.VMEM)
    shapes = [
        ((32, 8, D), BF16), ((4, 8, 8, D), BF16), ((8, 8, D), BF16),
        ((3 * QC, D), BF16), ((4, QC, D), BF16), ((D, FQ), BF16), ((D, FQ), BF16),
        ((4, 64, D), BF16), ((32, 8, 3 * QC), BF16), ((32, 8, 3 * QC), BF16),
        ((32, 8, QC), BF16), ((4, 8, 8, QC), BF16),
        ((4, 64, D), BF16), ((256, FQ), F32), ((4, 64, D), BF16),
        ((2, 4, 64, D), F32), ((2, 4, 64, D), BF16),
        ((2, 2, 32, D), BF16), ((2, 2, 32, D), BF16), ((2, 2, 64, D), BF16),
        ((64, D), BF16), ((64, D), F32), ((64, 1), F32), ((8, 8, D), BF16), ((8, 8, D), BF16),
        ((ROWS, D), BF16), ((3, ROWS, 256), BF16), ((3, 256, FQ), BF16),
        ((2, 4, 8, SLAB, CA2), BF16), ((2, 2, 4, SLAB, CA2), BF16), ((2, 2, 4, SLAB, CA2), BF16), ((2, 2, 8, SLAB, CA2), BF16),
        ((2, 8, SLAB, CA2), BF16), ((2, 7, SLAB, CA2), BF16),
        ((NB, 8, 144, 128), BF16), ((NB, 2, 144, 128), BF16), ((3, NB, 2, 144, 128), BF16), ((3, NB, 2, 144, 128), BF16),
        ((NB, 4, SLAB, 128), BF16), ((NB, 3, SLAB, 128), BF16),
        ((2, 18, FQ), F32),
    ]
    scratch = [pltpu.VMEM(shape, kind) for shape, kind in shapes]
    scratch += [
        pltpu.SemaphoreType.DMA((N_SEM,)), pltpu.SemaphoreType.DMA((N_SEM,)),
        pltpu.SemaphoreType.DMA((5,)), pltpu.SemaphoreType.DMA((20,)), pltpu.SemaphoreType.DMA((8,)),
        pltpu.SemaphoreType.DMA,
    ]
    results = [
        jax.ShapeDtypeStruct((32, 8, D), BF16),
        jax.ShapeDtypeStruct((32, 8, D), BF16),
        jax.ShapeDtypeStruct((18, FQ), F32),
        jax.ShapeDtypeStruct((18, FQ), F32),
    ]
    made = pl.pallas_call(
        kernel,
        out_shape=results,
        in_specs=[anywhere, vmem, anywhere, anywhere, vmem, anywhere, anywhere, anywhere],
        out_specs=[anywhere] * 4,
        scratch_shapes=scratch,
        compiler_params=pltpu.CompilerParams(
            collective_id=0, has_side_effects=True, vmem_limit_bytes=60 * 1024 * 1024
        ),
    )(
        hidden_in.reshape(32, 8, D),
        norm1_gain,
        qkv_weight.transpose(1, 2, 0).reshape(3 * QC, D),
        out_weight,
        norm2_gain,
        fc1_weight,
        fc2_weight,
        out_grad.reshape(32, 8, D),
    )
    block, grad_mid, grad_fc1, grad_fc2 = pl.pallas_call(
        place,
        out_shape=results,
        in_specs=[anywhere] * 4,
        out_specs=[anywhere] * 4,
        scratch_shapes=[pltpu.VMEM(made_one.shape, made_one.dtype) for made_one in results]
        + [pltpu.SemaphoreType.DMA((2, 10))],
        compiler_params=pltpu.CompilerParams(vmem_limit_bytes=60 * 1024 * 1024),
    )(*made)
    shape = hidden_in.shape
    return block.reshape(shape), grad_mid.reshape(shape), grad_fc1, grad_fc2


def solution(mesh):
    return jax.shard_map(
        local,
        mesh=mesh,
        in_specs=(
            P("dp", "seq", None, None),
            P(),
            P(None, None, "tensor"),
            P("tensor", None),
            P(),
            P(None, "tensor"),
            P(None, "tensor"),
            P("dp", "seq", None, None),
        ),
        out_specs=(
            P("dp", "seq", None, None),
            P("dp", "seq", None, None),
            P(("seq", "dp"), "tensor"),
            P(("seq", "dp"), "tensor"),
        ),
        check_vma=False,
    )
```

```python
import functools

import jax
import jax.numpy as jnp
import numpy as np
from jax import lax
from jax.experimental import pallas as pl
from jax.experimental.pallas import tpu as pltpu
from jax.sharding import PartitionSpec as P

MESH = pl.DeviceIdType.MESH
BF16 = jnp.bfloat16
F32 = jnp.float32

HDIM = 72
D = 1152
FQ = 1152
QC = 288
SLAB = 36
ROWS = 32 * SLAB
CA = 512
CB = 640
CA2 = CA // 2
NB = CB // 128
EPS = 1e-06
N_SEM = 224


def slab_sources(first, count):
    n = lax.broadcasted_iota(jnp.int32, (count, 1), 0) + first
    slab = (n * 1821) >> 16
    within = n - slab * SLAB
    core = jnp.where(within >= 18, 1, 0)
    z, y = slab >> 2, slab & 3
    return (((z >> 1) * 4 + y) * 2 + core) * 36 + (z & 1) * 18 + within - core * 18


def nn(a, b):
    return jnp.dot(a, b, preferred_element_type=F32)


def nt(a, b):
    return lax.dot_general(a, b, (((1,), (1,)), ((), ())), preferred_element_type=F32)


def normalize(values):
    center = values - jnp.mean(values, -1, keepdims=True)
    inv_std = lax.rsqrt(jnp.mean(center * center, -1, keepdims=True) + EPS)
    return center * inv_std, inv_std


def kernel(
    hid, gain1, wq_h, wo_h, gain2, w1_h, w2_h, og,
    out_b, out_g, out_1, out_2,
    hl, gs, hres, wq, wo, w1, w2, na, qkv, qrec, att, arec, gflat, ga, nb,
    pf, pb, xr1, xs2, xq, mid, xhat, inv2, bo, go,
    perm, lbuf, rbuf,
    wa, ya1, yas, yaq, ra, raq,
    wb, zb1, zbs, zbq, rb, rbq, fin,
    ssem, rsem, lsem, gsem, osem, asem,
):
    t = lax.axis_index("tensor")
    s = lax.axis_index("seq")
    dp = lax.axis_index("dp")
    zh = s // 8
    y = (s // 2) % 4
    core = s % 2
    zz = zh * 2 + dp

    def wrap(value, size):
        return (value + 2 * size) % size

    def x_dev(step):
        return {"tensor": wrap(t + step, 4)}

    def y_dev(step):
        return {"seq": zh * 8 + wrap(y + step, 4) * 2 + core}

    def z_dev(step):
        other = wrap(zz + step, 8)
        return {"seq": (other // 2) * 8 + y * 2 + core, "dp": other % 2}

    core_dev = {"seq": s + 1 - 2 * core}

    def peer_seq(plane, a, k):
        return a * 8 + wrap(plane - zh - y - a, 4) * 2 + k

    barrier = pltpu.get_barrier_semaphore()
    for dev in (x_dev(1), x_dev(-1), z_dev(1), z_dev(-1), z_dev(3), z_dev(-3)):
        pl.semaphore_signal(barrier, inc=1, device_id=dev, device_id_type=MESH)
    for other in range(32):
        pl.semaphore_signal(barrier, inc=1, device_id={"seq": other}, device_id_type=MESH)
    for step in range(1, 4):
        for a in range(4):
            for k in range(2):
                dev = {"seq": peer_seq(t, a, k), "tensor": wrap(t + step, 4)}
                pl.semaphore_signal(barrier, inc=1, device_id=dev, device_id_type=MESH)

    loads = [
        pltpu.make_async_copy(src, dst, lsem.at[i])
        for i, (src, dst) in enumerate(((hid, hl), (wq_h, wq), (wo_h, wo.at[t]), (w2_h, w2), (w1_h, w1)))
    ]
    for load in loads[:2]:
        load.start()

    g1 = gain1[...].reshape(1, D)
    loads[0].wait()

    def norm_rows(i, carry):
        x_hat, _ = normalize(hl[pl.ds(i * 8, 8)].astype(F32).reshape(64, D))
        na[i] = (x_hat * g1).astype(BF16)
        return carry

    lax.fori_loop(0, 4, norm_rows, 0)
    loads[1].wait()
    for load in loads[2:]:
        load.start()
    qkv[...] = nt(na[...].reshape(256, D), wq[...]).reshape(32, 8, 3 * QC).astype(BF16)
    pl.semaphore_wait(barrier, 62)

    count = [0]
    started = []

    def fresh(n=1):
        first = count[0]
        count[0] += n
        return first

    def send(src, dst, dev):
        i = fresh()
        copy = pltpu.make_async_remote_copy(
            src_ref=src, dst_ref=dst, send_sem=ssem.at[i], recv_sem=rsem.at[i], device_id=dev, device_id_type=MESH
        )
        copy.start()
        started.append(copy)
        return copy

    base_h, base_m = fresh(32), fresh(32)

    turns = (*range(16, 24), *range(8, 16), *range(24, 32), *range(1, 8))

    def to_patches(turn):
        other = lax.rem(s + turn, 32)
        return pltpu.make_async_remote_copy(
            src_ref=qkv.at[other], dst_ref=qrec.at[s], send_sem=ssem.at[base_h + turn], recv_sem=rsem.at[base_h + s],
            device_id={"seq": other}, device_id_type=MESH,
        )

    for turn in turns:
        to_patches(turn).start()
    pltpu.make_async_copy(qkv.at[s], qrec.at[s], rsem.at[base_h + s]).start()

    turned = [
        pltpu.make_async_copy(
            og.at[pl.ds(peer_seq(plane, a, 0), 2)], gs.at[plane, pl.ds(a * 2, 2)], gsem.at[plane * 4 + a]
        )
        for plane in range(4)
        for a in range(4)
    ] + [
        pltpu.make_async_copy(hid.at[pl.ds(peer_seq(t, a, 0), 2)], hres.at[pl.ds(a * 2, 2)], gsem.at[16 + a])
        for a in range(4)
    ]
    for copy in turned:
        copy.start()

    def gather_first(view, own):
        ups, downs = [None] * 4, [None] * 4
        for up, down in ((0, 2), (1, 3), (2, 0), (3, 1)):
            ups[up] = send(own(up), view(t, up), x_dev(1))
            downs[down] = send(own(down), view(t, down), x_dev(-1))
        return list(zip(ups, downs))

    def gather_second(view, copies):
        left, right = wrap(t - 1, 4), wrap(t + 1, 4)
        further = []
        for a in range(2):
            copies[a][0].wait_recv()
            further.append(send(view(left, a), view(left, a), x_dev(1)))
            copies[a + 2][1].wait_recv()
            further.append(send(view(right, a + 2), view(right, a + 2), x_dev(-1)))
        for a in range(2):
            copies[a + 2][0].wait_recv()
            copies[a][1].wait_recv()
        return further

    def gather_third(further):
        for copy in further:
            copy.wait_recv()

    def wo_part(plane, first, size):
        return wo.at[plane, pl.ds(pl.multiple_of(core * 144 + first, 16), size)]

    def wo_send(first, size):
        src = wo_part(t, first, size)
        return send(src, src, x_dev(1)), send(src, src, x_dev(-1))

    loads[2].wait()
    wo_first = wo_send(0, 144)

    def make_perm(i, carry):
        first = pl.multiple_of(i * 128, 128)
        wanted = slab_sources(first, 128)
        perm[pl.ds(first, 128), :] = jnp.where(
            lax.broadcasted_iota(jnp.int32, (128, D), 1) == wanted, 1.0, 0.0
        ).astype(BF16)
        return carry

    lax.fori_loop(0, ROWS // 128, make_perm, 0)

    wo_first[0].wait_recv()
    wo_first[1].wait_recv()
    left, right, far = wrap(t - 1, 4), wrap(t + 1, 4), wrap(t + 2, 4)
    wo_further = [
        send(wo_part(left, 0, 80), wo_part(left, 0, 80), x_dev(1)),
        send(wo_part(right, 80, 64), wo_part(right, 80, 64), x_dev(-1)),
    ]
    wo_swapped = [send(wo_part(plane, 0, 144), wo_part(plane, 0, 144), core_dev) for plane in (left, right)]

    for other in range(32):
        slab = qrec.at[other]
        pltpu.make_async_copy(slab, slab, rsem.at[base_h + other]).wait()
    q = qrec[:, :, 0:QC].reshape(256, QC)
    k_ = qrec[:, :, QC : 2 * QC].reshape(256, QC)
    v = qrec[:, :, 2 * QC : 3 * QC].reshape(256, QC)
    col = lax.broadcasted_iota(jnp.int32, (1, QC), 1)
    same = (lax.broadcasted_iota(jnp.int32, (256, 256), 0) & 7) == (lax.broadcasted_iota(jnp.int32, (256, 256), 1) & 7)
    total = jnp.zeros((256, QC), F32)
    for h in range(QC // HDIM):
        mine = (col >= h * HDIM) & (col < (h + 1) * HDIM)
        qh = jnp.where(mine, q, jnp.zeros_like(q))
        scores = nt(qh, k_) * HDIM ** (-0.5)
        scores = jnp.where(same, scores, -1e30)
        weights = jnp.exp(scores - jnp.max(scores, -1, keepdims=True))
        probs = (weights * (1.0 / jnp.sum(weights, -1, keepdims=True))).astype(BF16)
        total = jnp.where(mine, nn(probs, v), total)
    att[...] = total.reshape(32, 8, QC).astype(BF16)

    def plane_of(frame):
        return lax.rem(frame // 8 + frame // 2 % 4 + zh + y, 4)

    def to_frame(turn):
        frame = lax.rem(s + turn, 32)
        return pltpu.make_async_remote_copy(
            src_ref=att.at[frame], dst_ref=arec.at[t, zh * 2 + core],
            send_sem=ssem.at[base_m + turn], recv_sem=rsem.at[base_m + t * 8 + zh * 2 + core],
            device_id={"seq": frame, "tensor": plane_of(frame)}, device_id_type=MESH,
        )

    for turn in turns:
        to_frame(turn).start()
    stays = plane_of(s) == t

    @pl.when(jnp.logical_not(stays))
    def _():
        to_frame(0).start()

    @pl.when(stays)
    def _():
        here = arec.at[t, zh * 2 + core]
        pltpu.make_async_copy(att.at[s], here, rsem.at[base_m + t * 8 + zh * 2 + core]).start()

    for copy in wo_further:
        copy.wait_recv()
    wo_swapped.append(send(wo_part(far, 0, 144), wo_part(far, 0, 144), core_dev))

    def partial_sums(u, product):
        for n in range(3):
            value = product(n)
            pf[u, :, :, n * 384 : n * 384 + 384] = value.reshape(4, 64, 384)
            pb[u, :, :, n * 384 : n * 384 + 384] = value.astype(BF16).reshape(4, 64, 384)

    def reduce_first(u):
        far, right, left = wrap(t + 2, 4), wrap(t + 1, 4), wrap(t - 1, 4)
        lo, hi = pl.ds(0, 32), pl.ds(32, 32)
        r1 = send(pb.at[u, far, lo], xr1.at[u, 0], x_dev(1))
        l1 = send(pb.at[u, far, hi], xr1.at[u, 1], x_dev(-1))
        r2 = send(pb.at[u, right, hi], xq.at[u, 0, hi], x_dev(1))
        l2 = send(pb.at[u, left, lo], xq.at[u, 1, lo], x_dev(-1))
        return r1, l1, r2, l2

    def reduce_second(u, copies):
        right, left = wrap(t + 1, 4), wrap(t - 1, 4)
        lo, hi = pl.ds(0, 32), pl.ds(32, 32)
        r1, l1, r2, l2 = copies
        r1.wait_recv()
        xs2[u, 0] = (pf[u, right, 0:32, :] + xr1[u, 0].astype(F32)).astype(BF16)
        r3 = send(xs2.at[u, 0], xq.at[u, 0, lo], x_dev(1))
        l1.wait_recv()
        xs2[u, 1] = (pf[u, left, 32:64, :] + xr1[u, 1].astype(F32)).astype(BF16)
        l3 = send(xs2.at[u, 1], xq.at[u, 1, hi], x_dev(-1))
        return r2, l2, r3, l3

    def reduce_third(u, copies):
        for copy in copies:
            copy.wait_recv()
        return pf[u, t] + xq[u, 0].astype(F32) + xq[u, 1].astype(F32)

    for copy in turned:
        copy.wait()
    for plane in range(4):
        gflat[plane] = gs[plane].astype(F32).reshape(64, D).astype(BF16)
    loads[3].wait()
    loads[4].wait()
    g_all = gflat[...].reshape(256, D)
    for n in range(3):
        c = slice(n * 384, n * 384 + 384)
        ga[:, c] = nn(g_all, w2[:, c])
    for copy in wo_swapped:
        copy.wait_recv()
    for plane in range(4):
        for j in range(8):
            slab = arec.at[plane, j]
            pltpu.make_async_copy(slab, slab, rsem.at[base_m + plane * 8 + j]).wait()

    proj = sum(nn(arec[plane].astype(F32).reshape(64, QC).astype(BF16), wo[plane]) for plane in range(4))
    mid_rows = (hres[...].astype(F32).reshape(64, D) + proj).astype(BF16)
    mid[...] = mid_rows
    x_hat2, inv_std2 = normalize(mid_rows.astype(F32))
    xhat[...] = x_hat2
    inv2[...] = inv_std2
    g2 = gain2[...].reshape(1, D)
    nb[t] = (x_hat2 * g2).astype(BF16)

    def quarter(ref):
        return lambda plane, a: ref.at[plane, pl.ds(a * 16, 16)]

    n_first = gather_first(quarter(nb), lambda a: quarter(nb)(t, a))

    for n in range(3):
        c = slice(n * 384, n * 384 + 384)
        lbuf[0, c, :] = nt(perm[c, :], g_all).astype(BF16)
    n_further = gather_second(quarter(nb), n_first)

    swapped = []
    kept = 1 - core
    root = (2.0 / np.pi) ** 0.5
    for part in range(2):
        if part:
            gather_third(n_further)
        pair = lax.rem(t // 2 + part, 2)
        rows = pl.ds(pl.multiple_of(pair * 128, 128), 128)
        nb_pair = nb[pl.ds(pair * 2, 2)].reshape(128, D)
        for n in range(3):
            c = slice(n * 384, n * 384 + 384)
            lbuf[1, c, rows] = nt(perm[c, :], nb_pair).astype(BF16)
        if part:
            swapped.append(send(lbuf.at[core], lbuf.at[2], core_dev))
        for n in range(3):
            c = slice(n * 384, n * 384 + 384)
            pre = nn(nb_pair, w1[:, c])
            square = pre * pre
            th = jnp.tanh(root * (pre + 0.044715 * (square * pre)))
            half = 0.5 * (1.0 + th)
            rbuf[0, rows, c] = (pre * half).astype(BF16)
            slope = half + 0.5 * pre * (1.0 - th * th) * (root * (1.0 + 3 * 0.044715 * square))
            rbuf[1, rows, c] = (ga[rows, c] * slope).astype(BF16)
            lanes = pl.ds(n * 384, 384)
            swapped.append(send(rbuf.at[core, rows, lanes], rbuf.at[2, rows, lanes], core_dev))

    partial_sums(0, lambda n: nt(rbuf[0], w2[n * 384 : n * 384 + 384, :]))
    d_first = reduce_first(0)
    for copy in swapped:
        copy.wait_recv()

    def grad_b(i, carry):
        rows = pl.ds(pl.multiple_of(i * 288, 32), 288)
        value = nn(lbuf[kept, rows, :], rbuf[kept, :, CA:]) + nn(lbuf[2, rows, :], rbuf[2, :, CA:])
        for m in range(2):
            for u in range(NB):
                wb[u, i * 2 + m] = value[m * 144 : (m + 1) * 144, u * 128 : (u + 1) * 128].astype(BF16)
        return carry

    def grad_a(i, carry):
        rows = pl.ds(pl.multiple_of(i * 288, 32), 288)
        value = nn(lbuf[kept, rows, :], rbuf[kept, :, :CA]) + nn(lbuf[2, rows, :], rbuf[2, :, :CA])
        for m in range(8):
            for u in range(2):
                part = value[m * SLAB : (m + 1) * SLAB, u * CA2 : (u + 1) * CA2]
                wa[u, m % 4, i * 2 + m // 4] = part.astype(BF16)
        return carry

    def add(a, b):
        return (a.astype(F32) + b.astype(F32)).astype(BF16)

    halves = (pl.ds(0, 80), pl.ds(80, 64))

    def b_first(u):
        far = wrap(zz + 4, 8)
        return [
            send(wb.at[u, far, halves[d]], zb1.at[u, d, halves[d]], z_dev(1 - 2 * d)) for d in range(2)
        ]

    def b_step(n, u, copies):
        result = []
        for d in range(2):
            sign = 1 - 2 * d
            chunk = wrap(zz + sign * (3 - n), 8)
            copies[d].wait_recv()
            if n == 0:
                taken, other = (slice(0, 80), slice(80, 144))[:: 1 - 2 * d]
                zbs[n, u, d, taken, :] = add(wb[u, chunk, taken, :], zb1[u, d, taken, :])
                zbs[n, u, d, other, :] = wb[u, chunk, other, :]
            else:
                zbs[n, u, d] = add(wb[u, chunk], zbq[n - 1, u, d])
            result.append(send(zbs.at[n, u, d], zbq.at[n, u, d], z_dev(sign)))
        return result

    def b_last(u, copies):
        for copy in copies:
            copy.wait_recv()
        total = wb[u, zz].astype(F32) + zbq[2, u, 0].astype(F32) + zbq[2, u, 1].astype(F32)
        for i in range(4):
            rb[u, i] = total[i * SLAB : (i + 1) * SLAB].astype(BF16)

    def a_first(u):
        far, up, down = wrap(y + 2, 4), wrap(y + 1, 4), wrap(y - 1, 4)
        lo, hi = pl.ds(0, 4), pl.ds(4, 4)
        u1 = send(wa.at[u, far, lo], ya1.at[u, 0], y_dev(1))
        d1 = send(wa.at[u, far, hi], ya1.at[u, 1], y_dev(-1))
        u2 = send(wa.at[u, up, hi], yaq.at[u, 0, hi], y_dev(1))
        d2 = send(wa.at[u, down, lo], yaq.at[u, 1, lo], y_dev(-1))
        return u1, d1, u2, d2

    def a_second(u, copies):
        up, down = wrap(y + 1, 4), wrap(y - 1, 4)
        u1, d1, u2, d2 = copies
        u1.wait_recv()

        def body_up(i, carry):
            yas[u, 0, i] = add(wa[u, up, i], ya1[u, 0, i])
            return carry

        lax.fori_loop(0, 4, body_up, 0)
        u3 = send(yas.at[u, 0], yaq.at[u, 0, pl.ds(0, 4)], y_dev(1))
        d1.wait_recv()

        def body_down(i, carry):
            yas[u, 1, i] = add(wa[u, down, i + 4], ya1[u, 1, i])
            return carry

        lax.fori_loop(0, 4, body_down, 0)
        d3 = send(yas.at[u, 1], yaq.at[u, 1, pl.ds(4, 4)], y_dev(-1))
        return u2, d2, u3, d3

    def a_last(u, copies):
        for copy in copies:
            copy.wait_recv()

        def body(i, carry):
            total = wa[u, y, i].astype(F32) + yaq[u, 0, i].astype(F32) + yaq[u, 1, i].astype(F32)
            ra[u, i] = total.astype(BF16)
            return carry

        lax.fori_loop(0, 8, body, 0)

    def straight(rows, received, dev_of, here, n):
        return [
            send(rows.at[wrap(here + step, n)], received.at[step - 1], dev_of(step)) for step in (n // 2, *range(1, n // 2), *range(n // 2 + 1, n))
        ]

    def straight_sum(rows, received, here, copies):
        for copy in copies:
            copy.wait_recv()
        total = rows[here].astype(F32)
        for i in range(len(copies)):
            total = total + received[i].astype(F32)
        return total

    lax.fori_loop(0, 4, grad_a, 0)
    a1 = [a_first(u) for u in range(2)]
    lax.fori_loop(0, 4, grad_b, 0)
    b1 = [b_first(u) for u in range(NB)]
    partial_sums(1, lambda n: nt(rbuf[1], w1[n * 384 : n * 384 + 384, :]))
    e_first = reduce_first(1)
    d_second = reduce_second(0, d_first)
    a2 = [a_second(0, a1[0])]
    b2 = [b_step(0, u, b1[u]) for u in range(NB)]
    e_second = reduce_second(1, e_first)
    a2.append(a_second(1, a1[1]))
    b3 = [b_step(1, u, b2[u]) for u in range(NB)]

    def out_view(ref):
        return lambda plane, a: ref.at[pl.ds(peer_seq(plane, a, 0), 2)]

    def give(rows, ref, base):
        for a in range(4):
            copy = pltpu.make_async_copy(rows.at[pl.ds(a * 2, 2)], out_view(ref)(t, a), osem.at[base + a])
            copy.start()
            placed.append(copy)
        return gather_first(out_view(ref), lambda a: rows.at[pl.ds(a * 2, 2)])

    placed = []
    down_rows = reduce_third(0, d_second)
    bo[...] = (mid[...].astype(F32) + down_rows).reshape(8, 8, D).astype(BF16)
    o_first = give(bo, out_b, 0)
    a_last(0, a2[0])
    a3 = [straight(ra.at[0], raq.at[0], z_dev, zz, 8)]
    b4 = [b_step(2, u, b3[u]) for u in range(NB)]

    scaled = reduce_third(1, e_second) * g2
    x_hat2 = xhat[...]
    plain = jnp.mean(scaled, -1, keepdims=True)
    cross = jnp.mean(scaled * x_hat2, -1, keepdims=True)
    upstream = gs[t].astype(F32).reshape(64, D)
    go[...] = (upstream + inv2[...] * (scaled - plain - x_hat2 * cross)).reshape(8, 8, D).astype(BF16)
    m_first = give(go, out_g, 4)

    a_last(1, a2[1])
    a3.append(straight(ra.at[1], raq.at[1], z_dev, zz, 8))
    o_further = gather_second(out_view(out_b), o_first)
    b5 = []
    for u in range(NB):
        b_last(u, b4[u])
        b5.append(straight(rb.at[u], rbq.at[u], y_dev, y, 4))
    m_further = gather_second(out_view(out_g), m_first)
    sums = [
        *(((u * CA2, CA2), straight_sum(ra.at[u], raq.at[u], zz, a3[u])) for u in range(2)),
        *(((CA + u * 128, 128), straight_sum(rb.at[u], rbq.at[u], y, b5[u])) for u in range(NB)),
    ]
    for c in range(2):
        for (first, width), total in sums:
            fin[c, :, first : first + width] = total[c * 18 : c * 18 + 18]
    sf = fresh()

    def hand_over(src, dst):
        return pltpu.make_async_remote_copy(
            src_ref=src, dst_ref=dst, send_sem=ssem.at[sf], recv_sem=rsem.at[sf], device_id=core_dev, device_id_type=MESH
        )

    @pl.when(core == 0)
    def _():
        hand_over(fin.at[1], out_1).start()
        own = pltpu.make_async_copy(fin.at[0], out_1, asem)
        own.start()
        own.wait()
        hand_over(fin.at[1], out_2).wait()

    @pl.when(core == 1)
    def _():
        hand_over(fin.at[0], out_2).start()
        own = pltpu.make_async_copy(fin.at[1], out_2, asem)
        own.start()
        own.wait()
        hand_over(fin.at[0], out_1).wait()

    gather_third(o_further)
    gather_third(m_further)
    for copy in placed:
        copy.wait()

    for turn in turns:
        to_patches(turn).wait_send()
        to_frame(turn).wait_send()

    @pl.when(jnp.logical_not(stays))
    def _():
        to_frame(0).wait_send()

    for copy in started:
        copy.wait_send()


def place(*refs):
    sources, results, (buf_b, buf_g, buf_1, buf_2, sems) = refs[:4], refs[4:8], refs[8:]
    copies = []
    for src, dst, buf, parts in zip(sources, results, (buf_b, buf_g, buf_1, buf_2), (4, 4, 1, 1)):
        step = src.shape[0] // parts
        for i in range(parts):
            rows = pl.ds(i * step, step)
            n = len(copies)
            copies.append(
                (
                    pltpu.make_async_copy(src.at[rows], buf.at[rows], sems.at[0, n]),
                    pltpu.make_async_copy(buf.at[rows], dst.at[rows], sems.at[1, n]),
                )
            )
    for read, _ in copies:
        read.start()
    for read, write in copies:
        read.wait()
        write.start()
    for _, write in copies:
        write.wait()


def local(hidden_in, norm1_gain, qkv_weight, out_weight, norm2_gain, fc1_weight, fc2_weight, out_grad):
    anywhere = pl.BlockSpec(memory_space=pl.ANY)
    vmem = pl.BlockSpec(memory_space=pltpu.VMEM)
    shapes = [
        ((32, 8, D), BF16), ((4, 8, 8, D), BF16), ((8, 8, D), BF16),
        ((3 * QC, D), BF16), ((4, QC, D), BF16), ((D, FQ), BF16), ((D, FQ), BF16),
        ((4, 64, D), BF16), ((32, 8, 3 * QC), BF16), ((32, 8, 3 * QC), BF16),
        ((32, 8, QC), BF16), ((4, 8, 8, QC), BF16),
        ((4, 64, D), BF16), ((256, FQ), F32), ((4, 64, D), BF16),
        ((2, 4, 64, D), F32), ((2, 4, 64, D), BF16),
        ((2, 2, 32, D), BF16), ((2, 2, 32, D), BF16), ((2, 2, 64, D), BF16),
        ((64, D), BF16), ((64, D), F32), ((64, 1), F32), ((8, 8, D), BF16), ((8, 8, D), BF16),
        ((ROWS, D), BF16), ((3, ROWS, 256), BF16), ((3, 256, FQ), BF16),
        ((2, 4, 8, SLAB, CA2), BF16), ((2, 2, 4, SLAB, CA2), BF16), ((2, 2, 4, SLAB, CA2), BF16), ((2, 2, 8, SLAB, CA2), BF16),
        ((2, 8, SLAB, CA2), BF16), ((2, 7, SLAB, CA2), BF16),
        ((NB, 8, 144, 128), BF16), ((NB, 2, 144, 128), BF16), ((3, NB, 2, 144, 128), BF16), ((3, NB, 2, 144, 128), BF16),
        ((NB, 4, SLAB, 128), BF16), ((NB, 3, SLAB, 128), BF16),
        ((2, 18, FQ), F32),
    ]
    scratch = [pltpu.VMEM(shape, kind) for shape, kind in shapes]
    scratch += [
        pltpu.SemaphoreType.DMA((N_SEM,)), pltpu.SemaphoreType.DMA((N_SEM,)),
        pltpu.SemaphoreType.DMA((5,)), pltpu.SemaphoreType.DMA((20,)), pltpu.SemaphoreType.DMA((8,)),
        pltpu.SemaphoreType.DMA,
    ]
    results = [
        jax.ShapeDtypeStruct((32, 8, D), BF16),
        jax.ShapeDtypeStruct((32, 8, D), BF16),
        jax.ShapeDtypeStruct((18, FQ), F32),
        jax.ShapeDtypeStruct((18, FQ), F32),
    ]
    made = pl.pallas_call(
        kernel,
        out_shape=results,
        in_specs=[anywhere, vmem, anywhere, anywhere, vmem, anywhere, anywhere, anywhere],
        out_specs=[anywhere] * 4,
        scratch_shapes=scratch,
        compiler_params=pltpu.CompilerParams(
            collective_id=0, has_side_effects=True, vmem_limit_bytes=60 * 1024 * 1024
        ),
    )(
        hidden_in.reshape(32, 8, D),
        norm1_gain,
        qkv_weight.transpose(1, 2, 0).reshape(3 * QC, D),
        out_weight,
        norm2_gain,
        fc1_weight,
        fc2_weight,
        out_grad.reshape(32, 8, D),
    )
    block, grad_mid, grad_fc1, grad_fc2 = pl.pallas_call(
        place,
        out_shape=results,
        in_specs=[anywhere] * 4,
        out_specs=[anywhere] * 4,
        scratch_shapes=[pltpu.VMEM(made_one.shape, made_one.dtype) for made_one in results]
        + [pltpu.SemaphoreType.DMA((2, 10))],
        compiler_params=pltpu.CompilerParams(vmem_limit_bytes=60 * 1024 * 1024),
    )(*made)
    shape = hidden_in.shape
    return block.reshape(shape), grad_mid.reshape(shape), grad_fc1, grad_fc2


def solution(mesh):
    return jax.shard_map(
        local,
        mesh=mesh,
        in_specs=(
            P("dp", "seq", None, None),
            P(),
            P(None, None, "tensor"),
            P("tensor", None),
            P(),
            P(None, "tensor"),
            P(None, "tensor"),
            P("dp", "seq", None, None),
        ),
        out_specs=(
            P("dp", "seq", None, None),
            P("dp", "seq", None, None),
            P(("seq", "dp"), "tensor"),
            P(("seq", "dp"), "tensor"),
        ),
        check_vma=False,
    )
```
